32 devices in a mesh: fsdp: 32 (over z, y, x, core).
Axes of the slice: x: 2, y: 2, z: 4, core: 2. Of those that a mesh axis runs over, the one named last changes fastest.
Arguments:
- tokens: bfloat16 [32, 1024, 384], P('fsdp'), may hold values from -6 to 6
- seg_ids: int32 [32, 1024], P('fsdp'), may hold values from -1 to 19, as said below
- w_qkv: bfloat16 [442368], P('fsdp'), may hold values from -0.3125 to 0.3125
- w_out: bfloat16 [147456], P('fsdp'), may hold values from -0.875 to 0.875
- w_up: bfloat16 [589824], P('fsdp'), may hold values from -0.3125 to 0.3125
- w_down: bfloat16 [589824], P('fsdp'), may hold values from -0.15625 to 0.15625
- norm_gains: bfloat16 [768], P('fsdp'), may hold values from 0.099609375 to 1.8984375
- cotangent: bfloat16 [32, 1024, 384], P('fsdp'), may hold values from -6 to 6
Outputs:
- layer_out: bfloat16 [32, 1024, 384], P('fsdp')
- grad_tokens: float32 [32, 1024, 384], P('fsdp')
- grad_qkv: float32 [442368], P('fsdp')
- grad_out: float32 [147456], P('fsdp')
- grad_up: float32 [589824], P('fsdp')
- grad_down: float32 [589824], P('fsdp')
- grad_gains: float32 [768], P('fsdp')
The draws below stay inside these ranges and needn't reach their ends.
Inputs may be any that keep to these rules, and one draw needn't show every extreme that they name: `seg_ids`: in each pack, slots 0 to c * 51 - 1 hold images 0 to c - 1 in consecutive runs of 51 slots, and every later slot is -1; c is 10 to 20 (at least 1), and some pack holds 20 images.
All inputs are finite; a program needn't handle non-finite values.
Results may differ from the reference program's by a relative error of at most 0.012.
Values may be sent and summed in bfloat16 or wider, within the bound.
A program may use at most 192 MiB of HBM per device.

```python
import jax
import jax.numpy as jnp
from jax import lax

D = 384
HEADS = 6
HEAD_DIM = 64
FF = 1536
IMG_TOK = 51
IMAGES = 20
PACK_TOK = 1024
PACKS_ALL = 32


def draw_seg_ids(key, part):
    key = jax.random.fold_in(key, 5)
    count_key = jax.random.fold_in(key, 1)
    full_key = jax.random.fold_in(key, 2)
    lowest = max(IMAGES // 2, 1)
    counts = jax.random.randint(count_key, (PACKS_ALL,), lowest, IMAGES + 1)
    full_pack = jax.random.randint(full_key, (), 0, PACKS_ALL)
    counts = jnp.where(jnp.arange(PACKS_ALL) == full_pack, IMAGES, counts)
    image_index = jnp.arange(PACK_TOK) // IMG_TOK
    filled = image_index[None, :] < counts[:, None]
    return jnp.where(filled, image_index[None, :], -1).astype(jnp.int32)


def steps_of(stream_key, shape, cuts, low, largest):
    def one(axis_at, parts):
        draws = jax.random.uniform(jax.random.fold_in(jax.random.fold_in(stream_key, 6), axis_at), (parts,), jnp.float32, low / len(cuts), largest / len(cuts))
        return jnp.repeat(jnp.exp(draws), shape[axis_at] // parts).reshape((-1,) + (1,) * (len(shape) - axis_at - 1))

    level = one(*cuts[0])
    for cut in cuts[1:]:
        level = level * one(*cut)
    return level


def gaussian(stream_key, dims, scale, reach, pieces=(), kind=jnp.bfloat16):
    drawn = scale * jax.random.normal(stream_key, dims, jnp.float32)
    if pieces:
        drawn = drawn * steps_of(stream_key, dims, pieces, -0.22, 0.18)
    return jnp.clip(drawn, -reach, reach).astype(kind)


def setup_inputs(seed: int = 0) -> dict:
    key_of = jax.random.split(jax.random.key(seed), 9)
    return {
        "tokens": gaussian(key_of[0], (PACKS_ALL, PACK_TOK, D), 1.0, 6.0, ((0, 32),)),
        "seg_ids": draw_seg_ids(jax.random.fold_in(key_of[8], 71), 0),
        "w_qkv": gaussian(key_of[2], (3 * D * D,), D ** -0.5, 0.3125, ((0, 32),)),
        "w_out": gaussian(key_of[3], (D * D,), (D // 8) ** -0.5, 0.875, ((0, 32),)),
        "w_up": gaussian(key_of[4], (D * FF,), D ** -0.5, 0.3125, ((0, 32),)),
        "w_down": gaussian(key_of[5], (FF * D,), FF ** -0.5, 0.15625, ((0, 32),)),
        "norm_gains": jnp.clip(1.0 + 0.18 * jax.random.normal(key_of[6], (2 * D,), jnp.float32), 0.099609375, 1.8984375).astype(jnp.bfloat16),
        "cotangent": gaussian(key_of[7], (PACKS_ALL, PACK_TOK, D), 1.0, 6.0, ((0, 32),)),
    }


@jax.custom_vjp
def low(v):
    return lax.optimization_barrier(v.astype(jnp.bfloat16)).astype(jnp.float32)

@jax.custom_vjp
def low_back(v):
    return v

def low_keep(v):
    return (low(v), None)

def low_pass(kept, grad):
    return (grad,)

def back_keep(v):
    return (v, None)

def back_low(kept, grad):
    return (low(grad),)
low.defvjp(low_keep, low_pass)
low_back.defvjp(back_keep, back_low)
epsilon = 1e-06
masked = -1e+30
highest = lax.Precision.HIGHEST

def normalize(values):
    centred = values - lax.optimization_barrier(jnp.mean(values, axis=-1, keepdims=True))
    spread = lax.optimization_barrier(jnp.mean(centred * centred, axis=-1, keepdims=True))
    return centred * lax.rsqrt(spread + epsilon)

def product(left, right):
    return jnp.dot(left, right, precision=highest, preferred_element_type=jnp.float32)

def pack_forward(inputs, seg_pack, mat_qkv, mat_out, mat_up, mat_down, gain_one, gain_two):
    normed_one = low(normalize(inputs) * gain_one)
    qkv_all = low(low_back(product(normed_one, mat_qkv)))
    qkv_all = qkv_all.reshape(PACK_TOK, 3, HEADS, HEAD_DIM)
    queries = qkv_all[:, 0]
    key_rows = qkv_all[:, 1]
    value_rows = qkv_all[:, 2]
    scores = jnp.einsum('qhd,khd->hqk', queries, key_rows, precision=highest) * HEAD_DIM ** (-0.5)
    scores = low_back(scores)
    same_image = seg_pack[:, None] == seg_pack[None, :]
    scores = jnp.where(same_image[None], scores, masked)
    attn_probs = low(jax.nn.softmax(scores, axis=-1))
    context = jnp.einsum('hqk,khd->qhd', attn_probs, value_rows, precision=highest).reshape(PACK_TOK, D)
    context = low_back(low(context))
    hidden_res = inputs + low_back(product(context, mat_out))
    normed_two = low(normalize(hidden_res) * gain_two)
    pre_act = low_back(product(normed_two, mat_up))
    activated = low(jax.nn.gelu(pre_act, approximate=False))
    return hidden_res + low_back(product(activated, mat_down))

def reference(tokens, seg_ids, w_qkv, w_out, w_up, w_down, norm_gains, cotangent):
    mat_qkv = w_qkv.astype(jnp.float32).reshape(D, 3 * D)
    mat_out = w_out.astype(jnp.float32).reshape(D, D)
    mat_up = w_up.astype(jnp.float32).reshape(D, FF)
    mat_down = w_down.astype(jnp.float32).reshape(FF, D)
    gain_pair = norm_gains.astype(jnp.float32).reshape(2, D)
    inputs = tokens.astype(jnp.float32)

    def forward(inputs, mat_qkv, mat_out, mat_up, mat_down, gain_pair):

        def one_pack(item):
            return jax.checkpoint(pack_forward)(item[0], item[1], mat_qkv, mat_out, mat_up, mat_down, gain_pair[0], gain_pair[1])
        return lax.map(one_pack, (inputs, seg_ids))
    result, pullback = jax.vjp(forward, inputs, mat_qkv, mat_out, mat_up, mat_down, gain_pair)
    grads = pullback(cotangent.astype(jnp.float32))
    return (result.astype(jnp.bfloat16), grads[0], grads[1].reshape(-1), grads[2].reshape(-1), grads[3].reshape(-1), grads[4].reshape(-1), grads[5].reshape(-1))
```

```python
import functools

import jax
import jax.numpy as jnp
from jax import lax
from jax.experimental import pallas as pl
from jax.experimental.pallas import tpu as pltpu
from jax.sharding import PartitionSpec as P

MESH = pl.DeviceIdType.MESH

f32, bf16 = jnp.float32, jnp.bfloat16
D, HEADS, HD, FF, T = 384, 6, 64, 1536, 1024
PAIRS = 3
EPS = 1e-6
NEG = -1e30
KEYS = [(0, 160), (96, 320), (240, 416), (352, 1024)] + [(496, 1024)] * 4
NN = (((1,), (0,)), ((), ()))
NT = (((1,), (1,)), ((), ()))
TN = (((0,), (0,)), ((), ()))


def dot(a, b, dims=NN):
    return lax.dot_general(a, b, dims, preferred_element_type=f32)


def norm_rows(v):
    c = v - jnp.mean(v, axis=-1, keepdims=True)
    r = lax.rsqrt(jnp.mean(c * c, axis=-1, keepdims=True) + EPS)
    return c * r, r


def norm_back(g, xhat, r):
    m1 = jnp.mean(g, axis=-1, keepdims=True)
    m2 = jnp.mean(g * xhat, axis=-1, keepdims=True)
    return (g - m1 - xhat * m2) * r


def kernel(x_ref, seg_ref, wqkv_ref, wo_ref, w1_ref, w2_ref, gain_ref, dy_ref,
           out_ref, gx_ref, gqkv_ref, gout_ref, gup_ref, gdown_ref, ggain_ref,
           xhat, rstd, a, k_p, v_p, qz, ctx, ctxt, h, rinv, b, act, du, dh, dhr, dz, dkacc, dvacc, dqkv, *es):
    G1 = gain_ref[0:1, :]
    G2 = gain_ref[1:2, :]
    R = 256
    qz[...] = jnp.zeros_like(qz)
    dz[...] = jnp.zeros_like(dz)

    def stage_a(i, _):
        rows = pl.ds(pl.multiple_of(i * R, R), R)
        n, r = norm_rows(x_ref[rows, :].astype(f32))
        xhat[rows, :] = n
        rstd[0, rows, :] = jnp.broadcast_to(r, (R, 128))
        al = (n * G1).astype(bf16)
        a[rows, :] = al
        q = dot(al, wqkv_ref[:, 0:D]).astype(bf16).astype(f32) * 0.125
        kk = dot(al, wqkv_ref[:, D:2 * D]).astype(bf16)
        vv = dot(al, wqkv_ref[:, 2 * D:]).astype(bf16)
        for p in range(PAIRS):
            k_p[p, rows, :] = kk[:, 128 * p:128 * p + 128]
            v_p[p, rows, :] = vv[:, 128 * p:128 * p + 128]
            for s in range(R // 128):
                qt = q[128 * s:128 * s + 128, 128 * p:128 * p + 128].T.astype(bf16)
                qz[p, i * (R // 128) + s, 0:64, 0:128] = qt[0:64]
                qz[p, i * (R // 128) + s, 64:128, 128:256] = qt[64:128]
        return 0

    lax.fori_loop(0, T // R, stage_a, 0)

    segf = seg_ref[0:1, :].astype(f32)
    segcol = jnp.broadcast_to(segf, (128, T)).T
    for t in range(8):
        ks, ke = KEYS[t]
        bias = jnp.where(segcol[ks:ke, :] == segf[:, 128 * t:128 * t + 128], 0.0, NEG)
        e_t = es[t]

        def att(p, _, t=t, ks=ks, ke=ke, bias=bias, e_t=e_t):
            s = dot(k_p[p, ks:ke, :], qz[p, t])
            ee, ri = [], []
            for half in range(2):
                sh = s[:, 128 * half:128 * half + 128] + bias
                m = jnp.max(sh, axis=0, keepdims=True)
                ex = jnp.exp(sh - m)
                ri.append(1.0 / jnp.sum(ex, axis=0, keepdims=True))
                ee.append(ex.astype(bf16))
            e = jnp.concatenate(ee, axis=1)
            e_t[p] = e
            rr = jnp.concatenate(ri, axis=1)
            rinv[p, t] = jnp.broadcast_to(rr, (8, 256))
            ct = dot(v_p[p, ks:ke, :], e, TN)
            ct = jnp.concatenate([ct[0:64, 0:128] * ri[0], ct[64:128, 128:256] * ri[1]], axis=0)
            lanes = pl.ds(pl.multiple_of(p * 128, 128), 128)
            ctxt[lanes, 128 * t:128 * t + 128] = ct.astype(bf16)
            ctx[128 * t:128 * t + 128, lanes] = ct.T.astype(bf16)
            return 0

        lax.fori_loop(0, PAIRS, att, 0)

    FC = 512
    def stage_d(i, gacc):
        rows = pl.ds(pl.multiple_of(i * R, R), R)
        hh = x_ref[rows, :].astype(f32) + dot(ctx[rows, :], wo_ref[...])
        n, r = norm_rows(hh)
        bl = (n * G2).astype(bf16)
        b[rows, :] = bl
        dyl = dy_ref[rows, :]
        o = hh
        db = jnp.zeros((R, D), f32)
        for c in range(FF // FC):
            cols = slice(c * FC, c * FC + FC)
            u = dot(bl, w1_ref[:, cols])
            phi = 0.5 * (1.0 + lax.erf(u * 0.7071067811865476))
            al = (u * phi).astype(bf16)
            act[rows, cols] = al
            o = o + dot(al, w2_ref[cols, :])
            gp = phi + u * jnp.exp(-0.5 * u * u) * 0.3989422804014327
            dul = (gp * dot(dyl, w2_ref[cols, :], NT)).astype(bf16)
            du[rows, cols] = dul
            db = db + dot(dul, w1_ref[:, cols], NT)
        out_ref[rows, :] = o.astype(bf16)
        gacc = gacc + jnp.sum(db * n, axis=0, keepdims=True)
        dhl = dyl.astype(f32) + norm_back(db * G2, n, r)
        dh[rows, :] = dhl
        dhrl = dhl.astype(bf16)
        dhr[rows, :] = dhrl
        dct = dot(wo_ref[...], dhrl, NT)
        for p in range(PAIRS):
            for s in range(R // 128):
                tt = i * (R // 128) + s
                ri = rinv[p, tt, 0:1, :]
                dz[p, tt, 0:64, 0:128] = (dct[128 * p:128 * p + 64, 128 * s:128 * s + 128].astype(bf16).astype(f32) * ri[:, 0:128]).astype(bf16)
                dz[p, tt, 64:128, 128:256] = (dct[128 * p + 64:128 * p + 128, 128 * s:128 * s + 128].astype(bf16).astype(f32) * ri[:, 128:256]).astype(bf16)
        return gacc

    gg2 = lax.fori_loop(0, T // R, stage_d, jnp.zeros((1, D), f32))
    ggain_ref[1:2, :] = gg2

    def w_down(i, _):
        cols = pl.ds(pl.multiple_of(i * 256, 256), 256)
        gdown_ref[cols, :] = dot(act[:, cols], dy_ref[...], TN)
        gup_ref[:, cols] = dot(b[...], du[:, cols], TN)
        return 0

    lax.fori_loop(0, FF // 256, w_down, 0)
    gout_ref[...] = dot(ctxt[...], dhr[...])

    dkacc[...] = jnp.zeros_like(dkacc)
    dvacc[...] = jnp.zeros_like(dvacc)
    for t in range(8):
        ks, ke = KEYS[t]
        e_t = es[t]

        def attb(p, _, t=t, ks=ks, ke=ke, e_t=e_t):
            dzl = dz[p, t]
            dp = dot(v_p[p, ks:ke, :], dzl)
            e = e_t[p]
            ef = e.astype(f32)
            tt = ef * dp
            c = jnp.sum(tt, axis=0, keepdims=True) * rinv[p, t, 0:1, :]
            ds = (tt - ef * c).astype(bf16)
            dvacc[p, ks:ke, :] += dot(e, dzl, NT)
            dkacc[p, ks:ke, :] += dot(ds, qz[p, t], NT)
            dqt = dot(k_p[p, ks:ke, :], ds, TN)
            dqt = jnp.concatenate([dqt[0:64, 0:128], dqt[64:128, 128:256]], axis=0) * 0.125
            lanes = pl.ds(pl.multiple_of(p * 128, 128), 128)
            dqkv[128 * t:128 * t + 128, lanes] = dqt.T.astype(bf16)
            return 0

        lax.fori_loop(0, PAIRS, attb, 0)
    for p in range(PAIRS):
        dqkv[:, D + 128 * p:D + 128 * p + 128] = dkacc[p].astype(bf16)
        dqkv[:, 2 * D + 128 * p:2 * D + 128 * p + 128] = dvacc[p].astype(bf16)

    def w_qkv(i, _):
        cols = pl.ds(pl.multiple_of(i * 384, 384), 384)
        gqkv_ref[:, cols] = dot(a[...], dqkv[:, cols], TN)
        return 0

    lax.fori_loop(0, 3, w_qkv, 0)

    def stage_g(i, gacc):
        rows = pl.ds(pl.multiple_of(i * R, R), R)
        da = dot(dqkv[rows, :], wqkv_ref[...], NT)
        n = xhat[rows, :]
        gacc = gacc + jnp.sum(da * n, axis=0, keepdims=True)
        gx_ref[rows, :] = dh[rows, :] + norm_back(da * G1, n, rstd[0, rows, 0:1])
        return gacc

    ggain_ref[0:1, :] = lax.fori_loop(0, T // R, stage_g, jnp.zeros((1, D), f32))


SCRATCH = [
    pltpu.VMEM((T, D), f32),
    pltpu.VMEM((1, T, 128), f32),
    pltpu.VMEM((T, D), bf16),
    pltpu.VMEM((PAIRS, T, 128), bf16),
    pltpu.VMEM((PAIRS, T, 128), bf16),
    pltpu.VMEM((PAIRS, 8, 128, 256), bf16),
    pltpu.VMEM((T, D), bf16),
    pltpu.VMEM((D, T), bf16),
    pltpu.VMEM((8, 128), f32),
    pltpu.VMEM((PAIRS, 8, 8, 256), f32),
    pltpu.VMEM((T, D), bf16),
    pltpu.VMEM((T, FF), bf16),
    pltpu.VMEM((T, FF), bf16),
    pltpu.VMEM((T, D), f32),
    pltpu.VMEM((T, D), bf16),
    pltpu.VMEM((PAIRS, 8, 128, 256), bf16),
    pltpu.VMEM((PAIRS, T, 128), f32),
    pltpu.VMEM((PAIRS, T, 128), f32),
    pltpu.VMEM((T, 3 * D), bf16),
] + [pltpu.VMEM((PAIRS, ke - ks, 256), bf16) for ks, ke in KEYS]


def compute(x, seg, wqkv, wo, w1, w2, gains, dy):
    vm = pl.BlockSpec(memory_space=pltpu.VMEM)
    return pl.pallas_call(
        kernel,
        out_shape=[
            jax.ShapeDtypeStruct((T, D), bf16),
            jax.ShapeDtypeStruct((T, D), f32),
            jax.ShapeDtypeStruct((D, 3 * D), f32),
            jax.ShapeDtypeStruct((D, D), f32),
            jax.ShapeDtypeStruct((D, FF), f32),
            jax.ShapeDtypeStruct((FF, D), f32),
            jax.ShapeDtypeStruct((2, D), f32),
        ],
        in_specs=[vm] * 8,
        out_specs=[vm] * 7,
        scratch_shapes=SCRATCH,
        compiler_params=pltpu.CompilerParams(vmem_limit_bytes=62 * 2**20),
        name="layer",
    )(x, seg, wqkv, wo, w1, w2, gains, dy)


ZS, KS, CS = 4, 4, 2
PAD = 16
SHAPES = ((PAD, 3 * D), (PAD, D), (PAD, FF), (48, D))


def place():
    me = lax.axis_index("fsdp")
    return me // 8, (me // 2) % 4, me % 2


def device(z, k, c):
    return ((z * 4 + k) * 2 + c,)


def greet():
    z, k, c = place()
    barrier = pltpu.get_barrier_semaphore()
    partners = [(z, k, 1 - c)] + [(z, k ^ m, c) for m in (1, 2, 3)] + [(z ^ m, k, c) for m in (1, 2, 3)]
    for p in partners:
        pl.semaphore_signal(barrier, inc=1, device_id=device(*p), device_id_type=MESH)
    pl.semaphore_wait(barrier, len(partners))


def send(src, dst, sems, i, to):
    return pltpu.make_async_remote_copy(
        src_ref=src, dst_ref=dst, send_sem=sems.at[0, i], recv_sem=sems.at[1, i],
        device_id=device(*to), device_id_type=MESH)


class Gather:
    def __init__(self, buf, sems):
        z, k, c = place()
        self.z = [send(buf.at[z, k, c], buf.at[z, k, c], sems, m - 1, (z ^ m, k, c)) for m in (1, 2, 3)]
        self.k = [send(buf.at[:, k, c], buf.at[:, k, c], sems, m + 2, (z, k ^ m, c)) for m in (1, 2, 3)]
        self.c = [send(buf.at[:, :, c], buf.at[:, :, c], sems, 6, (z, k, 1 - c))]


class Scatter:
    def __init__(self, s, rc, rp, rz, sems):
        z, k, c = place()
        self.s, self.rc, self.rp, self.rz = s, rc, rp, rz
        self.c = [send(s.at[:, :, 1 - c], rc, sems, 0, (z, k, 1 - c))]
        self.k = [send(s.at[:, k ^ m, c], rp.at[m - 1], sems, m, (z, k ^ m, c)) for m in (1, 2, 3)]
        self.z = [send(s.at[z ^ m, k, c], rz.at[m - 1], sems, m + 3, (z ^ m, k, c)) for m in (1, 2, 3)]

    def add_c(self):
        z, k, c = place()
        for i in range(ZS):
            for j in range(KS):
                self.s[i, j, c] = (self.s[i, j, c].astype(f32) + self.rc[i, j].astype(f32)).astype(bf16)

    def add_k(self):
        z, k, c = place()
        for i in range(ZS):
            t = self.s[i, k, c].astype(f32)
            for m in range(3):
                t = t + self.rp[m, i].astype(f32)
            self.s[i, k, c] = t.astype(bf16)

    def add_z(self):
        z, k, c = place()
        t = self.s[z, k, c].astype(f32)
        for m in range(3):
            t = t + self.rz[m].astype(f32)
        return t


def start(copies):
    for x in copies:
        x.start()


def wait(copies):
    for x in copies:
        x.wait()


def spread_matrix(rows, cols):
    r = lax.broadcasted_iota(jnp.int32, (rows, cols), 0)
    q = lax.broadcasted_iota(jnp.int32, (rows, cols), 1)
    at = jnp.where(r < D, r + 4 * ((r * 21846) >> 18), 16 * (r - D) + 12)
    return (at == q).astype(f32).astype(bf16)


def gain_mask():
    d = lax.broadcasted_iota(jnp.int32, (32, 2 * D), 0)
    j = lax.broadcasted_iota(jnp.int32, (32, 2 * D), 1)
    return ((j * 43691) >> 20) == d


def gain_comb():
    i = lax.broadcasted_iota(jnp.int32, (128, 2 * D), 0)
    j = lax.broadcasted_iota(jnp.int32, (128, 2 * D), 1)
    return (j - 24 * ((j * 43691) >> 20) == i).astype(f32).astype(bf16)


def gather_kernel(sq, so, su, sd, wqkv, wo, w1, w2, gains, bq, bo, bu, bd, semq, semo, semu, semd):
    z, k, c = place()
    bufs = (bq, bo, bu, bd)
    for ref, buf in zip((sq, so, su, sd), bufs):
        buf[z, k, c] = ref[...]
    greet()
    gs = [Gather(b, s) for b, s in zip(bufs, (semq, semo, semu, semd))]
    for g in gs:
        start(g.z)
    for g in gs:
        wait(g.z)
        start(g.k)
    for g in gs:
        wait(g.k)
        start(g.c)
    for g in gs:
        wait(g.c)
    u = spread_matrix(D, 512)
    wide = bq[...].reshape(512, 3 * D)
    pick = spread_matrix(D + 32, 512)[D:]
    g32 = dot(pick, wide[:, 0:128]).astype(bf16)
    gall = jnp.sum(jnp.where(gain_mask(), dot(g32, gain_comb()), 0.0), axis=0, keepdims=True)
    gains[0:1, :] = gall[:, 0:D]
    gains[1:2, :] = gall[:, D:]
    wqkv[...] = dot(u, wide).astype(bf16)
    wo[...] = dot(u, bo[...].reshape(512, D)).astype(bf16)
    w1[...] = dot(u, bu[...].reshape(512, FF)).astype(bf16)
    w2[...] = bd[...].reshape(FF, D)


def gather(sq, so, su, sd):
    vm = pl.BlockSpec(memory_space=pltpu.VMEM)
    dma = pltpu.SemaphoreType.DMA
    return pl.pallas_call(
        gather_kernel,
        out_shape=[
            jax.ShapeDtypeStruct((D, 3 * D), bf16),
            jax.ShapeDtypeStruct((D, D), bf16),
            jax.ShapeDtypeStruct((D, FF), bf16),
            jax.ShapeDtypeStruct((FF, D), bf16),
            jax.ShapeDtypeStruct((2, D), f32),
        ],
        in_specs=[vm] * 4,
        out_specs=[vm] * 5,
        scratch_shapes=[pltpu.VMEM((ZS, KS, CS) + s, bf16) for s in SHAPES] + [dma((2, 7))] * 4,
        compiler_params=pltpu.CompilerParams(collective_id=0, has_side_effects=True, vmem_limit_bytes=60 * 2**20),
        name="gather",
    )(sq, so, su, sd)


def scatter_kernel(gq, go, gu, gd, gg, oq, oo, ou, od, sq, so, su, sd, cq, co, cu, cd, pq, po, pu, pd, zq, zo, zu, zd,
                   semq, semo, semu, semd):
    greet()
    ut = spread_matrix(D + 32, 512)
    grow = jnp.concatenate([gg[0:1, :], gg[1:2, :]], axis=1)
    grow = jnp.where(gain_mask(), jnp.broadcast_to(grow, (32, 2 * D)), 0.0).astype(bf16)
    grow = dot(grow, gain_comb(), NT).astype(bf16)
    gqb = gq[...].astype(bf16)
    full = jnp.concatenate([gqb, jnp.concatenate([grow, jnp.zeros((32, 3 * D - 128), bf16)], axis=1)], axis=0)
    sq[...] = dot(ut, full, TN).astype(bf16).reshape(sq.shape)
    so[...] = dot(ut[0:D], go[...].astype(bf16), TN).astype(bf16).reshape(so.shape)
    su[...] = dot(ut[0:D], gu[...].astype(bf16), TN).astype(bf16).reshape(su.shape)
    sd[...] = gd[...].astype(bf16).reshape(sd.shape)
    ss = [
        Scatter(sd, cd, pd, zd, semd),
        Scatter(su, cu, pu, zu, semu),
        Scatter(so, co, po, zo, semo),
        Scatter(sq, cq, pq, zq, semq),
    ]
    for s in ss:
        start(s.c)
    for s in ss:
        wait(s.c)
        s.add_c()
        start(s.k)
    for s in ss:
        wait(s.k)
        s.add_k()
        start(s.z)
    for s, o in zip(ss, (od, ou, oo, oq)):
        wait(s.z)
        o[...] = s.add_z()


def scatter(gq, go, gu, gd, gg):
    vm = pl.BlockSpec(memory_space=pltpu.VMEM)
    dma = pltpu.SemaphoreType.DMA
    return pl.pallas_call(
        scatter_kernel,
        out_shape=[jax.ShapeDtypeStruct(s, f32) for s in SHAPES],
        in_specs=[vm] * 5,
        out_specs=[vm] * 4,
        scratch_shapes=[pltpu.VMEM((ZS, KS, CS) + s, bf16) for s in SHAPES]
        + [pltpu.VMEM((ZS, KS) + s, bf16) for s in SHAPES]
        + [pltpu.VMEM((3, ZS) + s, bf16) for s in SHAPES]
        + [pltpu.VMEM((3,) + s, bf16) for s in SHAPES]
        + [dma((2, 7))] * 4,
        compiler_params=pltpu.CompilerParams(collective_id=1, has_side_effects=True, vmem_limit_bytes=60 * 2**20),
        name="scatter",
    )(gq, go, gu, gd, gg)


def pad_rows(m):
    return jnp.pad(m, ((0, PAD - m.shape[0]), (0, 0)))


def body_direct(tokens, seg_ids, w_qkv, w_out, w_up, w_down, norm_gains, cotangent):
    gain_row = jnp.pad(norm_gains, (0, 3 * D - norm_gains.shape[0])).reshape(1, 3 * D)
    sq = pad_rows(jnp.concatenate([w_qkv.reshape(-1, 3 * D), gain_row], axis=0))
    so = pad_rows(w_out.reshape(-1, D))
    su = pad_rows(w_up.reshape(-1, FF))
    wqkv, wo, w1, w2, gains = gather(sq, so, su, w_down.reshape(-1, D))
    out, gx, gq, go, gu, gd, gg = compute(tokens[0], seg_ids, wqkv, wo, w1, w2, gains, cotangent[0])
    oq, oo, ou, od = scatter(gq, go, gu, gd, gg)
    return (out[None], gx[None], oq[:12].reshape(-1), oo[:12].reshape(-1), ou[:12].reshape(-1), od.reshape(-1),
            oq[12, :24])


def body_plain(tokens, seg_ids, w_qkv, w_out, w_up, w_down, norm_gains, cotangent):
    whole = [lax.all_gather(w, "fsdp", axis=0, tiled=True) for w in (w_qkv, w_out, w_up, w_down, norm_gains)]
    out, gx, *grads = compute(
        tokens[0], seg_ids, whole[0].reshape(D, 3 * D), whole[1].reshape(D, D), whole[2].reshape(D, FF),
        whole[3].reshape(FF, D), whole[4].astype(f32).reshape(2, D), cotangent[0])
    shards = [lax.psum_scatter(g.reshape(-1), "fsdp", scatter_dimension=0, tiled=True) for g in grads]
    return (out[None], gx[None], *shards)


def solution(mesh):
    direct = mesh.shape["fsdp"] == ZS * KS * CS
    rows, flat = P("fsdp", None, None), P("fsdp")
    return jax.shard_map(
        body_direct if direct else body_plain,
        mesh=mesh,
        in_specs=(rows, P("fsdp", None), flat, flat, flat, flat, flat, rows),
        out_specs=(rows, rows, flat, flat, flat, flat, flat),
        check_vma=False,
    )
```

```python
import functools

import jax
import jax.numpy as jnp
from jax import lax
from jax.experimental import pallas as pl
from jax.experimental.pallas import tpu as pltpu
from jax.sharding import PartitionSpec as P

MESH = pl.DeviceIdType.MESH
f32, bf16 = jnp.float32, jnp.bfloat16
D, HEADS, HD, FF, T = 384, 6, 64, 1536, 1024
PAIRS, TILES = 3, 8
EPS = 1e-6
NEG = -1e30
HALF = FF // 2
PAD = 16
KEYS = [(0, 160), (96, 320), (240, 416), (352, 1024)] + [(496, 1024)] * 4
NN = (((1,), (0,)), ((), ()))
NT = (((1,), (1,)), ((), ()))
TN = (((0,), (0,)), ((), ()))
DEVICES = 32


def dot(a, b, dims=NN):
    return lax.dot_general(a, b, dims, preferred_element_type=f32)


def norm_rows(v):
    c = v - jnp.mean(v, axis=-1, keepdims=True)
    r = lax.rsqrt(jnp.mean(c * c, axis=-1, keepdims=True) + EPS)
    return c * r, r


def norm_back(g, xhat, r):
    m1 = jnp.mean(g, axis=-1, keepdims=True)
    m2 = jnp.mean(g * xhat, axis=-1, keepdims=True)
    return (g - m1 - xhat * m2) * r


def spread_matrix(rows, cols):
    r = lax.broadcasted_iota(jnp.int32, (rows, cols), 0)
    q = lax.broadcasted_iota(jnp.int32, (rows, cols), 1)
    at = jnp.where(r < D, r + 4 * ((r * 21846) >> 18), 16 * (r - D) + 12)
    return (at == q).astype(f32).astype(bf16)


def gain_mask():
    d = lax.broadcasted_iota(jnp.int32, (32, 2 * D), 0)
    j = lax.broadcasted_iota(jnp.int32, (32, 2 * D), 1)
    return ((j * 43691) >> 20) == d


def gain_comb():
    i = lax.broadcasted_iota(jnp.int32, (128, 2 * D), 0)
    j = lax.broadcasted_iota(jnp.int32, (128, 2 * D), 1)
    return (j - 24 * ((j * 43691) >> 20) == i).astype(f32).astype(bf16)


BOX = (2, 2, 2, 2, 2)


def place():
    me = lax.axis_index("fsdp")
    return me // 8, (me // 4) % 2, (me // 2) % 2, me % 2


def device(z, y, x, c):
    return (((z * 2 + y) * 2 + x) * 2 + c,)


class Copy:
    def __init__(self, *args):
        self.args = args

    def make(self):
        src, dst, sems, i, to = self.args
        return pltpu.make_async_remote_copy(
            src_ref=src, dst_ref=dst, send_sem=sems.at[0, i], recv_sem=sems.at[1, i],
            device_id=device(*to), device_id_type=MESH)

    def start(self):
        self.make().start()

    def wait(self):
        self.make().wait()


send = Copy


def greet():
    z, y, x, c = place()
    barrier = pltpu.get_barrier_semaphore()
    partners = [(z, y, x, 1 - c), (z, y, 1 - x, c), (z, 1 - y, x, c), (z, 1 - y, 1 - x, c)]
    partners += [(z ^ m, y, x, c) for m in (1, 2, 3)]
    for p in partners:
        pl.semaphore_signal(barrier, inc=1, device_id=device(*p), device_id_type=MESH)
    pl.semaphore_wait(barrier, len(partners))


def start(copies):
    for q in copies:
        q.start()


def wait(copies):
    for q in copies:
        q.wait()


def gather_steps(b, sems, split):
    z, y, x, c = place()
    zh, zl = z // 2, z % 2
    own = b.at[zh, zl, y, x, c]
    line = [send(own, own, sems, m - 1, (z ^ m, y, x, c)) for m in (1, 2, 3)]
    col = b.at[:, :, y, x, c]
    near = [send(col, col, sems, 3, (z, y, 1 - x, c)), send(col, col, sems, 4, (z, 1 - y, x, c))]
    core = [send(b.at[:, :, :, :, c], b.at[:, :, :, :, c], sems, 7, (z, y, x, 1 - c))]
    if not split:
        far = [send(col, col, sems, 5, (z, 1 - y, 1 - x, c))]
        return [line, near + far, core]
    fx, fy = b.at[:, 0, y, 1 - x, c], b.at[:, 1, 1 - y, x, c]
    far = [send(fx, fx, sems, 5, (z, 1 - y, x, c)), send(fy, fy, sems, 6, (z, y, 1 - x, c))]
    return [line, near, far, core]


class Scatter:
    def __init__(self, s, rc, rx, ry, sx, sy, sems, h=pl.ds(0, 2), nh=2):
        z, y, x, c = place()
        self.s, self.rc, self.rx, self.ry, self.sx, self.sy, self.h0, self.nh = s, rc, rx, ry, sx, sy, h.start, nh
        self.core = [send(s.at[h, :, :, :, 1 - c], rc.at[h], sems, 0, (z, y, x, 1 - c))]
        self.near = [
            send(s.at[h, 0, :, 1 - x, c], rx.at[h], sems, 1, (z, y, 1 - x, c)),
            send(s.at[h, 1, 1 - y, :, c], ry.at[h], sems, 2, (z, 1 - y, x, c)),
        ]
        self.far = [
            send(s.at[h, 0, 1 - y, x, c], sy.at[h], sems, 3, (z, 1 - y, x, c)),
            send(s.at[h, 1, y, 1 - x, c], sx.at[h], sems, 4, (z, y, 1 - x, c)),
        ]

    def add_core(self):
        z, y, x, c = place()
        s, rc = self.s, self.rc
        for i in range(self.h0, self.h0 + self.nh):
            for j in range(2):
                for k in range(2):
                    for l in range(2):
                        s[i, j, k, l, c] = (s[i, j, k, l, c].astype(f32) + rc[i, j, k, l].astype(f32)).astype(bf16)

    def add_near(self):
        z, y, x, c = place()
        s = self.s
        for i in range(self.h0, self.h0 + self.nh):
            s[i, 0, 1 - y, x, c] = (s[i, 0, 1 - y, x, c].astype(f32) + self.rx[i, 1 - y].astype(f32)).astype(bf16)
            s[i, 1, y, 1 - x, c] = (s[i, 1, y, 1 - x, c].astype(f32) + self.ry[i, 1 - x].astype(f32)).astype(bf16)

    def add_far(self):
        z, y, x, c = place()
        s = self.s
        for i in range(self.h0, self.h0 + self.nh):
            s[i, 0, y, x, c] = (s[i, 0, y, x, c].astype(f32) + self.rx[i, y].astype(f32)
                                + self.sy[i].astype(f32)).astype(bf16)
            s[i, 1, y, x, c] = (s[i, 1, y, x, c].astype(f32) + self.ry[i, x].astype(f32)
                                + self.sx[i].astype(f32)).astype(bf16)

    def core_to_near(self):
        wait(self.core)
        self.add_core()
        start(self.near)

    def near_to_far(self):
        wait(self.near)
        self.add_near()
        start(self.far)

    def end_far(self):
        wait(self.far)
        self.add_far()


def line_steps(s, rz, sems):
    z, y, x, c = place()
    return [send(s.at[(z ^ m) // 2, (z ^ m) % 2, y, x, c], rz.at[m - 1], sems, m + 4, (z ^ m, y, x, c))
            for m in (1, 2, 3)]


def line_sum(s, rz):
    z, y, x, c = place()
    return s[z // 2, z % 2, y, x, c].astype(f32) + rz[0].astype(f32) + rz[1].astype(f32) + rz[2].astype(f32)


def layer_kernel(
    x_ref, seg_ref, fq, fo, fu, fd, fg, dy_ref,
    out_hbm, gx_hbm, oq, oo, ou, od, og,
    bq, bo, bu, bd, u512, wqkv, wo, w1, w2, gains, flat, sf,
    xhat, rstd, a, k_p, v_p, qz, ctx, ctxt, rinv, hhat, rstd2, b, act, du, oacc, dbacc, out_v, dh, dhr, dz,
    dkacc, dvacc, dqkv, es, biases,
    sq, so, su, sd, cq, co, cu, cd, xq, xo, xu, xd, yq, yo, yu, yd, vq, vo, vu, vd, hq, ho, hu, hd, zq, zo, zu, zd,
    gsem, ssem, lsem,
):
    z, y, x, c = place()
    zh, zl = z // 2, z % 2

    sf[...] = jnp.zeros_like(sf)

    def to_slot(src, width, rows, dst, cols):
        n = rows * width
        flat[0:n, :] = src[...].astype(f32)
        for j in range(width):
            if rows == 12:
                sf[0:12, :] = flat[pl.ds(j, rows, stride=width), :]
                piece = sf[...]
            else:
                piece = flat[pl.ds(j, rows, stride=width), :]
            dref, cj = dst(j) if callable(dst) else (dst, j)
            dref[zh, zl, y, x, c, :, 128 * cj:128 * cj + 128] = piece.astype(bf16)

    to_slot(fq, 9, 12, lambda j: (bq.at[j % 3], j // 3), None)
    sf[12:13, 0:24] = fg[...].astype(f32)
    sf[0:12, :] = flat[pl.ds(0, 12, stride=9), :]
    bq[0, zh, zl, y, x, c, :, 0:128] = sf[...].astype(bf16)
    sf[...] = jnp.zeros_like(sf)
    greet()
    gq = [gather_steps(bq.at[p], gsem.at[p], False) for p in range(PAIRS)]
    start(gq[0][0])
    start(gq[1][0])
    start(gq[2][0])
    to_slot(fo, 3, 12, bo, None)
    to_slot(fu, 12, 12, bu, None)
    to_slot(fd, 3, 48, bd, None)
    go = gather_steps(bo, gsem.at[3], True)
    gu = gather_steps(bu, gsem.at[4], True)
    gd = gather_steps(bd, gsem.at[5], True)

    u512[...] = spread_matrix(D + 32, 512)
    qz[...] = jnp.zeros_like(qz)
    dz[...] = jnp.zeros_like(dz)

    def norm_in(i, _):
        rows = pl.ds(pl.multiple_of(i * 256, 256), 256)
        n, r = norm_rows(x_ref[rows, :].astype(f32))
        xhat[rows, :] = n
        rstd[rows, :] = jnp.broadcast_to(r, (256, 128))
        return 0

    lax.fori_loop(0, T // 256, norm_in, 0)
    segf = seg_ref[0:1, :].astype(f32)
    segcol = jnp.broadcast_to(segf, (128, T)).T
    for t in range(TILES):
        ks, ke = KEYS[t]
        biases[t][...] = jnp.where(segcol[ks:ke, :] == segf[:, 128 * t:128 * t + 128], 0.0, NEG)

    wait(gq[0][0])
    start(gq[0][1])
    wait(gq[1][0])
    start(gq[1][1])
    wait(gq[2][0])
    start(gq[2][1])
    start(go[0])
    start(gu[0])
    start(gd[0])
    wait(gq[0][1])
    start(gq[0][2])
    wait(gq[0][2])

    wide = bq[0, ..., 0:128].reshape(512, 128)
    g32 = dot(u512[D:, :], wide).astype(bf16)
    gall = jnp.sum(jnp.where(gain_mask(), dot(g32, gain_comb()), 0.0), axis=0, keepdims=True)
    gains[0:1, :] = gall[:, 0:D]
    gains[1:2, :] = gall[:, D:]
    G1 = gains[0:1, :]
    G2 = gains[1:2, :]
    a[...] = (xhat[...] * G1).astype(bf16)

    def forward_pair(p, _):
        lanes = pl.ds(pl.multiple_of(p * 128, 128), 128)

        @pl.when(p > 0)
        def _():
            wait(gather_steps(bq.at[p], gsem.at[p], False)[2])

        w = dot(u512[0:D, :], bq[p].reshape(512, D)).astype(bf16)
        for j in range(3):
            wqkv[:, pl.ds(pl.multiple_of(j * D + p * 128, 128), 128)] = w[:, 128 * j:128 * j + 128]
        for i in range(2):
            rows = slice(512 * i, 512 * i + 512)
            qkv = dot(a[rows, :], w)
            q = qkv[:, 0:128].astype(bf16).astype(f32) * 0.125
            k_p[p, rows, :] = qkv[:, 128:256].astype(bf16)
            v_p[p, rows, :] = qkv[:, 256:384].astype(bf16)
            for s in range(4):
                qt = q[128 * s:128 * s + 128, :].T.astype(bf16)
                qz[p, 4 * i + s, 0:64, 0:128] = qt[0:64]
                qz[p, 4 * i + s, 64:128, 128:256] = qt[64:128]

        @pl.when(p == 0)
        def _():
            wait(gq[1][1])
            start(gq[1][2])
            wait(gq[2][1])
            start(gq[2][2])
            wait(go[0])
            start(go[1])
            wait(gu[0])
            start(gu[1])
            wait(gd[0])
            start(gd[1])

        @pl.when(p == 1)
        def _():
            wait(go[1])
            start(go[2])
            wait(gu[1])
            start(gu[2])

        @pl.when(p == 2)
        def _():
            wait(gd[1])
            start(gd[2])
            wait(go[2])
            start(go[3])
            wait(gu[2])
            start(gu[3])

        for t in range(TILES):
            ks, ke = KEYS[t]
            s = dot(k_p[p, ks:ke, :], qz[p, t])
            ee, ri = [], []
            for half in range(2):
                sh = s[:, 128 * half:128 * half + 128] + biases[t][...]
                m = jnp.max(sh, axis=0, keepdims=True)
                ex = jnp.exp(sh - m)
                ri.append(1.0 / jnp.sum(ex, axis=0, keepdims=True))
                ee.append(ex.astype(bf16))
            e = jnp.concatenate(ee, axis=1)
            es[t][p] = e
            rr = jnp.concatenate(ri, axis=1)
            rinv[p, t] = jnp.broadcast_to(rr, (8, 256))
            ct = dot(v_p[p, ks:ke, :], e, TN)
            ct = jnp.concatenate([ct[0:64, 0:128] * ri[0], ct[64:128, 128:256] * ri[1]], axis=0)
            ctxt[lanes, 128 * t:128 * t + 128] = ct.astype(bf16)
            ctx[128 * t:128 * t + 128, lanes] = ct.T.astype(bf16)
        return 0

    lax.fori_loop(0, PAIRS, forward_pair, 0)

    wait(gd[2])
    start(gd[3])
    wait(go[3])
    wo[...] = dot(u512[0:D, :], bo[...].reshape(512, D)).astype(bf16)
    for i in range(2):
        rows = slice(512 * i, 512 * i + 512)
        hh = x_ref[rows, :].astype(f32) + dot(ctx[rows, :], wo[...])
        n, r = norm_rows(hh)
        hhat[rows, :] = n
        rstd2[rows, :] = jnp.broadcast_to(r, (512, 128))
        b[rows, :] = (n * G2).astype(bf16)
        oacc[rows, :] = hh
    wait(gu[3])
    w1[...] = dot(u512[0:D, :], bu[...].reshape(512, FF)).astype(bf16)
    wait(gd[3])
    w2[...] = bd[...].reshape(FF, D)

    rs_u = [Scatter(su.at[j], cu.at[j], xu.at[j], yu.at[j], vu.at[j], hu.at[j], ssem.at[j]) for j in range(2)]
    rs_d = [Scatter(sd, cd, xd, yd, vd, hd, ssem.at[2 + j], pl.ds(j, 1), 1) for j in range(2)]
    rs_o = Scatter(so, co, xo, yo, vo, ho, ssem.at[4])
    ln_u = [line_steps(su.at[j], zu.at[j], ssem.at[j]) for j in range(2)]
    ln_d = line_steps(sd, zd, ssem.at[2])
    ln_o = line_steps(so, zo, ssem.at[4])

    for j in range(2):
        cols = slice(HALF * j, HALF * j + HALF)
        for i in range(2):
            rows = slice(512 * i, 512 * i + 512)
            u = dot(b[rows, :], w1[:, cols])
            phi = 0.5 * (1.0 + lax.erf(u * 0.7071067811865476))
            al = (u * phi).astype(bf16)
            act[rows, :] = al
            oacc[rows, :] += dot(al, w2[cols, :])
            gp = phi + u * jnp.exp(-0.5 * u * u) * 0.3989422804014327
            dul = (gp * dot(dy_ref[rows, :], w2[cols, :], NT)).astype(bf16)
            du[rows, :] = dul
            db = dot(dul, w1[:, cols], NT)
            if j == 0:
                dbacc[rows, :] = db
            else:
                dbacc[rows, :] += db
            if j == 1:
                if i == 0:
                    rs_d[0].core_to_near()
                    rs_u[0].core_to_near()
                else:
                    rs_d[0].near_to_far()
                    rs_u[0].near_to_far()
        sd[j] = dot(act[...], dy_ref[...], TN).astype(bf16).reshape((2, 2, 2, 2, 48, D))
        start(rs_d[j].core)
        gup = dot(b[...], du[...], TN).astype(bf16)
        su[j] = dot(u512[0:D, :], gup, TN).astype(bf16).reshape(BOX + (PAD, HALF))
        start(rs_u[j].core)

    out_v[...] = oacc[...].astype(bf16)
    out_copy = pltpu.make_async_copy(out_v, out_hbm, lsem.at[0])
    out_copy.start()
    rs_d[0].end_far()
    rs_u[0].end_far()
    start(ln_u[0])
    gg2 = jnp.zeros((1, D), f32)
    for i in range(2):
        rows = slice(512 * i, 512 * i + 512)
        n = hhat[rows, :]
        db = dbacc[rows, :]
        gg2 = gg2 + jnp.sum(db * n, axis=0, keepdims=True)
        dhl = dy_ref[rows, :].astype(f32) + norm_back(db * G2, n, rstd2[rows, 0:1])
        dh[rows, :] = dhl
        dhrl = dhl.astype(bf16)
        dhr[rows, :] = dhrl
        dct = dot(wo[...], dhrl, NT)
        for p in range(PAIRS):
            for s in range(4):
                t = 4 * i + s
                ri = rinv[p, t, 0:1, :]
                top = dct[128 * p:128 * p + 64, 128 * s:128 * s + 128].astype(bf16).astype(f32)
                low = dct[128 * p + 64:128 * p + 128, 128 * s:128 * s + 128].astype(bf16).astype(f32)
                dz[p, t, 0:64, 0:128] = (top * ri[:, 0:128]).astype(bf16)
                dz[p, t, 64:128, 128:256] = (low * ri[:, 128:256]).astype(bf16)
    gout = dot(ctxt[...], dhr[...]).astype(bf16)
    so[...] = dot(u512[0:D, :], gout, TN).astype(bf16).reshape(BOX + (PAD, D))
    start(rs_o.core)
    rs_d[1].core_to_near()
    rs_u[1].core_to_near()

    dkacc[...] = jnp.zeros_like(dkacc)
    dvacc[...] = jnp.zeros_like(dvacc)

    def rs_q(p):
        return Scatter(sq.at[p], cq.at[p], xq.at[p], yq.at[p], vq.at[p], hq.at[p], ssem.at[5 + p])

    def ln_q(p):
        return line_steps(sq.at[p], zq.at[p], ssem.at[5 + p])

    def backward_pair(p, gg1):
        lanes = pl.ds(pl.multiple_of(p * 128, 128), 128)
        for t in range(TILES):
            ks, ke = KEYS[t]
            dzl = dz[p, t]
            dp = dot(v_p[p, ks:ke, :], dzl)
            e = es[t][p]
            ef = e.astype(f32)
            tt = ef * dp
            cc = jnp.sum(tt, axis=0, keepdims=True) * rinv[p, t, 0:1, :]
            ds = (tt - ef * cc).astype(bf16)
            dvacc[p, ks:ke, :] += dot(e, dzl, NT)
            dkacc[p, ks:ke, :] += dot(ds, qz[p, t], NT)
            dqt = dot(k_p[p, ks:ke, :], ds, TN)
            dqt = jnp.concatenate([dqt[0:64, 0:128], dqt[64:128, 128:256]], axis=0) * 0.125
            dqkv[p, 128 * t:128 * t + 128, 0:128] = dqt.T.astype(bf16)
        dqkv[p, :, 128:256] = dkacc[p].astype(bf16)
        dqkv[p, :, 256:384] = dvacc[p].astype(bf16)
        g = dot(a[...], dqkv[p], TN)
        for j in range(3):
            wj = wqkv[:, pl.ds(pl.multiple_of(j * D + p * 128, 128), 128)].astype(f32)
            gg1 = gg1 + wj * g[:, 128 * j:128 * j + 128]
        gsum = jnp.sum(gg1.T, axis=0, keepdims=True) / G1
        grow = jnp.concatenate([gsum, gg2], axis=1)
        grow = jnp.where(gain_mask(), jnp.broadcast_to(grow, (32, 2 * D)), 0.0).astype(bf16)
        grow = dot(grow, gain_comb(), NT)
        grow = jnp.where(p == 2, grow, 0.0).astype(bf16)
        low = jnp.concatenate([grow, jnp.zeros((32, D - 128), bf16)], axis=1)
        full = jnp.concatenate([g.astype(bf16), low], axis=0)
        sq[p] = dot(u512[...], full, TN).astype(bf16).reshape(BOX + (PAD, D))
        start(rs_q(p).core)

        @pl.when(p == 0)
        def _():
            rs_d[1].near_to_far()
            rs_u[1].near_to_far()
            rs_o.core_to_near()

        @pl.when(p == 1)
        def _():
            rs_d[1].end_far()
            start(ln_d)
            rs_u[1].end_far()
            start(ln_u[1])
            rs_o.near_to_far()
            rs_q(0).core_to_near()

        return gg1

    lax.fori_loop(0, PAIRS, backward_pair, jnp.zeros((D, 128), f32))

    def da_rows(i):
        rows = slice(512 * i, 512 * i + 512)
        da = jnp.zeros((512, D), f32)
        for p in range(PAIRS):
            w = jnp.concatenate([wqkv[:, j * D + p * 128:j * D + p * 128 + 128] for j in range(3)], axis=1)
            da = da + dot(dqkv[p, rows, :], w, NT)
        oacc[rows, :] = dh[rows, :] + norm_back(da * G1, xhat[rows, :], rstd[rows, 0:1])
        copy = pltpu.make_async_copy(oacc.at[rows], gx_hbm.at[rows], lsem.at[1 + i])
        copy.start()
        return copy

    def from_slot(v, width, rows, dst, first=0, cols=None):
        for k, j in enumerate(cols if cols is not None else range(first, first + v.shape[1] // 128)):
            dst[pl.ds(j, rows, stride=width), :] = v[0:rows, 128 * k:128 * k + 128]

    rs_q(0).near_to_far()
    rs_o.end_far()
    start(ln_o)
    rs_q(1).core_to_near()
    gx0 = da_rows(0)
    rs_q(2).core_to_near()
    rs_q(0).end_far()
    start(ln_q(0))
    rs_q(1).near_to_far()
    gx1 = da_rows(1)
    rs_q(2).near_to_far()
    rs_q(1).end_far()
    start(ln_q(1))
    for j in range(2):
        wait(ln_u[j])
        from_slot(line_sum(su.at[j], zu.at[j]), 12, 12, ou, 6 * j)
    wait(ln_d)
    from_slot(line_sum(sd, zd), 3, 48, od)
    wait(ln_o)
    from_slot(line_sum(so, zo), 3, 12, oo)
    rs_q(2).end_far()
    start(ln_q(2))
    for p in range(PAIRS):
        wait(ln_q(p))
        v = line_sum(sq.at[p], zq.at[p])
        from_slot(v, 9, 12, oq, cols=(p, 3 + p, 6 + p))
        if p == 2:
            og[...] = v[12:13, 0:24]
    out_copy.wait()
    gx0.wait()
    gx1.wait()


def vm(shape, dtype):
    return pltpu.VMEM(shape, dtype)


WIDE = ((PAIRS,), (PAD, D)), ((), (PAD, D)), ((2,), (PAD, HALF)), ((), (48, D))


def layer(x, seg, fq, fo, fu, fd, fg, dy):
    spec = pl.BlockSpec(memory_space=pltpu.VMEM)
    hbm = pl.BlockSpec(memory_space=pl.ANY)
    dma = pltpu.SemaphoreType.DMA
    scratch = [
        vm((PAIRS,) + BOX + (PAD, D), bf16), vm(BOX + (PAD, D), bf16), vm(BOX + (PAD, FF), bf16),
        vm(BOX + (48, D), bf16),
        vm((D + 32, 512), bf16), vm((D, 3 * D), bf16), vm((D, D), bf16), vm((D, FF), bf16), vm((FF, D), bf16),
        vm((8, D), f32), vm((144, 128), f32), vm((PAD, 128), f32),
        vm((T, D), f32), vm((T, 128), f32), vm((T, D), bf16), vm((PAIRS, T, 128), bf16), vm((PAIRS, T, 128), bf16),
        vm((PAIRS, TILES, 128, 256), bf16), vm((T, D), bf16), vm((D, T), bf16), vm((PAIRS, TILES, 8, 256), f32),
        vm((T, D), f32), vm((T, 128), f32), vm((T, D), bf16), vm((T, HALF), bf16), vm((T, HALF), bf16),
        vm((T, D), f32), vm((T, D), f32), vm((T, D), bf16), vm((T, D), f32), vm((T, D), bf16),
        vm((PAIRS, TILES, 128, 256), bf16), vm((PAIRS, T, 128), f32), vm((PAIRS, T, 128), f32),
        vm((PAIRS, T, D), bf16),
        [vm((PAIRS, ke - ks, 256), bf16) for ks, ke in KEYS],
        [vm((ke - ks, 128), f32) for ks, ke in KEYS],
    ]
    for lead in (BOX, BOX[:4], BOX[:2], BOX[:2], BOX[:1], BOX[:1], (3,)):
        scratch += [vm(g + lead + s, bf16) for g, s in WIDE]
    scratch += [dma((6, 2, 8)), dma((8, 2, 8)), dma((3,))]
    flops = 2 * T * (3 * (3 * D * D + D * D + 2 * D * FF)) + 12 * 2 * 330 * T * D
    return pl.pallas_call(
        layer_kernel,
        out_shape=[
            jax.ShapeDtypeStruct((T, D), bf16),
            jax.ShapeDtypeStruct((T, D), f32),
            jax.ShapeDtypeStruct(fq.shape, f32),
            jax.ShapeDtypeStruct(fo.shape, f32),
            jax.ShapeDtypeStruct(fu.shape, f32),
            jax.ShapeDtypeStruct(fd.shape, f32),
            jax.ShapeDtypeStruct(fg.shape, f32),
        ],
        in_specs=[spec] * 8,
        out_specs=[hbm] * 2 + [spec] * 5,
        scratch_shapes=scratch,
        compiler_params=pltpu.CompilerParams(collective_id=0, has_side_effects=True, vmem_limit_bytes=62 * 2**20),
        cost_estimate=pl.CostEstimate(flops=flops, bytes_accessed=5 * 2**20, transcendentals=T * (FF + 2508)),
        name="layer",
    )(x, seg, fq, fo, fu, fd, fg, dy)


def body_direct(tokens, seg_ids, w_qkv, w_out, w_up, w_down, norm_gains, cotangent):
    def lanes(w):
        return w.reshape(-1, 128)

    out, gx, oq, oo, ou, od, og = layer(
        tokens[0], seg_ids, lanes(w_qkv), lanes(w_out), lanes(w_up), lanes(w_down), norm_gains.reshape(1, -1),
        cotangent[0])
    return (out[None], gx[None], oq.reshape(-1), oo.reshape(-1), ou.reshape(-1), od.reshape(-1), og.reshape(-1))


def plain_kernel(x_ref, seg_ref, wqkv_ref, wo_ref, w1_ref, w2_ref, gain_ref, dy_ref,
           out_ref, gx_ref, gqkv_ref, gout_ref, gup_ref, gdown_ref, ggain_ref,
           xhat, rstd, a, k_p, v_p, qz, ctx, ctxt, h, rinv, b, act, du, dh, dhr, dz, dkacc, dvacc, dqkv, *rest):
    es, biases = rest[:8], rest[8:]
    G1 = gain_ref[0:1, :]
    G2 = gain_ref[1:2, :]
    R = 256
    qz[...] = jnp.zeros_like(qz)
    dz[...] = jnp.zeros_like(dz)

    def stage_a(i, _):
        rows = pl.ds(pl.multiple_of(i * R, R), R)
        n, r = norm_rows(x_ref[rows, :].astype(f32))
        xhat[rows, :] = n
        rstd[0, rows, :] = jnp.broadcast_to(r, (R, 128))
        al = (n * G1).astype(bf16)
        a[rows, :] = al
        q = dot(al, wqkv_ref[:, 0:D]).astype(bf16).astype(f32) * 0.125
        kk = dot(al, wqkv_ref[:, D:2 * D]).astype(bf16)
        vv = dot(al, wqkv_ref[:, 2 * D:]).astype(bf16)
        for p in range(PAIRS):
            k_p[p, rows, :] = kk[:, 128 * p:128 * p + 128]
            v_p[p, rows, :] = vv[:, 128 * p:128 * p + 128]
            for s in range(R // 128):
                qt = q[128 * s:128 * s + 128, 128 * p:128 * p + 128].T.astype(bf16)
                qz[p, i * (R // 128) + s, 0:64, 0:128] = qt[0:64]
                qz[p, i * (R // 128) + s, 64:128, 128:256] = qt[64:128]
        return 0

    lax.fori_loop(0, T // R, stage_a, 0)

    segf = seg_ref[0:1, :].astype(f32)
    segcol = jnp.broadcast_to(segf, (128, T)).T
    for t in range(8):
        ks, ke = KEYS[t]
        biases[t][...] = jnp.where(segcol[ks:ke, :] == segf[:, 128 * t:128 * t + 128], 0.0, NEG)

    def att(p, _):
        lanes = pl.ds(pl.multiple_of(p * 128, 128), 128)
        for t in range(8):
            ks, ke = KEYS[t]
            s = dot(k_p[p, ks:ke, :], qz[p, t])
            ee, ri = [], []
            for half in range(2):
                sh = s[:, 128 * half:128 * half + 128] + biases[t][...]
                m = jnp.max(sh, axis=0, keepdims=True)
                ex = jnp.exp(sh - m)
                ri.append(1.0 / jnp.sum(ex, axis=0, keepdims=True))
                ee.append(ex.astype(bf16))
            e = jnp.concatenate(ee, axis=1)
            es[t][p] = e
            rr = jnp.concatenate(ri, axis=1)
            rinv[p, t] = jnp.broadcast_to(rr, (8, 256))
            ct = dot(v_p[p, ks:ke, :], e, TN)
            ct = jnp.concatenate([ct[0:64, 0:128] * ri[0], ct[64:128, 128:256] * ri[1]], axis=0)
            ctxt[lanes, 128 * t:128 * t + 128] = ct.astype(bf16)
            ctx[128 * t:128 * t + 128, lanes] = ct.T.astype(bf16)
        return 0

    lax.fori_loop(0, PAIRS, att, 0)

    FC = 512
    def stage_d(i, gacc):
        rows = pl.ds(pl.multiple_of(i * R, R), R)
        hh = x_ref[rows, :].astype(f32) + dot(ctx[rows, :], wo_ref[...])
        n, r = norm_rows(hh)
        bl = (n * G2).astype(bf16)
        b[rows, :] = bl
        dyl = dy_ref[rows, :]
        o = hh
        db = jnp.zeros((R, D), f32)
        for c in range(FF // FC):
            cols = slice(c * FC, c * FC + FC)
            u = dot(bl, w1_ref[:, cols])
            phi = 0.5 * (1.0 + lax.erf(u * 0.7071067811865476))
            al = (u * phi).astype(bf16)
            act[rows, cols] = al
            o = o + dot(al, w2_ref[cols, :])
            gp = phi + u * jnp.exp(-0.5 * u * u) * 0.3989422804014327
            dul = (gp * dot(dyl, w2_ref[cols, :], NT)).astype(bf16)
            du[rows, cols] = dul
            db = db + dot(dul, w1_ref[:, cols], NT)
        out_ref[rows, :] = o.astype(bf16)
        gacc = gacc + jnp.sum(db * n, axis=0, keepdims=True)
        dhl = dyl.astype(f32) + norm_back(db * G2, n, r)
        dh[rows, :] = dhl
        dhrl = dhl.astype(bf16)
        dhr[rows, :] = dhrl
        dct = dot(wo_ref[...], dhrl, NT)
        for p in range(PAIRS):
            for s in range(R // 128):
                tt = i * (R // 128) + s
                ri = rinv[p, tt, 0:1, :]
                dz[p, tt, 0:64, 0:128] = (dct[128 * p:128 * p + 64, 128 * s:128 * s + 128].astype(bf16).astype(f32) * ri[:, 0:128]).astype(bf16)
                dz[p, tt, 64:128, 128:256] = (dct[128 * p + 64:128 * p + 128, 128 * s:128 * s + 128].astype(bf16).astype(f32) * ri[:, 128:256]).astype(bf16)
        return gacc

    def sd():
        ggain_ref[1:2, :] = lax.fori_loop(0, T // R, stage_d, jnp.zeros((1, D), f32))
    sd()

    def w_down(i, _):
        cols = pl.ds(pl.multiple_of(i * 256, 256), 256)
        gdown_ref[cols, :] = dot(act[:, cols], dy_ref[...], TN)
        gup_ref[:, cols] = dot(b[...], du[:, cols], TN)
        return 0

    lax.fori_loop(0, FF // 256, w_down, 0)
    gout_ref[...] = dot(ctxt[...], dhr[...])

    dkacc[...] = jnp.zeros_like(dkacc)
    dvacc[...] = jnp.zeros_like(dvacc)
    def attb(p, _):
        lanes = pl.ds(pl.multiple_of(p * 128, 128), 128)
        for t in range(8):
            ks, ke = KEYS[t]
            dzl = dz[p, t]
            dp = dot(v_p[p, ks:ke, :], dzl)
            e = es[t][p]
            ef = e.astype(f32)
            tt = ef * dp
            c = jnp.sum(tt, axis=0, keepdims=True) * rinv[p, t, 0:1, :]
            ds = (tt - ef * c).astype(bf16)
            dvacc[p, ks:ke, :] += dot(e, dzl, NT)
            dkacc[p, ks:ke, :] += dot(ds, qz[p, t], NT)
            dqt = dot(k_p[p, ks:ke, :], ds, TN)
            dqt = jnp.concatenate([dqt[0:64, 0:128], dqt[64:128, 128:256]], axis=0) * 0.125
            dqkv[128 * t:128 * t + 128, lanes] = dqt.T.astype(bf16)
        return 0

    lax.fori_loop(0, PAIRS, attb, 0)
    for p in range(PAIRS):
        dqkv[:, D + 128 * p:D + 128 * p + 128] = dkacc[p].astype(bf16)
        dqkv[:, 2 * D + 128 * p:2 * D + 128 * p + 128] = dvacc[p].astype(bf16)

    def w_qkv(i, _):
        cols = pl.ds(pl.multiple_of(i * 384, 384), 384)
        gqkv_ref[:, cols] = dot(a[...], dqkv[:, cols], TN)
        return 0

    lax.fori_loop(0, 3, w_qkv, 0)

    def stage_g(i, gacc):
        rows = pl.ds(pl.multiple_of(i * R, R), R)
        da = dot(dqkv[rows, :], wqkv_ref[...], NT)
        n = xhat[rows, :]
        gacc = gacc + jnp.sum(da * n, axis=0, keepdims=True)
        gx_ref[rows, :] = dh[rows, :] + norm_back(da * G1, n, rstd[0, rows, 0:1])
        return gacc

    def sg():
        ggain_ref[0:1, :] = lax.fori_loop(0, T // R, stage_g, jnp.zeros((1, D), f32))
    sg()


PLAIN_SCRATCH = [
    pltpu.VMEM((T, D), f32),
    pltpu.VMEM((1, T, 128), f32),
    pltpu.VMEM((T, D), bf16),
    pltpu.VMEM((PAIRS, T, 128), bf16),
    pltpu.VMEM((PAIRS, T, 128), bf16),
    pltpu.VMEM((PAIRS, 8, 128, 256), bf16),
    pltpu.VMEM((T, D), bf16),
    pltpu.VMEM((D, T), bf16),
    pltpu.VMEM((8, 128), f32),
    pltpu.VMEM((PAIRS, 8, 8, 256), f32),
    pltpu.VMEM((T, D), bf16),
    pltpu.VMEM((T, FF), bf16),
    pltpu.VMEM((T, FF), bf16),
    pltpu.VMEM((T, D), f32),
    pltpu.VMEM((T, D), bf16),
    pltpu.VMEM((PAIRS, 8, 128, 256), bf16),
    pltpu.VMEM((PAIRS, T, 128), f32),
    pltpu.VMEM((PAIRS, T, 128), f32),
    pltpu.VMEM((T, 3 * D), bf16),
] + [pltpu.VMEM((PAIRS, ke - ks, 256), bf16) for ks, ke in KEYS] + [pltpu.VMEM((ke - ks, 128), f32) for ks, ke in KEYS]


def plain_layer(x, seg, wqkv, wo, w1, w2, gains, dy):
    vm = pl.BlockSpec(memory_space=pltpu.VMEM)
    return pl.pallas_call(
        plain_kernel,
        out_shape=[
            jax.ShapeDtypeStruct((T, D), bf16),
            jax.ShapeDtypeStruct((T, D), f32),
            jax.ShapeDtypeStruct((D, 3 * D), f32),
            jax.ShapeDtypeStruct((D, D), f32),
            jax.ShapeDtypeStruct((D, FF), f32),
            jax.ShapeDtypeStruct((FF, D), f32),
            jax.ShapeDtypeStruct((2, D), f32),
        ],
        in_specs=[vm] * 8,
        out_specs=[vm] * 7,
        scratch_shapes=PLAIN_SCRATCH,
        compiler_params=pltpu.CompilerParams(vmem_limit_bytes=62 * 2**20),
        name="plain_layer",
    )(x, seg, wqkv, wo, w1, w2, gains, dy)


def body_plain(tokens, seg_ids, w_qkv, w_out, w_up, w_down, norm_gains, cotangent):
    whole = [lax.all_gather(w, "fsdp", axis=0, tiled=True) for w in (w_qkv, w_out, w_up, w_down, norm_gains)]
    out, gx, *grads = plain_layer(
        tokens[0], seg_ids, whole[0].reshape(D, 3 * D), whole[1].reshape(D, D), whole[2].reshape(D, FF),
        whole[3].reshape(FF, D), whole[4].astype(f32).reshape(2, D), cotangent[0])
    shards = [lax.psum_scatter(g.reshape(-1), "fsdp", scatter_dimension=0, tiled=True) for g in grads]
    return (out[None], gx[None], *shards)


def solution(mesh):
    direct = mesh.shape["fsdp"] == DEVICES
    rows, flat = P("fsdp", None, None), P("fsdp")
    return jax.shard_map(
        body_direct if direct else body_plain,
        mesh=mesh,
        in_specs=(rows, P("fsdp", None), flat, flat, flat, flat, flat, rows),
        out_specs=(rows, rows, flat, flat, flat, flat, flat),
        check_vma=False,
    )
```

```python
import functools

import jax
import jax.numpy as jnp
from jax import lax
from jax.experimental import pallas as pl
from jax.experimental.pallas import tpu as pltpu
from jax.sharding import PartitionSpec as P

MESH = pl.DeviceIdType.MESH
f32, bf16 = jnp.float32, jnp.bfloat16
D, HEADS, HD, FF, T = 384, 6, 64, 1536, 1024
PAIRS, TILES = 3, 8
EPS = 1e-6
NEG = -1e30
HALF = FF // 2
PAD = 16
KEYS = [(0, 160), (96, 320), (240, 416), (352, 1024)] + [(496, 1024)] * 4
NN = (((1,), (0,)), ((), ()))
NT = (((1,), (1,)), ((), ()))
TN = (((0,), (0,)), ((), ()))
DEVICES = 32


def dot(a, b, dims=NN):
    return lax.dot_general(a, b, dims, preferred_element_type=f32)


def norm_rows(v):
    c = v - jnp.mean(v, axis=-1, keepdims=True)
    r = lax.rsqrt(jnp.mean(c * c, axis=-1, keepdims=True) + EPS)
    return c * r, r


def norm_back(g, xhat, r):
    m1 = jnp.mean(g, axis=-1, keepdims=True)
    m2 = jnp.mean(g * xhat, axis=-1, keepdims=True)
    return (g - m1 - xhat * m2) * r


def spread_matrix(rows, cols):
    r = lax.broadcasted_iota(jnp.int32, (rows, cols), 0)
    q = lax.broadcasted_iota(jnp.int32, (rows, cols), 1)
    at = jnp.where(r < D, r + 4 * ((r * 21846) >> 18), 16 * (r - D) + 12)
    return (at == q).astype(f32).astype(bf16)


def gain_mask():
    d = lax.broadcasted_iota(jnp.int32, (32, 2 * D), 0)
    j = lax.broadcasted_iota(jnp.int32, (32, 2 * D), 1)
    return ((j * 43691) >> 20) == d


def gain_comb():
    i = lax.broadcasted_iota(jnp.int32, (128, 2 * D), 0)
    j = lax.broadcasted_iota(jnp.int32, (128, 2 * D), 1)
    return (j - 24 * ((j * 43691) >> 20) == i).astype(f32).astype(bf16)


BOX = (2, 2, 2, 2, 2)


def place():
    me = lax.axis_index("fsdp")
    return me // 8, (me // 4) % 2, (me // 2) % 2, me % 2


def device(z, y, x, c):
    return (((z * 2 + y) * 2 + x) * 2 + c,)


class Copy:
    def __init__(self, *args):
        self.args = args

    def make(self):
        src, dst, sems, i, to = self.args
        return pltpu.make_async_remote_copy(
            src_ref=src, dst_ref=dst, send_sem=sems.at[0, i], recv_sem=sems.at[1, i],
            device_id=device(*to), device_id_type=MESH)

    def start(self):
        self.make().start()

    def wait(self):
        self.make().wait()


def greet():
    z, y, x, c = place()
    barrier = pltpu.get_barrier_semaphore()
    partners = [(z, y, x, 1 - c), (z, y, 1 - x, c), (z, 1 - y, x, c), (z, 1 - y, 1 - x, c)]
    partners += [(z ^ m, y, x, c) for m in (1, 2, 3)]
    for p in partners:
        pl.semaphore_signal(barrier, inc=1, device_id=device(*p), device_id_type=MESH)
    return lambda: pl.semaphore_wait(barrier, len(partners))


def start(copies):
    for q in copies:
        q.start()


def wait(copies):
    for q in copies:
        q.wait()


def line_of(b, sems):
    z, y, x, c = place()
    own = b.at[z // 2, z % 2, y, x, c]
    return [Copy(own, own, sems, m - 1, (z ^ m, y, x, c)) for m in (1, 2, 3)]


def plane_direct(b, sems):
    z, y, x, c = place()
    col = b.at[:, :, y, x, c]
    near = [Copy(col, col, sems, 3, (z, y, 1 - x, c)), Copy(col, col, sems, 4, (z, 1 - y, x, c)),
            Copy(col, col, sems, 5, (z, 1 - y, 1 - x, c))]
    return [near, [Copy(b.at[:, :, :, :, c], b.at[:, :, :, :, c], sems, 7, (z, y, x, 1 - c))]]


def plane_split(b, sems, h=pl.ds(0, 2)):
    z, y, x, c = place()
    col = b.at[h, :, y, x, c]
    near = [Copy(col, col, sems, 3, (z, y, 1 - x, c)), Copy(col, col, sems, 4, (z, 1 - y, x, c))]
    fx, fy = b.at[h, 0, y, 1 - x, c], b.at[h, 1, 1 - y, x, c]
    far = [Copy(fx, fx, sems, 5, (z, 1 - y, x, c)), Copy(fy, fy, sems, 6, (z, y, 1 - x, c))]
    return [near, far, [Copy(b.at[h, :, :, :, c], b.at[h, :, :, :, c], sems, 7, (z, y, x, 1 - c))]]


class Scatter:
    def __init__(self, s, rc, rx, ry, sx, sy, sems, h=pl.ds(0, 2), nh=2):
        z, y, x, c = place()
        self.s, self.rc, self.rx, self.ry, self.sx, self.sy, self.h0, self.nh = s, rc, rx, ry, sx, sy, h.start, nh
        self.core = [Copy(s.at[h, :, :, :, 1 - c], rc.at[h], sems, 0, (z, y, x, 1 - c))]
        self.near = [
            Copy(s.at[h, 0, :, 1 - x, c], rx.at[h], sems, 1, (z, y, 1 - x, c)),
            Copy(s.at[h, 1, 1 - y, :, c], ry.at[h], sems, 2, (z, 1 - y, x, c)),
        ]
        self.far = [
            Copy(s.at[h, 0, 1 - y, x, c], sy.at[h], sems, 3, (z, 1 - y, x, c)),
            Copy(s.at[h, 1, y, 1 - x, c], sx.at[h], sems, 4, (z, y, 1 - x, c)),
        ]

    def add_core(self):
        z, y, x, c = place()
        s, rc = self.s, self.rc
        for i in range(self.h0, self.h0 + self.nh):
            for j in range(2):
                for k in range(2):
                    for l in range(2):
                        s[i, j, k, l, c] = (s[i, j, k, l, c].astype(f32) + rc[i, j, k, l].astype(f32)).astype(bf16)

    def add_near(self):
        z, y, x, c = place()
        s = self.s
        for i in range(self.h0, self.h0 + self.nh):
            s[i, 0, 1 - y, x, c] = (s[i, 0, 1 - y, x, c].astype(f32) + self.rx[i, 1 - y].astype(f32)).astype(bf16)
            s[i, 1, y, 1 - x, c] = (s[i, 1, y, 1 - x, c].astype(f32) + self.ry[i, 1 - x].astype(f32)).astype(bf16)

    def add_far(self):
        z, y, x, c = place()
        s = self.s
        for i in range(self.h0, self.h0 + self.nh):
            s[i, 0, y, x, c] = (s[i, 0, y, x, c].astype(f32) + self.rx[i, y].astype(f32)
                                + self.sy[i].astype(f32)).astype(bf16)
            s[i, 1, y, x, c] = (s[i, 1, y, x, c].astype(f32) + self.ry[i, x].astype(f32)
                                + self.sx[i].astype(f32)).astype(bf16)

    def core_to_near(self):
        wait(self.core)
        self.add_core()
        start(self.near)

    def near_to_far(self):
        wait(self.near)
        self.add_near()
        start(self.far)

    def end_far(self):
        wait(self.far)
        self.add_far()


def line_steps(s, rz, sems):
    z, y, x, c = place()
    return [Copy(s.at[(z ^ m) // 2, (z ^ m) % 2, y, x, c], rz.at[m - 1], sems, m + 4, (z ^ m, y, x, c))
            for m in (1, 2, 3)]


def line_sum(s, rz):
    z, y, x, c = place()
    return s[z // 2, z % 2, y, x, c].astype(f32) + rz[0].astype(f32) + rz[1].astype(f32) + rz[2].astype(f32)


def layer_kernel(
    x_ref, seg_ref, fq, fo, fu, fd, fg, dy_ref,
    out_hbm, gx_hbm, oq, oo, ou, od, og,
    bq, bo, bu, bd, u512, wqkv, wo, w1, w2, gains, flat, sf,
    xhat, rstd, a, k_p, v_p, qz, ctx, ctxt, rinv, hhat, rstd2, b, act, du, hid, dbacc, out_v, dh, dhr, dz,
    dkacc, dvacc, dqkv, es, biases,
    sq, so, su, sd, cq, co, cu, cd, xq, xo, xu, xd, yq, yo, yu, yd, vq, vo, vu, vd, hq, ho, hu, hd, zq, zo, zu, zd,
    gsem, ssem, lsem,
):
    z, y, x, c = place()
    zh, zl = z // 2, z % 2

    greeted = greet()
    sf[...] = jnp.zeros_like(sf)

    def to_slot(src, width, rows, dst, cols):
        n = rows * width
        flat[0:n, :] = src[...].astype(f32)
        for j in cols:
            piece = flat[pl.ds(j, rows, stride=width), :]
            if rows == 12:
                sf[0:12, :] = piece
                piece = sf[...]
            ref, k = dst(j)
            ref[zh, zl, y, x, c, :, 128 * k:128 * k + 128] = piece.astype(bf16)
            if width == 9 and j == 0:
                sf[...] = jnp.zeros_like(sf)

    sf[12:13, 0:24] = fg[...].astype(f32)
    to_slot(fq, 9, 12, lambda j: (bq.at[j % 3], j // 3), (0, 3, 6))
    gq = [[line_of(bq.at[p], gsem.at[p])] + plane_direct(bq.at[p], gsem.at[p]) for p in range(PAIRS)]
    go = [line_of(bo, gsem.at[3])] + plane_split(bo, gsem.at[3])
    gu = [[line_of(bu.at[k], gsem.at[4 + k])] + plane_split(bu.at[k], gsem.at[4 + k]) for k in range(2)]
    gd_line = line_of(bd, gsem.at[6])
    gd = [plane_split(bd, gsem.at[6 + k], pl.ds(k, 1)) for k in range(2)]
    greeted()
    start(gq[0][0])
    to_slot(fq, 9, 12, lambda j: (bq.at[j % 3], j // 3), (1, 4, 7, 2, 5, 8))
    start(gq[1][0])
    start(gq[2][0])
    to_slot(fo, 3, 12, lambda j: (bo, j), range(3))
    start(go[0])
    to_slot(fu, 12, 12, lambda j: (bu.at[j // 6], j % 6), range(12))
    start(gu[0][0])
    to_slot(fd, 3, 48, lambda j: (bd, j), range(3))
    start(gd_line)
    start(gu[1][0])

    def norm_in(i, _):
        rows = pl.ds(pl.multiple_of(i * 512, 512), 512)
        n, r = norm_rows(x_ref[rows, :].astype(f32))
        xhat[rows, :] = n
        rstd[rows, :] = jnp.broadcast_to(r, (512, 128))
        return 0

    wait(gq[0][0])
    start(gq[0][1])
    lax.fori_loop(0, T // 512, norm_in, 0)
    wait(gq[1][0])
    start(gq[1][1])
    wait(gq[2][0])
    start(gq[2][1])
    u512[...] = spread_matrix(D + 32, 512)
    qz[...] = jnp.zeros_like(qz)
    dz[...] = jnp.zeros_like(dz)
    wait(gq[0][1])
    start(gq[0][2])
    wait(go[0])
    start(go[1])
    segf = seg_ref[0:1, :].astype(f32)
    segcol = jnp.broadcast_to(segf, (128, T)).T
    for t in range(TILES):
        ks, ke = KEYS[t]
        biases[t][...] = jnp.where(segcol[ks:ke, :] == segf[:, 128 * t:128 * t + 128], 0.0, NEG)
    wait(gq[0][2])

    wide = bq[0, ..., 0:128].reshape(512, 128)
    g32 = dot(u512[D:, :], wide).astype(bf16)
    gall = jnp.sum(jnp.where(gain_mask(), dot(g32, gain_comb()), 0.0), axis=0, keepdims=True)
    gains[0:1, :] = gall[:, 0:D]
    gains[1:2, :] = gall[:, D:]
    G1 = gains[0:1, :]
    G2 = gains[1:2, :]
    a[...] = (xhat[...] * G1).astype(bf16)

    def advance(*moves):
        for g, k in moves:
            wait(g[k])
            start(g[k + 1])

    def gather_progress(p, at):
        steps = {
            (0, 0): lambda: advance((gq[1], 1), (gu[0], 0)),
            (0, 2): lambda: (advance((gq[2], 1), (go, 1)), wait(gd_line), start(gd[0][0])),
            (1, 0): lambda: advance((gu[0], 1)),
            (1, 2): lambda: (advance((gd[0], 0), (gu[1], 0)), start(gd[1][0])),
            (2, 0): lambda: advance((go, 2)),
            (2, 1): lambda: advance((gu[0], 2)),
            (2, 2): lambda: advance((gd[0], 1)),
        }
        for q in range(PAIRS):
            if (q, at) in steps:
                @pl.when(p == q)
                def _(q=q):
                    steps[q, at]()

    def forward_pair(p, _):
        lanes = pl.ds(pl.multiple_of(p * 128, 128), 128)

        @pl.when(p > 0)
        def _():
            wait(plane_direct(bq.at[p], gsem.at[p])[1])

        w = dot(u512[0:D, :], bq[p].reshape(512, D)).astype(bf16)
        for j in range(3):
            wqkv[:, pl.ds(pl.multiple_of(j * D + p * 128, 128), 128)] = w[:, 128 * j:128 * j + 128]
        for i in range(2):
            rows = slice(512 * i, 512 * i + 512)
            qkv = dot(a[rows, :], w)
            q = qkv[:, 0:128].astype(bf16).astype(f32) * 0.125
            k_p[p, rows, :] = qkv[:, 128:256].astype(bf16)
            v_p[p, rows, :] = qkv[:, 256:384].astype(bf16)
            for s in range(4):
                qt = q[128 * s:128 * s + 128, :].T.astype(bf16)
                qz[p, 4 * i + s, 0:64, 0:128] = qt[0:64]
                qz[p, 4 * i + s, 64:128, 128:256] = qt[64:128]

        gather_progress(p, 0)

        def scores(t):
            ks, ke = KEYS[t]
            return dot(k_p[p, ks:ke, :], qz[p, t])

        def weigh(t, s):
            ee, ri = [], []
            for half in range(2):
                sh = s[:, 128 * half:128 * half + 128] + biases[t][...]
                m = jnp.max(sh, axis=0, keepdims=True)
                ex = jnp.exp(sh - m)
                ri.append(1.0 / jnp.sum(ex, axis=0, keepdims=True))
                ee.append(ex.astype(bf16))
            e = jnp.concatenate(ee, axis=1)
            es[t][p] = e
            rinv[p, t] = jnp.broadcast_to(jnp.concatenate(ri, axis=1), (8, 256))
            return t, e, ri

        def mix(t, e, ri):
            ks, ke = KEYS[t]
            ct = dot(v_p[p, ks:ke, :], e, TN)
            ct = jnp.concatenate([ct[0:64, 0:128] * ri[0], ct[64:128, 128:256] * ri[1]], axis=0)
            ctxt[lanes, 128 * t:128 * t + 128] = ct.astype(bf16)
            ctx[128 * t:128 * t + 128, lanes] = ct.T.astype(bf16)

        s, last = scores(0), None
        for t in range(TILES):
            ahead = scores(t + 1) if t + 1 < TILES else None
            now = weigh(t, s)
            if last is not None:
                mix(*last)
            s, last = ahead, now
            if t == 3:
                gather_progress(p, 1)
        mix(*last)
        gather_progress(p, 2)
        return 0

    lax.fori_loop(0, PAIRS, forward_pair, 0)

    wait(go[3])
    wo[...] = dot(u512[0:D, :], bo[...].reshape(512, D)).astype(bf16)
    for i in range(2):
        rows = slice(512 * i, 512 * i + 512)
        hh = x_ref[rows, :].astype(f32) + dot(ctx[rows, :], wo[...])
        n, r = norm_rows(hh)
        hhat[rows, :] = n
        rstd2[rows, :] = jnp.broadcast_to(r, (512, 128))
        b[rows, :] = (n * G2).astype(bf16)
        hid[rows, :] = hh

    rs_u = [Scatter(su.at[j], cu.at[j], xu.at[j], yu.at[j], vu.at[j], hu.at[j], ssem.at[j]) for j in range(2)]
    rs_d = [Scatter(sd, cd, xd, yd, vd, hd, ssem.at[2 + j], pl.ds(j, 1), 1) for j in range(2)]
    rs_o = Scatter(so, co, xo, yo, vo, ho, ssem.at[4])
    ln_u = [line_steps(su.at[j], zu.at[j], ssem.at[j]) for j in range(2)]
    ln_d = line_steps(sd, zd, ssem.at[2])
    ln_o = line_steps(so, zo, ssem.at[4])

    for j in range(2):
        cols = slice(HALF * j, HALF * j + HALF)
        wait(gu[j][3])
        w1[:, cols] = dot(u512[0:D, :], bu[j].reshape(512, HALF)).astype(bf16)
        wait(gd[j][2])
        w2[cols, :] = bd[j].reshape(HALF, D)
        for i in range(2):
            rows = slice(512 * i, 512 * i + 512)
            u = dot(b[rows, :], w1[:, cols])
            phi = 0.5 * (1.0 + lax.erf(u * 0.7071067811865476))
            act[rows, cols] = (u * phi).astype(bf16)
            gp = phi + u * jnp.exp(-0.5 * u * u) * 0.3989422804014327
            dul = (gp * dot(dy_ref[rows, :], w2[cols, :], NT)).astype(bf16)
            du[rows, :] = dul
            db = dot(dul, w1[:, cols], NT)
            if j == 0:
                dbacc[rows, :] = db
            else:
                dbacc[rows, :] += db
            if (j, i) == (0, 0):
                advance((gu[1], 1), (gd[1], 0))
            if (j, i) == (0, 1):
                advance((gu[1], 2), (gd[1], 1))
            if (j, i) == (1, 0):
                rs_d[0].core_to_near()
                rs_u[0].core_to_near()
        sd[j] = dot(act[:, cols], dy_ref[...], TN).astype(bf16).reshape((2, 2, 2, 2, 48, D))
        start(rs_d[j].core)
        gup = dot(b[...], du[...], TN).astype(bf16)
        su[j] = dot(u512[0:D, :], gup, TN).astype(bf16).reshape(BOX + (PAD, HALF))
        start(rs_u[j].core)

    gg2 = jnp.zeros((1, D), f32)
    for i in range(2):
        rows = slice(512 * i, 512 * i + 512)
        n = hhat[rows, :]
        db = dbacc[rows, :]
        gg2 = gg2 + jnp.sum(db * n, axis=0, keepdims=True)
        dhl = dy_ref[rows, :].astype(f32) + norm_back(db * G2, n, rstd2[rows, 0:1])
        dh[rows, :] = dhl
        dhrl = dhl.astype(bf16)
        dhr[rows, :] = dhrl
        dct = dot(wo[...], dhrl, NT)
        for p in range(PAIRS):
            for s in range(4):
                t = 4 * i + s
                ri = rinv[p, t, 0:1, :]
                top = dct[128 * p:128 * p + 64, 128 * s:128 * s + 128].astype(bf16).astype(f32)
                low = dct[128 * p + 64:128 * p + 128, 128 * s:128 * s + 128].astype(bf16).astype(f32)
                dz[p, t, 0:64, 0:128] = (top * ri[:, 0:128]).astype(bf16)
                dz[p, t, 64:128, 128:256] = (low * ri[:, 128:256]).astype(bf16)
        if i == 0:
            rs_d[0].near_to_far()
            rs_u[0].near_to_far()
            rs_d[1].core_to_near()
        else:
            rs_u[1].core_to_near()
    gout = dot(ctxt[...], dhr[...]).astype(bf16)
    so[...] = dot(u512[0:D, :], gout, TN).astype(bf16).reshape(BOX + (PAD, D))
    start(rs_o.core)

    dkacc[...] = jnp.zeros_like(dkacc)
    dvacc[...] = jnp.zeros_like(dvacc)

    def rs_q(p):
        return Scatter(sq.at[p], cq.at[p], xq.at[p], yq.at[p], vq.at[p], hq.at[p], ssem.at[5 + p])

    def ln_q(p):
        return line_steps(sq.at[p], zq.at[p], ssem.at[5 + p])

    def scatter_progress(p, at):
        def ends(*pairs):
            for r, line in pairs:
                r.end_far()
                if line is not None:
                    start(line)

        steps = {
            (0, 0): lambda: rs_o.core_to_near(),
            (0, 1): lambda: ends((rs_d[0], None), (rs_u[0], ln_u[0])),
            (1, 0): lambda: (rs_d[1].near_to_far(), rs_q(0).core_to_near()),
            (1, 1): lambda: rs_u[1].near_to_far(),
            (2, 0): lambda: (ends((rs_d[1], ln_d)), rs_o.near_to_far()),
            (2, 1): lambda: (ends((rs_u[1], ln_u[1])), rs_q(0).near_to_far(), rs_q(1).core_to_near()),
        }
        for q in range(PAIRS):
            if (q, at) in steps:
                @pl.when(p == q)
                def _(q=q):
                    steps[q, at]()

    def backward_pair(p, gg1):
        lanes = pl.ds(pl.multiple_of(p * 128, 128), 128)
        def pulls(t):
            ks, ke = KEYS[t]
            return dot(v_p[p, ks:ke, :], dz[p, t])

        def weigh(t, dp):
            e = es[t][p].astype(f32)
            tt = e * dp
            cc = jnp.sum(tt, axis=0, keepdims=True) * rinv[p, t, 0:1, :]
            return t, (tt - e * cc).astype(bf16)

        def spread(t, ds):
            ks, ke = KEYS[t]
            dvacc[p, ks:ke, :] += dot(es[t][p], dz[p, t], NT)
            dkacc[p, ks:ke, :] += dot(ds, qz[p, t], NT)
            dqt = dot(k_p[p, ks:ke, :], ds, TN)
            dqt = jnp.concatenate([dqt[0:64, 0:128], dqt[64:128, 128:256]], axis=0) * 0.125
            dqkv[p, 128 * t:128 * t + 128, 0:128] = dqt.T.astype(bf16)

        dp, last = pulls(0), None
        for t in range(TILES):
            ahead = pulls(t + 1) if t + 1 < TILES else None
            now = weigh(t, dp)
            if last is not None:
                spread(*last)
            dp, last = ahead, now
            if t == 3:
                scatter_progress(p, 0)
        spread(*last)
        scatter_progress(p, 1)
        dqkv[p, :, 128:256] = dkacc[p].astype(bf16)
        dqkv[p, :, 256:384] = dvacc[p].astype(bf16)
        g = dot(a[...], dqkv[p], TN)
        for j in range(3):
            wj = wqkv[:, pl.ds(pl.multiple_of(j * D + p * 128, 128), 128)].astype(f32)
            gg1 = gg1 + wj * g[:, 128 * j:128 * j + 128]
        gsum = jnp.sum(gg1.T, axis=0, keepdims=True) / G1
        grow = jnp.concatenate([gsum, gg2], axis=1)
        grow = jnp.where(gain_mask(), jnp.broadcast_to(grow, (32, 2 * D)), 0.0).astype(bf16)
        grow = dot(grow, gain_comb(), NT)
        grow = jnp.where(p == 2, grow, 0.0).astype(bf16)
        low = jnp.concatenate([grow, jnp.zeros((32, D - 128), bf16)], axis=1)
        full = jnp.concatenate([g.astype(bf16), low], axis=0)
        sq[p] = dot(u512[...], full, TN).astype(bf16).reshape(BOX + (PAD, D))
        start(rs_q(p).core)

        return gg1

    lax.fori_loop(0, PAIRS, backward_pair, jnp.zeros((D, 128), f32))

    def da_rows(i):
        rows = slice(512 * i, 512 * i + 512)
        da = jnp.zeros((512, D), f32)
        for p in range(PAIRS):
            w = jnp.concatenate([wqkv[:, j * D + p * 128:j * D + p * 128 + 128] for j in range(3)], axis=1)
            da = da + dot(dqkv[p, rows, :], w, NT)
        dbacc[rows, :] = dh[rows, :] + norm_back(da * G1, xhat[rows, :], rstd[rows, 0:1])
        copy = pltpu.make_async_copy(dbacc.at[rows], gx_hbm.at[rows], lsem.at[i])
        copy.start()
        return copy

    def from_slot(v, width, rows, dst, first=0, cols=None):
        for k, j in enumerate(cols if cols is not None else range(first, first + v.shape[1] // 128)):
            dst[pl.ds(j, rows, stride=width), :] = v[0:rows, 128 * k:128 * k + 128]

    def out_rows(i):
        rows = slice(512 * i, 512 * i + 512)
        out_v[rows, :] = (hid[rows, :] + dot(act[rows, :], w2[...])).astype(bf16)
        copy = pltpu.make_async_copy(out_v.at[rows], out_hbm.at[rows], lsem.at[2 + i])
        copy.start()
        return copy

    done = [da_rows(0)]
    rs_q(2).core_to_near()
    rs_o.end_far()
    start(ln_o)
    rs_q(0).end_far()
    start(ln_q(0))
    done.append(da_rows(1))
    rs_q(1).near_to_far()
    done.append(out_rows(0))
    rs_q(2).near_to_far()
    rs_q(1).end_far()
    start(ln_q(1))
    done.append(out_rows(1))
    for j in range(2):
        wait(ln_u[j])
        from_slot(line_sum(su.at[j], zu.at[j]), 12, 12, ou, 6 * j)
    wait(ln_d)
    from_slot(line_sum(sd, zd), 3, 48, od)
    wait(ln_o)
    from_slot(line_sum(so, zo), 3, 12, oo)
    rs_q(2).end_far()
    start(ln_q(2))
    for p in range(PAIRS):
        wait(ln_q(p))
        v = line_sum(sq.at[p], zq.at[p])
        from_slot(v, 9, 12, oq, cols=(p, 3 + p, 6 + p))
        if p == 2:
            og[...] = v[12:13, 0:24]
    for q in done:
        q.wait()


def vm(shape, dtype):
    return pltpu.VMEM(shape, dtype)


WIDE = ((PAIRS,), (PAD, D)), ((), (PAD, D)), ((2,), (PAD, HALF)), ((), (48, D))


def layer(x, seg, fq, fo, fu, fd, fg, dy):
    spec = pl.BlockSpec(memory_space=pltpu.VMEM)
    hbm = pl.BlockSpec(memory_space=pl.ANY)
    dma = pltpu.SemaphoreType.DMA
    scratch = [
        vm((PAIRS,) + BOX + (PAD, D), bf16), vm(BOX + (PAD, D), bf16), vm((2,) + BOX + (PAD, HALF), bf16),
        vm(BOX + (48, D), bf16),
        vm((D + 32, 512), bf16), vm((D, 3 * D), bf16), vm((D, D), bf16), vm((D, FF), bf16), vm((FF, D), bf16),
        vm((8, D), f32), vm((144, 128), f32), vm((PAD, 128), f32),
        vm((T, D), f32), vm((T, 128), f32), vm((T, D), bf16), vm((PAIRS, T, 128), bf16), vm((PAIRS, T, 128), bf16),
        vm((PAIRS, TILES, 128, 256), bf16), vm((T, D), bf16), vm((D, T), bf16), vm((PAIRS, TILES, 8, 256), f32),
        vm((T, D), f32), vm((T, 128), f32), vm((T, D), bf16), vm((T, FF), bf16), vm((T, HALF), bf16),
        vm((T, D), f32), vm((T, D), f32), vm((T, D), bf16), vm((T, D), f32), vm((T, D), bf16),
        vm((PAIRS, TILES, 128, 256), bf16), vm((PAIRS, T, 128), f32), vm((PAIRS, T, 128), f32),
        vm((PAIRS, T, D), bf16),
        [vm((PAIRS, ke - ks, 256), bf16) for ks, ke in KEYS],
        [vm((ke - ks, 128), f32) for ks, ke in KEYS],
    ]
    for lead in (BOX, BOX[:4], BOX[:2], BOX[:2], BOX[:1], BOX[:1], (3,)):
        scratch += [vm(g + lead + s, bf16) for g, s in WIDE]
    scratch += [dma((8, 2, 8)), dma((8, 2, 8)), dma((4,))]
    flops = 2 * T * (3 * (3 * D * D + D * D + 2 * D * FF)) + 12 * 2 * 330 * T * D
    return pl.pallas_call(
        layer_kernel,
        out_shape=[
            jax.ShapeDtypeStruct((T, D), bf16),
            jax.ShapeDtypeStruct((T, D), f32),
            jax.ShapeDtypeStruct(fq.shape, f32),
            jax.ShapeDtypeStruct(fo.shape, f32),
            jax.ShapeDtypeStruct(fu.shape, f32),
            jax.ShapeDtypeStruct(fd.shape, f32),
            jax.ShapeDtypeStruct(fg.shape, f32),
        ],
        in_specs=[spec] * 8,
        out_specs=[hbm] * 2 + [spec] * 5,
        scratch_shapes=scratch,
        compiler_params=pltpu.CompilerParams(collective_id=0, has_side_effects=True, vmem_limit_bytes=62 * 2**20),
        cost_estimate=pl.CostEstimate(flops=flops, bytes_accessed=5 * 2**20, transcendentals=T * (FF + 2508)),
        name="layer",
    )(x, seg, fq, fo, fu, fd, fg, dy)


def hand_over_kernel(*refs):
    ins, outs, stage, sem = refs[:7], refs[7:14], refs[14:21], refs[21]
    loads, stores = [], []
    for i, (src, mid, dst) in enumerate(zip(ins, stage, outs)):
        parts = PARTS if src.shape[0] == T else 1
        n = src.shape[0] // parts
        for k in range(parts):
            rows = pl.ds(n * k, n)
            loads.append(pltpu.make_async_copy(src.at[rows], mid.at[rows], sem.at[0, i, k]))
            stores.append(pltpu.make_async_copy(mid.at[rows], dst.at[rows], sem.at[1, i, k]))
    for q in loads:
        q.start()
    for p, q in zip(loads, stores):
        p.wait()
        q.start()
    for q in stores:
        q.wait()


PARTS = 4


def hand_over(arrays):
    hbm = pl.BlockSpec(memory_space=pl.ANY)
    return pl.pallas_call(
        hand_over_kernel,
        out_shape=[jax.ShapeDtypeStruct(v.shape, v.dtype) for v in arrays],
        in_specs=[hbm] * 7,
        out_specs=[hbm] * 7,
        scratch_shapes=[pltpu.VMEM(v.shape, v.dtype) for v in arrays] + [pltpu.SemaphoreType.DMA((2, 7, PARTS))],
        name="hand_over",
    )(*arrays)


def body_direct(tokens, seg_ids, w_qkv, w_out, w_up, w_down, norm_gains, cotangent):
    def lanes(w):
        return w.reshape(-1, 128)

    out, gx, oq, oo, ou, od, og = hand_over(layer(
        tokens[0], seg_ids, lanes(w_qkv), lanes(w_out), lanes(w_up), lanes(w_down), norm_gains.reshape(1, -1),
        cotangent[0]))
    return (out[None], gx[None], oq.reshape(-1), oo.reshape(-1), ou.reshape(-1), od.reshape(-1), og.reshape(-1))


def plain_kernel(x_ref, seg_ref, wqkv_ref, wo_ref, w1_ref, w2_ref, gain_ref, dy_ref,
           out_ref, gx_ref, gqkv_ref, gout_ref, gup_ref, gdown_ref, ggain_ref,
           xhat, rstd, a, k_p, v_p, qz, ctx, ctxt, h, rinv, b, act, du, dh, dhr, dz, dkacc, dvacc, dqkv, *rest):
    es, biases = rest[:8], rest[8:]
    G1 = gain_ref[0:1, :]
    G2 = gain_ref[1:2, :]
    R = 256
    qz[...] = jnp.zeros_like(qz)
    dz[...] = jnp.zeros_like(dz)

    def stage_a(i, _):
        rows = pl.ds(pl.multiple_of(i * R, R), R)
        n, r = norm_rows(x_ref[rows, :].astype(f32))
        xhat[rows, :] = n
        rstd[0, rows, :] = jnp.broadcast_to(r, (R, 128))
        al = (n * G1).astype(bf16)
        a[rows, :] = al
        q = dot(al, wqkv_ref[:, 0:D]).astype(bf16).astype(f32) * 0.125
        kk = dot(al, wqkv_ref[:, D:2 * D]).astype(bf16)
        vv = dot(al, wqkv_ref[:, 2 * D:]).astype(bf16)
        for p in range(PAIRS):
            k_p[p, rows, :] = kk[:, 128 * p:128 * p + 128]
            v_p[p, rows, :] = vv[:, 128 * p:128 * p + 128]
            for s in range(R // 128):
                qt = q[128 * s:128 * s + 128, 128 * p:128 * p + 128].T.astype(bf16)
                qz[p, i * (R // 128) + s, 0:64, 0:128] = qt[0:64]
                qz[p, i * (R // 128) + s, 64:128, 128:256] = qt[64:128]
        return 0

    lax.fori_loop(0, T // R, stage_a, 0)

    segf = seg_ref[0:1, :].astype(f32)
    segcol = jnp.broadcast_to(segf, (128, T)).T
    for t in range(8):
        ks, ke = KEYS[t]
        biases[t][...] = jnp.where(segcol[ks:ke, :] == segf[:, 128 * t:128 * t + 128], 0.0, NEG)

    def att(p, _):
        lanes = pl.ds(pl.multiple_of(p * 128, 128), 128)
        for t in range(8):
            ks, ke = KEYS[t]
            s = dot(k_p[p, ks:ke, :], qz[p, t])
            ee, ri = [], []
            for half in range(2):
                sh = s[:, 128 * half:128 * half + 128] + biases[t][...]
                m = jnp.max(sh, axis=0, keepdims=True)
                ex = jnp.exp(sh - m)
                ri.append(1.0 / jnp.sum(ex, axis=0, keepdims=True))
                ee.append(ex.astype(bf16))
            e = jnp.concatenate(ee, axis=1)
            es[t][p] = e
            rr = jnp.concatenate(ri, axis=1)
            rinv[p, t] = jnp.broadcast_to(rr, (8, 256))
            ct = dot(v_p[p, ks:ke, :], e, TN)
            ct = jnp.concatenate([ct[0:64, 0:128] * ri[0], ct[64:128, 128:256] * ri[1]], axis=0)
            ctxt[lanes, 128 * t:128 * t + 128] = ct.astype(bf16)
            ctx[128 * t:128 * t + 128, lanes] = ct.T.astype(bf16)
        return 0

    lax.fori_loop(0, PAIRS, att, 0)

    FC = 512
    def stage_d(i, gacc):
        rows = pl.ds(pl.multiple_of(i * R, R), R)
        hh = x_ref[rows, :].astype(f32) + dot(ctx[rows, :], wo_ref[...])
        n, r = norm_rows(hh)
        bl = (n * G2).astype(bf16)
        b[rows, :] = bl
        dyl = dy_ref[rows, :]
        o = hh
        db = jnp.zeros((R, D), f32)
        for c in range(FF // FC):
            cols = slice(c * FC, c * FC + FC)
            u = dot(bl, w1_ref[:, cols])
            phi = 0.5 * (1.0 + lax.erf(u * 0.7071067811865476))
            al = (u * phi).astype(bf16)
            act[rows, cols] = al
            o = o + dot(al, w2_ref[cols, :])
            gp = phi + u * jnp.exp(-0.5 * u * u) * 0.3989422804014327
            dul = (gp * dot(dyl, w2_ref[cols, :], NT)).astype(bf16)
            du[rows, cols] = dul
            db = db + dot(dul, w1_ref[:, cols], NT)
        out_ref[rows, :] = o.astype(bf16)
        gacc = gacc + jnp.sum(db * n, axis=0, keepdims=True)
        dhl = dyl.astype(f32) + norm_back(db * G2, n, r)
        dh[rows, :] = dhl
        dhrl = dhl.astype(bf16)
        dhr[rows, :] = dhrl
        dct = dot(wo_ref[...], dhrl, NT)
        for p in range(PAIRS):
            for s in range(R // 128):
                tt = i * (R // 128) + s
                ri = rinv[p, tt, 0:1, :]
                dz[p, tt, 0:64, 0:128] = (dct[128 * p:128 * p + 64, 128 * s:128 * s + 128].astype(bf16).astype(f32) * ri[:, 0:128]).astype(bf16)
                dz[p, tt, 64:128, 128:256] = (dct[128 * p + 64:128 * p + 128, 128 * s:128 * s + 128].astype(bf16).astype(f32) * ri[:, 128:256]).astype(bf16)
        return gacc

    def sd():
        ggain_ref[1:2, :] = lax.fori_loop(0, T // R, stage_d, jnp.zeros((1, D), f32))
    sd()

    def w_down(i, _):
        cols = pl.ds(pl.multiple_of(i * 256, 256), 256)
        gdown_ref[cols, :] = dot(act[:, cols], dy_ref[...], TN)
        gup_ref[:, cols] = dot(b[...], du[:, cols], TN)
        return 0

    lax.fori_loop(0, FF // 256, w_down, 0)
    gout_ref[...] = dot(ctxt[...], dhr[...])

    dkacc[...] = jnp.zeros_like(dkacc)
    dvacc[...] = jnp.zeros_like(dvacc)
    def attb(p, _):
        lanes = pl.ds(pl.multiple_of(p * 128, 128), 128)
        for t in range(8):
            ks, ke = KEYS[t]
            dzl = dz[p, t]
            dp = dot(v_p[p, ks:ke, :], dzl)
            e = es[t][p]
            ef = e.astype(f32)
            tt = ef * dp
            c = jnp.sum(tt, axis=0, keepdims=True) * rinv[p, t, 0:1, :]
            ds = (tt - ef * c).astype(bf16)
            dvacc[p, ks:ke, :] += dot(e, dzl, NT)
            dkacc[p, ks:ke, :] += dot(ds, qz[p, t], NT)
            dqt = dot(k_p[p, ks:ke, :], ds, TN)
            dqt = jnp.concatenate([dqt[0:64, 0:128], dqt[64:128, 128:256]], axis=0) * 0.125
            dqkv[128 * t:128 * t + 128, lanes] = dqt.T.astype(bf16)
        return 0

    lax.fori_loop(0, PAIRS, attb, 0)
    for p in range(PAIRS):
        dqkv[:, D + 128 * p:D + 128 * p + 128] = dkacc[p].astype(bf16)
        dqkv[:, 2 * D + 128 * p:2 * D + 128 * p + 128] = dvacc[p].astype(bf16)

    def w_qkv(i, _):
        cols = pl.ds(pl.multiple_of(i * 384, 384), 384)
        gqkv_ref[:, cols] = dot(a[...], dqkv[:, cols], TN)
        return 0

    lax.fori_loop(0, 3, w_qkv, 0)

    def stage_g(i, gacc):
        rows = pl.ds(pl.multiple_of(i * R, R), R)
        da = dot(dqkv[rows, :], wqkv_ref[...], NT)
        n = xhat[rows, :]
        gacc = gacc + jnp.sum(da * n, axis=0, keepdims=True)
        gx_ref[rows, :] = dh[rows, :] + norm_back(da * G1, n, rstd[0, rows, 0:1])
        return gacc

    def sg():
        ggain_ref[0:1, :] = lax.fori_loop(0, T // R, stage_g, jnp.zeros((1, D), f32))
    sg()


PLAIN_SCRATCH = [
    pltpu.VMEM((T, D), f32),
    pltpu.VMEM((1, T, 128), f32),
    pltpu.VMEM((T, D), bf16),
    pltpu.VMEM((PAIRS, T, 128), bf16),
    pltpu.VMEM((PAIRS, T, 128), bf16),
    pltpu.VMEM((PAIRS, 8, 128, 256), bf16),
    pltpu.VMEM((T, D), bf16),
    pltpu.VMEM((D, T), bf16),
    pltpu.VMEM((8, 128), f32),
    pltpu.VMEM((PAIRS, 8, 8, 256), f32),
    pltpu.VMEM((T, D), bf16),
    pltpu.VMEM((T, FF), bf16),
    pltpu.VMEM((T, FF), bf16),
    pltpu.VMEM((T, D), f32),
    pltpu.VMEM((T, D), bf16),
    pltpu.VMEM((PAIRS, 8, 128, 256), bf16),
    pltpu.VMEM((PAIRS, T, 128), f32),
    pltpu.VMEM((PAIRS, T, 128), f32),
    pltpu.VMEM((T, 3 * D), bf16),
] + [pltpu.VMEM((PAIRS, ke - ks, 256), bf16) for ks, ke in KEYS] + [pltpu.VMEM((ke - ks, 128), f32) for ks, ke in KEYS]


def plain_layer(x, seg, wqkv, wo, w1, w2, gains, dy):
    vm = pl.BlockSpec(memory_space=pltpu.VMEM)
    return pl.pallas_call(
        plain_kernel,
        out_shape=[
            jax.ShapeDtypeStruct((T, D), bf16),
            jax.ShapeDtypeStruct((T, D), f32),
            jax.ShapeDtypeStruct((D, 3 * D), f32),
            jax.ShapeDtypeStruct((D, D), f32),
            jax.ShapeDtypeStruct((D, FF), f32),
            jax.ShapeDtypeStruct((FF, D), f32),
            jax.ShapeDtypeStruct((2, D), f32),
        ],
        in_specs=[vm] * 8,
        out_specs=[vm] * 7,
        scratch_shapes=PLAIN_SCRATCH,
        compiler_params=pltpu.CompilerParams(vmem_limit_bytes=62 * 2**20),
        name="plain_layer",
    )(x, seg, wqkv, wo, w1, w2, gains, dy)


def body_plain(tokens, seg_ids, w_qkv, w_out, w_up, w_down, norm_gains, cotangent):
    whole = [lax.all_gather(w, "fsdp", axis=0, tiled=True) for w in (w_qkv, w_out, w_up, w_down, norm_gains)]
    out, gx, *grads = plain_layer(
        tokens[0], seg_ids, whole[0].reshape(D, 3 * D), whole[1].reshape(D, D), whole[2].reshape(D, FF),
        whole[3].reshape(FF, D), whole[4].astype(f32).reshape(2, D), cotangent[0])
    shards = [lax.psum_scatter(g.reshape(-1), "fsdp", scatter_dimension=0, tiled=True) for g in grads]
    return (out[None], gx[None], *shards)


def solution(mesh):
    direct = mesh.shape["fsdp"] == DEVICES
    rows, flat = P("fsdp", None, None), P("fsdp")
    return jax.shard_map(
        body_direct if direct else body_plain,
        mesh=mesh,
        in_specs=(rows, P("fsdp", None), flat, flat, flat, flat, flat, rows),
        out_specs=(rows, rows, flat, flat, flat, flat, flat),
        check_vma=False,
    )
```

```python
import functools

import jax
import jax.numpy as jnp
from jax import lax
from jax.experimental import pallas as pl
from jax.experimental.pallas import tpu as pltpu
from jax.sharding import PartitionSpec as P

MESH = pl.DeviceIdType.MESH
f32, bf16 = jnp.float32, jnp.bfloat16
D, HEADS, HD, FF, T = 384, 6, 64, 1536, 1024
PAIRS, TILES = 3, 8
EPS = 1e-6
NEG = -1e30
HALF = FF // 2
PAD = 16
KEYS = [(0, 160), (96, 320), (240, 416), (352, 1024)] + [(496, 1024)] * 4
NN = (((1,), (0,)), ((), ()))
NT = (((1,), (1,)), ((), ()))
TN = (((0,), (0,)), ((), ()))
DEVICES = 32
AHEAD = 4


def dot(a, b, dims=NN):
    return lax.dot_general(a, b, dims, preferred_element_type=f32)


def norm_rows(v):
    c = v - jnp.mean(v, axis=-1, keepdims=True)
    r = lax.rsqrt(jnp.mean(c * c, axis=-1, keepdims=True) + EPS)
    return c * r, r


def norm_back(g, xhat, r):
    m1 = jnp.mean(g, axis=-1, keepdims=True)
    m2 = jnp.mean(g * xhat, axis=-1, keepdims=True)
    return (g - m1 - xhat * m2) * r


def spread_matrix(rows, cols):
    r = lax.broadcasted_iota(jnp.int32, (rows, cols), 0)
    q = lax.broadcasted_iota(jnp.int32, (rows, cols), 1)
    at = jnp.where(r < D, r + 4 * ((r * 21846) >> 18), 16 * (r - D) + 12)
    return (at == q).astype(f32).astype(bf16)


def gain_mask():
    d = lax.broadcasted_iota(jnp.int32, (32, 2 * D), 0)
    j = lax.broadcasted_iota(jnp.int32, (32, 2 * D), 1)
    return ((j * 43691) >> 20) == d


def gain_comb():
    i = lax.broadcasted_iota(jnp.int32, (128, 2 * D), 0)
    j = lax.broadcasted_iota(jnp.int32, (128, 2 * D), 1)
    return (j - 24 * ((j * 43691) >> 20) == i).astype(f32).astype(bf16)


BOX = (2, 2, 2, 2, 2)


def place():
    me = lax.axis_index("fsdp")
    return me // 8, (me // 4) % 2, (me // 2) % 2, me % 2


def device(z, y, x, c):
    return (((z * 2 + y) * 2 + x) * 2 + c,)


class Copy:
    def __init__(self, *args):
        self.args = args

    def make(self):
        src, dst, sems, i, to = self.args
        return pltpu.make_async_remote_copy(
            src_ref=src, dst_ref=dst, send_sem=sems.at[0, i], recv_sem=sems.at[1, i],
            device_id=device(*to), device_id_type=MESH)

    def start(self):
        self.make().start()

    def wait(self):
        self.make().wait()


def greet():
    z, y, x, c = place()
    barrier = pltpu.get_barrier_semaphore()
    partners = [(z, y, x, 1 - c), (z, y, 1 - x, c), (z, 1 - y, x, c), (z, 1 - y, 1 - x, c)]
    partners += [(z ^ m, y, x, c) for m in (1, 2, 3)]
    for p in partners:
        pl.semaphore_signal(barrier, inc=1, device_id=device(*p), device_id_type=MESH)
    return lambda: pl.semaphore_wait(barrier, len(partners))


def start(copies):
    for q in copies:
        q.start()


def wait(copies):
    for q in copies:
        q.wait()


def line_of(b, sems):
    z, y, x, c = place()
    own = b.at[z // 2, z % 2, y, x, c]
    return [Copy(own, own, sems, m - 1, (z ^ m, y, x, c)) for m in (1, 2, 3)]


def plane_direct(b, sems):
    z, y, x, c = place()
    col = b.at[:, :, y, x, c]
    near = [Copy(col, col, sems, 3, (z, y, 1 - x, c)), Copy(col, col, sems, 4, (z, 1 - y, x, c)),
            Copy(col, col, sems, 5, (z, 1 - y, 1 - x, c))]
    return [near, [Copy(b.at[:, :, :, :, c], b.at[:, :, :, :, c], sems, 7, (z, y, x, 1 - c))]]


def plane_first(b, sems):
    z, y, x, c = place()
    own, plane = b.at[z // 2, z % 2, y, x, c], b.at[z // 2, z % 2, :, :, c]
    near = [Copy(own, own, sems, m - 1, (z, y ^ (m >> 1), x ^ (m & 1), c)) for m in (1, 2, 3)]
    line = [Copy(plane, plane, sems, m + 2, (z ^ m, y, x, c)) for m in (1, 2, 3)]
    return [near, line, [Copy(b.at[:, :, :, :, c], b.at[:, :, :, :, c], sems, 7, (z, y, x, 1 - c))]]


def plane_split(b, sems, h=pl.ds(0, 2)):
    z, y, x, c = place()
    col = b.at[h, :, y, x, c]
    near = [Copy(col, col, sems, 3, (z, y, 1 - x, c)), Copy(col, col, sems, 4, (z, 1 - y, x, c))]
    fx, fy = b.at[h, 0, y, 1 - x, c], b.at[h, 1, 1 - y, x, c]
    far = [Copy(fx, fx, sems, 5, (z, 1 - y, x, c)), Copy(fy, fy, sems, 6, (z, y, 1 - x, c))]
    return [near, far, [Copy(b.at[h, :, :, :, c], b.at[h, :, :, :, c], sems, 7, (z, y, x, 1 - c))]]


class Scatter:
    def __init__(self, s, rc, rx, ry, sx, sy, sems, h=pl.ds(0, 2), nh=2):
        z, y, x, c = place()
        self.s, self.rc, self.rx, self.ry, self.sx, self.sy, self.h0, self.nh = s, rc, rx, ry, sx, sy, h.start, nh
        self.core = [Copy(s.at[h, :, :, :, 1 - c], rc.at[h], sems, 0, (z, y, x, 1 - c))]
        self.near = [
            Copy(s.at[h, 0, :, 1 - x, c], rx.at[h], sems, 1, (z, y, 1 - x, c)),
            Copy(s.at[h, 1, 1 - y, :, c], ry.at[h], sems, 2, (z, 1 - y, x, c)),
        ]
        self.far = [
            Copy(s.at[h, 0, 1 - y, x, c], sy.at[h], sems, 3, (z, 1 - y, x, c)),
            Copy(s.at[h, 1, y, 1 - x, c], sx.at[h], sems, 4, (z, y, 1 - x, c)),
        ]

    def add_core(self):
        z, y, x, c = place()
        s, rc = self.s, self.rc
        for i in range(self.h0, self.h0 + self.nh):
            for j in range(2):
                for k in range(2):
                    for l in range(2):
                        s[i, j, k, l, c] = (s[i, j, k, l, c].astype(f32) + rc[i, j, k, l].astype(f32)).astype(bf16)

    def add_near(self):
        z, y, x, c = place()
        s = self.s
        for i in range(self.h0, self.h0 + self.nh):
            s[i, 0, 1 - y, x, c] = (s[i, 0, 1 - y, x, c].astype(f32) + self.rx[i, 1 - y].astype(f32)).astype(bf16)
            s[i, 1, y, 1 - x, c] = (s[i, 1, y, 1 - x, c].astype(f32) + self.ry[i, 1 - x].astype(f32)).astype(bf16)

    def add_far(self):
        z, y, x, c = place()
        s = self.s
        for i in range(self.h0, self.h0 + self.nh):
            s[i, 0, y, x, c] = (s[i, 0, y, x, c].astype(f32) + self.rx[i, y].astype(f32)
                                + self.sy[i].astype(f32)).astype(bf16)
            s[i, 1, y, x, c] = (s[i, 1, y, x, c].astype(f32) + self.ry[i, x].astype(f32)
                                + self.sx[i].astype(f32)).astype(bf16)

    def core_to_near(self):
        wait(self.core)
        self.add_core()
        start(self.near)

    def near_to_far(self):
        wait(self.near)
        self.add_near()
        start(self.far)

    def end_far(self):
        wait(self.far)
        self.add_far()


class PlaneScatter(Scatter):
    def __init__(self, s, rc, rp, sems):
        z, y, x, c = place()
        self.s, self.rc, self.rp, self.h0, self.nh = s, rc, rp, 0, 2
        self.core = [Copy(s.at[:, :, :, :, 1 - c], rc, sems, 0, (z, y, x, 1 - c))]
        self.plane = [
            Copy(s.at[:, :, y ^ (m >> 1), x ^ (m & 1), c], rp.at[m - 1], sems, m, (z, y ^ (m >> 1), x ^ (m & 1), c))
            for m in (1, 2, 3)]

    def core_to_plane(self):
        wait(self.core)
        self.add_core()
        start(self.plane)

    def end_plane(self):
        z, y, x, c = place()
        wait(self.plane)
        for i in range(2):
            for j in range(2):
                t = self.s[i, j, y, x, c].astype(f32)
                for m in range(3):
                    t = t + self.rp[m, i, j].astype(f32)
                self.s[i, j, y, x, c] = t.astype(bf16)


def line_steps(s, rz, sems):
    z, y, x, c = place()
    return [Copy(s.at[(z ^ m) // 2, (z ^ m) % 2, y, x, c], rz.at[m - 1], sems, m + 4, (z ^ m, y, x, c))
            for m in (1, 2, 3)]


def line_sum(s, rz):
    z, y, x, c = place()
    return s[z // 2, z % 2, y, x, c].astype(f32) + rz[0].astype(f32) + rz[1].astype(f32) + rz[2].astype(f32)


def layer_kernel(
    x_hbm, seg_ref, fq, fo, fu, fd, fg, dy_hbm,
    out_hbm, gx_hbm, oq, oo, ou, od, og,
    bq, bo, bu, bd, u512, wqkv, wo, w1, gains, flat, sf,
    xhat, rstd, a, k_p, v_p, qz, ctx, ctxt, rinv, hhat, rstd2, act, du, hid, dbacc, dh, dhr, dz,
    dkacc, dvacc, dqkv, es, biases,
    sd, cq, co, cu, cd, xq, xo, xu, xd, yu, yd, vu, vd, hu, hd, zq, zo, zu, zd,
    x_ref, dy_ref, gsem, ssem, lsem,
):
    z, y, x, c = place()
    zh, zl = z // 2, z % 2

    greeted = greet()
    b = out_v = ctx
    sq, so, su = bq, bo, bu
    get_x = pltpu.make_async_copy(x_hbm, x_ref, lsem.at[4])
    get_x.start()
    get_dy = pltpu.make_async_copy(dy_hbm, dy_ref, lsem.at[5])
    get_dy.start()
    sf[...] = jnp.zeros_like(sf)

    def to_slot(src, width, rows, dst, cols):
        n = rows * width
        flat[0:n, :] = src[...].astype(f32)
        for j in cols:
            piece = flat[pl.ds(j, rows, stride=width), :]
            if rows == 12:
                sf[0:12, :] = piece
                piece = sf[...]
            ref, k = dst(j)
            ref[zh, zl, y, x, c, :, 128 * k:128 * k + 128] = piece.astype(bf16)
            if width == 9 and j == 0:
                sf[...] = jnp.zeros_like(sf)

    sf[12:13, 0:24] = fg[...].astype(f32)
    to_slot(fq, 9, 12, lambda j: (bq.at[j % 3], j // 3), (0, 3, 6))
    gq = [[line_of(bq.at[p], gsem.at[p])] + plane_direct(bq.at[p], gsem.at[p]) for p in range(PAIRS)]
    go = [line_of(bo, gsem.at[3])] + plane_split(bo, gsem.at[3])
    gu = [[line_of(bu.at[0], gsem.at[4])] + plane_split(bu.at[0], gsem.at[4]), plane_first(bu.at[1], gsem.at[5])]
    gd_line = line_of(bd, gsem.at[6])
    gd = [plane_split(bd, gsem.at[6 + k], pl.ds(k, 1)) for k in range(2)]
    greeted()
    start(gq[0][0])
    to_slot(fq, 9, 12, lambda j: (bq.at[j % 3], j // 3), (1, 4, 7, 2, 5, 8))
    start(gq[1][0])
    start(gq[2][0])
    to_slot(fo, 3, 12, lambda j: (bo, j), range(3))
    start(go[0])
    to_slot(fu, 12, 12, lambda j: (bu.at[j // 6], j % 6), range(12))
    start(gu[0][0])
    to_slot(fd, 3, 48, lambda j: (bd, j), range(3))
    start(gd_line)
    start(gu[1][0])

    def norm_in(i, _):
        rows = pl.ds(pl.multiple_of(i * 512, 512), 512)
        n, r = norm_rows(x_ref[rows, :].astype(f32))
        xhat[rows, :] = n
        rstd[rows, :] = jnp.broadcast_to(r, (512, 128))
        return 0

    wait(gq[0][0])
    start(gq[0][1])
    get_x.wait()
    lax.fori_loop(0, T // 512, norm_in, 0)
    wait(gq[1][0])
    start(gq[1][1])
    wait(gq[2][0])
    start(gq[2][1])
    u512[...] = spread_matrix(D + 32, 512)
    qz[...] = jnp.zeros_like(qz)
    dz[...] = jnp.zeros_like(dz)
    wait(gq[0][1])
    start(gq[0][2])
    wait(gu[1][0])
    start(gu[1][1])
    wait(go[0])
    start(go[1])
    segf = seg_ref[0:1, :].astype(f32)
    segcol = jnp.broadcast_to(segf, (128, T)).T
    for t in range(TILES):
        ks, ke = KEYS[t]
        biases[t][...] = jnp.where(segcol[ks:ke, :] == segf[:, 128 * t:128 * t + 128], 0.0, NEG)
    comb, mask = gain_comb(), gain_mask()
    wait(gq[0][2])

    wide = bq[0, ..., 0:128].reshape(512, 128)
    g32 = dot(u512[D:, :], wide).astype(bf16)
    gall = jnp.sum(jnp.where(mask, dot(g32, comb), 0.0), axis=0, keepdims=True)
    gains[0:1, :] = gall[:, 0:D]
    gains[1:2, :] = gall[:, D:]
    G1 = gains[0:1, :]
    G2 = gains[1:2, :]
    a[...] = (xhat[...] * G1).astype(bf16)

    def advance(*moves):
        for g, k in moves:
            wait(g[k])
            start(g[k + 1])

    def project(p):
        if p > 0:
            wait(gq[p][2])
        w = dot(u512[0:D, :], bq[p].reshape(512, D)).astype(bf16)
        for j in range(3):
            wqkv[:, j * D + p * 128:j * D + p * 128 + 128] = w[:, 128 * j:128 * j + 128]
        for i in range(2):
            rows = slice(512 * i, 512 * i + 512)
            qkv = dot(a[rows, :], w)
            q = qkv[:, 0:128].astype(bf16).astype(f32) * 0.125
            k_p[p, rows, :] = qkv[:, 128:256].astype(bf16)
            v_p[p, rows, :] = qkv[:, 256:384].astype(bf16)
            for s in range(4):
                qt = q[128 * s:128 * s + 128, :].T.astype(bf16)
                qz[p, 4 * i + s, 0:64, 0:128] = qt[0:64]
                qz[p, 4 * i + s, 64:128, 128:256] = qt[64:128]

    def scores(p, t):
        ks, ke = KEYS[t]
        return dot(k_p[p, ks:ke, :], qz[p, t])

    def weigh(p, t, s):
        ee, ri = [], []
        for half in range(2):
            sh = s[:, 128 * half:128 * half + 128] + biases[t][...]
            m = jnp.max(sh, axis=0, keepdims=True)
            ex = jnp.exp(sh - m)
            ri.append(1.0 / jnp.sum(ex, axis=0, keepdims=True))
            ee.append(ex.astype(bf16))
        e = jnp.concatenate(ee, axis=1)
        es[t][p] = e
        rinv[p, t] = jnp.broadcast_to(jnp.concatenate(ri, axis=1), (8, 256))
        return p, t, e, ri

    def mix(p, t, e, ri):
        ks, ke = KEYS[t]
        ct = dot(v_p[p, ks:ke, :], e, TN)
        ct = jnp.concatenate([ct[0:64, 0:128] * ri[0], ct[64:128, 128:256] * ri[1]], axis=0)
        ctxt[128 * p:128 * p + 128, 128 * t:128 * t + 128] = ct.astype(bf16)
        ctx[128 * t:128 * t + 128, 128 * p:128 * p + 128] = ct.T.astype(bf16)

    def advance(*moves):
        for g, k in moves:
            wait(g[k])
            start(g[k + 1])

    moves = {
        (0, 0): lambda: advance((gq[1], 1), (gu[0], 0)),
        (0, 6): lambda: (advance((gq[2], 1), (go, 1)), wait(gd_line), start(gd[0][0])),
        (1, 0): lambda: advance((gu[0], 1)),
        (1, 6): lambda: (advance((gd[0], 0)), start(gd[1][0])),
        (2, 0): lambda: advance((go, 2)),
        (2, 4): lambda: advance((gu[0], 2)),
        (2, 7): lambda: advance((gd[0], 1)),
    }
    project(0)
    s, last = scores(0, 0), None
    for n in range(PAIRS * TILES):
        p, t = n // TILES, n % TILES
        if (p, t) in moves:
            moves[p, t]()
        if t == AHEAD and p + 1 < PAIRS:
            project(p + 1)
        ahead = scores((n + 1) // TILES, (n + 1) % TILES) if n + 1 < PAIRS * TILES else None
        now = weigh(p, t, s)
        if last is not None:
            mix(*last)
        s, last = ahead, now
    mix(*last)

    get_dy.wait()
    wait(go[3])
    wo[...] = dot(u512[0:D, :], bo[...].reshape(512, D)).astype(bf16)
    for i in range(2):
        rows = slice(512 * i, 512 * i + 512)
        hh = x_ref[rows, :].astype(f32) + dot(ctx[rows, :], wo[...])
        n, r = norm_rows(hh)
        hhat[rows, :] = n
        rstd2[rows, :] = jnp.broadcast_to(r, (512, 128))
        b[rows, :] = (n * G2).astype(bf16)
        hid[rows, :] = hh

    rs_u = [Scatter(su.at[j], cu.at[j], xu.at[j], yu.at[j], vu.at[j], hu.at[j], ssem.at[j]) for j in range(2)]
    rs_d = [Scatter(sd, cd, xd, yd, vd, hd, ssem.at[2 + j], pl.ds(j, 1), 1) for j in range(2)]
    rs_o = PlaneScatter(so, co, xo, ssem.at[4])
    ln_u = [line_steps(su.at[j], zu.at[j], ssem.at[j]) for j in range(2)]
    ln_d = line_steps(sd, zd, ssem.at[2])
    ln_o = line_steps(so, zo, ssem.at[4])

    def half(j):
        return slice(HALF * j, HALF * j + HALF)

    def block(i):
        return slice(512 * i, 512 * i + 512)

    def up(j, i):
        return dot(b[block(i), :], w1[:, half(j)])

    def bend(j, i, u):
        phi = 0.5 * (1.0 + lax.erf(u * 0.7071067811865476))
        act[block(i), half(j)] = (u * phi).astype(bf16)
        return phi + u * jnp.exp(-0.5 * u * u) * 0.3989422804014327

    def pull(j, i):
        return dot(dy_ref[block(i), :], bd[j].reshape(HALF, D), NT)

    def back(j, i, dul):
        du[block(i), :] = dul
        db = dot(dul, w1[:, half(j)], NT)
        if j == 0:
            dbacc[block(i), :] = db
        else:
            dbacc[block(i), :] += db

    def down_gradient(j):
        sd[j] = dot(act[:, half(j)], dy_ref[...], TN).astype(bf16).reshape((2, 2, 2, 2, 48, D))
        start(rs_d[j].core)

    def up_gradient(j):
        gup = dot(b[...], du[...], TN).astype(bf16)
        su[j] = dot(u512[0:D, :], gup, TN).astype(bf16).reshape(BOX + (PAD, HALF))
        start(rs_u[j].core)

    def arrive(j):
        wait(gu[j][-1])
        w1[:, half(j)] = dot(u512[0:D, :], bu[j].reshape(512, HALF)).astype(bf16)

    arrive(0)
    u, v = up(0, 0), up(0, 1)
    gp0 = bend(0, 0, u)
    du[block(0), :] = gp0.astype(bf16)
    gp1 = bend(0, 1, v)
    du[block(1), :] = gp1.astype(bf16)
    advance((gd[1], 0), (gu[1], 1))
    down_gradient(0)
    wait(gd[0][2])
    for i in range(2):
        back(0, i, (du[block(i), :].astype(f32) * pull(0, i)).astype(bf16))
    advance((gd[1], 1))
    up_gradient(0)
    arrive(1)
    u, v = up(1, 0), up(1, 1)
    gp0 = bend(1, 0, u)
    du[block(0), :] = gp0.astype(bf16)
    rs_d[0].core_to_near()
    gp1 = bend(1, 1, v)
    du[block(1), :] = gp1.astype(bf16)
    down_gradient(1)
    rs_u[0].core_to_near()
    wait(gd[1][2])
    for i in range(2):
        back(1, i, (du[block(i), :].astype(f32) * pull(1, i)).astype(bf16))
    up_gradient(1)

    gg2 = jnp.zeros((1, D), f32)
    for i in range(2):
        rows = slice(512 * i, 512 * i + 512)
        n = hhat[rows, :]
        db = dbacc[rows, :]
        gg2 = gg2 + jnp.sum(db * n, axis=0, keepdims=True)
        dhl = dy_ref[rows, :].astype(f32) + norm_back(db * G2, n, rstd2[rows, 0:1])
        dh[rows, :] = dhl
        dhrl = dhl.astype(bf16)
        dhr[rows, :] = dhrl
        dct = dot(wo[...], dhrl, NT)
        for p in range(PAIRS):
            for s in range(4):
                t = 4 * i + s
                ri = rinv[p, t, 0:1, :]
                top = dct[128 * p:128 * p + 64, 128 * s:128 * s + 128].astype(bf16).astype(f32)
                low = dct[128 * p + 64:128 * p + 128, 128 * s:128 * s + 128].astype(bf16).astype(f32)
                dz[p, t, 0:64, 0:128] = (top * ri[:, 0:128]).astype(bf16)
                dz[p, t, 64:128, 128:256] = (low * ri[:, 128:256]).astype(bf16)
        if i == 0:
            rs_d[0].near_to_far()
            rs_u[0].near_to_far()
            rs_d[1].core_to_near()
        else:
            rs_u[1].core_to_near()
    gout = dot(ctxt[...], dhr[...]).astype(bf16)
    so[...] = dot(u512[0:D, :], gout, TN).astype(bf16).reshape(BOX + (PAD, D))
    start(rs_o.core)


    rs_q = [PlaneScatter(sq.at[p], cq.at[p], xq.at[p], ssem.at[5 + p]) for p in range(PAIRS)]
    ln_q = [line_steps(sq.at[p], zq.at[p], ssem.at[5 + p]) for p in range(PAIRS)]

    def ends(r, line=None):
        r.end_far()
        if line is not None:
            start(line)

    def plane_ends(r, line):
        r.end_plane()
        start(line)

    def pulls(p, t):
        ks, ke = KEYS[t]
        return dot(v_p[p, ks:ke, :], dz[p, t])

    def slope(p, t, dp):
        e = es[t][p].astype(f32)
        tt = e * dp
        cc = jnp.sum(tt, axis=0, keepdims=True) * rinv[p, t, 0:1, :]
        return p, t, (tt - e * cc).astype(bf16)

    def spread(p, t, ds):
        ks, ke = KEYS[t]
        dv = dot(es[t][p], dz[p, t], NT)
        dk = dot(ds, qz[p, t], NT)
        if t == 0:
            dvacc[p % 2] = jnp.zeros((T, 128), f32)
            dkacc[p % 2] = jnp.zeros((T, 128), f32)
        dvacc[p % 2, ks:ke, :] += dv
        dkacc[p % 2, ks:ke, :] += dk
        dqt = dot(k_p[p, ks:ke, :], ds, TN)
        dqt = jnp.concatenate([dqt[0:64, 0:128], dqt[64:128, 128:256]], axis=0) * 0.125
        dqkv[p, 128 * t:128 * t + 128, 0:128] = dqt.T.astype(bf16)

    def pair_gradient(p, gg1):
        dqkv[p, :, 128:256] = dkacc[p % 2].astype(bf16)
        dqkv[p, :, 256:384] = dvacc[p % 2].astype(bf16)
        g = dot(a[...], dqkv[p], TN)
        for j in range(3):
            gg1 = gg1 + wqkv[:, j * D + p * 128:j * D + p * 128 + 128].astype(f32) * g[:, 128 * j:128 * j + 128]
        full = g.astype(bf16)
        if p == PAIRS - 1:
            gsum = jnp.sum(gg1.T, axis=0, keepdims=True) / G1
            grow = jnp.concatenate([gsum, gg2], axis=1)
            grow = jnp.where(gain_mask(), jnp.broadcast_to(grow, (32, 2 * D)), 0.0).astype(bf16)
            grow = dot(grow, gain_comb(), NT).astype(bf16)
            low = jnp.concatenate([grow, jnp.zeros((32, D - 128), bf16)], axis=1)
            full = dot(u512[...], jnp.concatenate([full, low], axis=0), TN)
        else:
            full = dot(u512[0:D, :], full, TN)
        sq[p] = full.astype(bf16).reshape(BOX + (PAD, D))
        start(rs_q[p].core)
        return gg1

    moves = {
        (0, 4): lambda: rs_o.core_to_plane(),
        (0, 6): lambda: (ends(rs_d[0]), ends(rs_u[0], ln_u[0])),
        (1, 4): lambda: rs_q[0].core_to_plane(),
        (1, 7): lambda: rs_d[1].near_to_far(),
        (2, 0): lambda: rs_u[1].near_to_far(),
        (2, 2): lambda: plane_ends(rs_o, ln_o),
        (2, 4): lambda: (rs_q[1].core_to_plane(), plane_ends(rs_q[0], ln_q[0])),
        (2, 6): lambda: (ends(rs_d[1], ln_d), ends(rs_u[1], ln_u[1])),
    }
    gg1 = jnp.zeros((D, 128), f32)
    dp, last = pulls(0, 0), None
    for n in range(PAIRS * TILES):
        p, t = n // TILES, n % TILES
        if (p, t) in moves:
            moves[p, t]()
        ahead = pulls((n + 1) // TILES, (n + 1) % TILES) if n + 1 < PAIRS * TILES else None
        now = slope(p, t, dp)
        if last is not None:
            spread(*last)
        dp, last = ahead, now
        if t == 1 and p > 0:
            gg1 = pair_gradient(p - 1, gg1)
    spread(*last)
    pair_gradient(PAIRS - 1, gg1)
    def da_rows(i):
        rows = slice(512 * i, 512 * i + 512)
        da = jnp.zeros((512, D), f32)
        for p in range(PAIRS):
            w = jnp.concatenate([wqkv[:, j * D + p * 128:j * D + p * 128 + 128] for j in range(3)], axis=1)
            da = da + dot(dqkv[p, rows, :], w, NT)
        dbacc[rows, :] = dh[rows, :] + norm_back(da * G1, xhat[rows, :], rstd[rows, 0:1])
        copy = pltpu.make_async_copy(dbacc.at[rows], gx_hbm.at[rows], lsem.at[i])
        copy.start()
        return copy

    def from_slot(v, width, rows, dst, first=0, cols=None):
        for k, j in enumerate(cols if cols is not None else range(first, first + v.shape[1] // 128)):
            dst[pl.ds(j, rows, stride=width), :] = v[0:rows, 128 * k:128 * k + 128]

    w2 = bd[...].reshape(FF, D)

    def out_rows(i):
        rows = slice(512 * i, 512 * i + 512)
        out_v[rows, :] = (hid[rows, :] + dot(act[rows, :], w2)).astype(bf16)
        copy = pltpu.make_async_copy(out_v.at[rows], out_hbm.at[rows], lsem.at[2 + i])
        copy.start()
        return copy

    done = [da_rows(0)]
    rs_q[2].core_to_plane()
    plane_ends(rs_q[1], ln_q[1])
    done.append(da_rows(1))
    done.append(out_rows(0))
    plane_ends(rs_q[2], ln_q[2])
    done.append(out_rows(1))
    for j in range(2):
        wait(ln_u[j])
        from_slot(line_sum(su.at[j], zu.at[j]), 12, 12, ou, 6 * j)
    wait(ln_d)
    from_slot(line_sum(sd, zd), 3, 48, od)
    wait(ln_o)
    from_slot(line_sum(so, zo), 3, 12, oo)
    for p in range(PAIRS):
        wait(ln_q[p])
        v = line_sum(sq.at[p], zq.at[p])
        from_slot(v, 9, 12, oq, cols=(p, 3 + p, 6 + p))
        if p == 2:
            og[...] = v[12:13, 0:24]
    for q in done:
        q.wait()


def vm(shape, dtype):
    return pltpu.VMEM(shape, dtype)


WIDE = ((PAIRS,), (PAD, D)), ((), (PAD, D)), ((2,), (PAD, HALF)), ((), (48, D))


def layer(x, seg, fq, fo, fu, fd, fg, dy):
    spec = pl.BlockSpec(memory_space=pltpu.VMEM)
    hbm = pl.BlockSpec(memory_space=pl.ANY)
    dma = pltpu.SemaphoreType.DMA
    scratch = [
        vm((PAIRS,) + BOX + (PAD, D), bf16), vm(BOX + (PAD, D), bf16), vm((2,) + BOX + (PAD, HALF), bf16),
        vm(BOX + (48, D), bf16),
        vm((D + 32, 512), bf16), vm((D, 3 * D), bf16), vm((D, D), bf16), vm((D, FF), bf16),
        vm((8, D), f32), vm((144, 128), f32), vm((PAD, 128), f32),
        vm((T, D), f32), vm((T, 128), f32), vm((T, D), bf16), vm((PAIRS, T, 128), bf16), vm((PAIRS, T, 128), bf16),
        vm((PAIRS, TILES, 128, 256), bf16), vm((T, D), bf16), vm((D, T), bf16), vm((PAIRS, TILES, 8, 256), f32),
        vm((T, D), f32), vm((T, 128), f32), vm((T, FF), bf16), vm((T, HALF), bf16),
        vm((T, D), f32), vm((T, D), f32), vm((T, D), f32), vm((T, D), bf16),
        vm((PAIRS, TILES, 128, 256), bf16), vm((2, T, 128), f32), vm((2, T, 128), f32),
        vm((PAIRS, T, D), bf16),
        [vm((PAIRS, ke - ks, 256), bf16) for ks, ke in KEYS],
        [vm((ke - ks, 128), f32) for ks, ke in KEYS],
    ]
    scratch += [vm(BOX + (48, D), bf16)]
    scratch += [vm(g + BOX[:4] + s, bf16) for g, s in WIDE]
    scratch += [vm(g + (3, 2, 2) + s, bf16) for g, s in WIDE[:2]]
    scratch += [vm(g + BOX[:2] + s, bf16) for g, s in WIDE[2:]]
    for lead in (BOX[:2], BOX[:1], BOX[:1]):
        scratch += [vm(g + lead + s, bf16) for g, s in WIDE[2:]]
    scratch += [vm(g + (3,) + s, bf16) for g, s in WIDE]
    scratch += [vm((T, D), bf16), vm((T, D), bf16), dma((8, 2, 8)), dma((8, 2, 8)), dma((6,))]
    flops = 2 * T * (3 * (3 * D * D + D * D + 2 * D * FF)) + 12 * 2 * 330 * T * D
    return pl.pallas_call(
        layer_kernel,
        out_shape=[
            jax.ShapeDtypeStruct((T, D), bf16),
            jax.ShapeDtypeStruct((T, D), f32),
            jax.ShapeDtypeStruct(fq.shape, f32),
            jax.ShapeDtypeStruct(fo.shape, f32),
            jax.ShapeDtypeStruct(fu.shape, f32),
            jax.ShapeDtypeStruct(fd.shape, f32),
            jax.ShapeDtypeStruct(fg.shape, f32),
        ],
        in_specs=[hbm] + [spec] * 6 + [hbm],
        out_specs=[hbm] * 2 + [spec] * 5,
        scratch_shapes=scratch,
        compiler_params=pltpu.CompilerParams(collective_id=0, has_side_effects=True, vmem_limit_bytes=62 * 2**20),
        cost_estimate=pl.CostEstimate(flops=flops, bytes_accessed=5 * 2**20, transcendentals=T * (FF + 2508)),
        name="layer",
    )(x, seg, fq, fo, fu, fd, fg, dy)


def hand_over_kernel(*refs):
    ins, outs, stage, sem = refs[:7], refs[7:14], refs[14:21], refs[21]
    loads, stores = [], []
    for i, (src, mid, dst) in enumerate(zip(ins, stage, outs)):
        parts = PARTS if src.shape[0] == T else 1
        n = src.shape[0] // parts
        for k in range(parts):
            rows = pl.ds(n * k, n)
            loads.append(pltpu.make_async_copy(src.at[rows], mid.at[rows], sem.at[0, i, k]))
            stores.append(pltpu.make_async_copy(mid.at[rows], dst.at[rows], sem.at[1, i, k]))
    for q in loads:
        q.start()
    for p, q in zip(loads, stores):
        p.wait()
        q.start()
    for q in stores:
        q.wait()


PARTS = 4


def hand_over(arrays):
    hbm = pl.BlockSpec(memory_space=pl.ANY)
    return pl.pallas_call(
        hand_over_kernel,
        out_shape=[jax.ShapeDtypeStruct(v.shape, v.dtype) for v in arrays],
        in_specs=[hbm] * 7,
        out_specs=[hbm] * 7,
        scratch_shapes=[pltpu.VMEM(v.shape, v.dtype) for v in arrays] + [pltpu.SemaphoreType.DMA((2, 7, PARTS))],
        name="hand_over",
    )(*arrays)


def body_direct(tokens, seg_ids, w_qkv, w_out, w_up, w_down, norm_gains, cotangent):
    def lanes(w):
        return w.reshape(-1, 128)

    out, gx, oq, oo, ou, od, og = hand_over(layer(
        tokens[0], seg_ids, lanes(w_qkv), lanes(w_out), lanes(w_up), lanes(w_down), norm_gains.reshape(1, -1),
        cotangent[0]))
    return (out[None], gx[None], oq.reshape(-1), oo.reshape(-1), ou.reshape(-1), od.reshape(-1), og.reshape(-1))


def plain_kernel(x_ref, seg_ref, wqkv_ref, wo_ref, w1_ref, w2_ref, gain_ref, dy_ref,
           out_ref, gx_ref, gqkv_ref, gout_ref, gup_ref, gdown_ref, ggain_ref,
           xhat, rstd, a, k_p, v_p, qz, ctx, ctxt, h, rinv, b, act, du, dh, dhr, dz, dkacc, dvacc, dqkv, *rest):
    es, biases = rest[:8], rest[8:]
    G1 = gain_ref[0:1, :]
    G2 = gain_ref[1:2, :]
    R = 256
    qz[...] = jnp.zeros_like(qz)
    dz[...] = jnp.zeros_like(dz)

    def stage_a(i, _):
        rows = pl.ds(pl.multiple_of(i * R, R), R)
        n, r = norm_rows(x_ref[rows, :].astype(f32))
        xhat[rows, :] = n
        rstd[0, rows, :] = jnp.broadcast_to(r, (R, 128))
        al = (n * G1).astype(bf16)
        a[rows, :] = al
        q = dot(al, wqkv_ref[:, 0:D]).astype(bf16).astype(f32) * 0.125
        kk = dot(al, wqkv_ref[:, D:2 * D]).astype(bf16)
        vv = dot(al, wqkv_ref[:, 2 * D:]).astype(bf16)
        for p in range(PAIRS):
            k_p[p, rows, :] = kk[:, 128 * p:128 * p + 128]
            v_p[p, rows, :] = vv[:, 128 * p:128 * p + 128]
            for s in range(R // 128):
                qt = q[128 * s:128 * s + 128, 128 * p:128 * p + 128].T.astype(bf16)
                qz[p, i * (R // 128) + s, 0:64, 0:128] = qt[0:64]
                qz[p, i * (R // 128) + s, 64:128, 128:256] = qt[64:128]
        return 0

    lax.fori_loop(0, T // R, stage_a, 0)

    segf = seg_ref[0:1, :].astype(f32)
    segcol = jnp.broadcast_to(segf, (128, T)).T
    for t in range(8):
        ks, ke = KEYS[t]
        biases[t][...] = jnp.where(segcol[ks:ke, :] == segf[:, 128 * t:128 * t + 128], 0.0, NEG)

    def att(p, _):
        lanes = pl.ds(pl.multiple_of(p * 128, 128), 128)
        for t in range(8):
            ks, ke = KEYS[t]
            s = dot(k_p[p, ks:ke, :], qz[p, t])
            ee, ri = [], []
            for half in range(2):
                sh = s[:, 128 * half:128 * half + 128] + biases[t][...]
                m = jnp.max(sh, axis=0, keepdims=True)
                ex = jnp.exp(sh - m)
                ri.append(1.0 / jnp.sum(ex, axis=0, keepdims=True))
                ee.append(ex.astype(bf16))
            e = jnp.concatenate(ee, axis=1)
            es[t][p] = e
            rr = jnp.concatenate(ri, axis=1)
            rinv[p, t] = jnp.broadcast_to(rr, (8, 256))
            ct = dot(v_p[p, ks:ke, :], e, TN)
            ct = jnp.concatenate([ct[0:64, 0:128] * ri[0], ct[64:128, 128:256] * ri[1]], axis=0)
            ctxt[lanes, 128 * t:128 * t + 128] = ct.astype(bf16)
            ctx[128 * t:128 * t + 128, lanes] = ct.T.astype(bf16)
        return 0

    lax.fori_loop(0, PAIRS, att, 0)

    FC = 512
    def stage_d(i, gacc):
        rows = pl.ds(pl.multiple_of(i * R, R), R)
        hh = x_ref[rows, :].astype(f32) + dot(ctx[rows, :], wo_ref[...])
        n, r = norm_rows(hh)
        bl = (n * G2).astype(bf16)
        b[rows, :] = bl
        dyl = dy_ref[rows, :]
        o = hh
        db = jnp.zeros((R, D), f32)
        for c in range(FF // FC):
            cols = slice(c * FC, c * FC + FC)
            u = dot(bl, w1_ref[:, cols])
            phi = 0.5 * (1.0 + lax.erf(u * 0.7071067811865476))
            al = (u * phi).astype(bf16)
            act[rows, cols] = al
            o = o + dot(al, w2_ref[cols, :])
            gp = phi + u * jnp.exp(-0.5 * u * u) * 0.3989422804014327
            dul = (gp * dot(dyl, w2_ref[cols, :], NT)).astype(bf16)
            du[rows, cols] = dul
            db = db + dot(dul, w1_ref[:, cols], NT)
        out_ref[rows, :] = o.astype(bf16)
        gacc = gacc + jnp.sum(db * n, axis=0, keepdims=True)
        dhl = dyl.astype(f32) + norm_back(db * G2, n, r)
        dh[rows, :] = dhl
        dhrl = dhl.astype(bf16)
        dhr[rows, :] = dhrl
        dct = dot(wo_ref[...], dhrl, NT)
        for p in range(PAIRS):
            for s in range(R // 128):
                tt = i * (R // 128) + s
                ri = rinv[p, tt, 0:1, :]
                dz[p, tt, 0:64, 0:128] = (dct[128 * p:128 * p + 64, 128 * s:128 * s + 128].astype(bf16).astype(f32) * ri[:, 0:128]).astype(bf16)
                dz[p, tt, 64:128, 128:256] = (dct[128 * p + 64:128 * p + 128, 128 * s:128 * s + 128].astype(bf16).astype(f32) * ri[:, 128:256]).astype(bf16)
        return gacc

    def sd():
        ggain_ref[1:2, :] = lax.fori_loop(0, T // R, stage_d, jnp.zeros((1, D), f32))
    sd()

    def w_down(i, _):
        cols = pl.ds(pl.multiple_of(i * 256, 256), 256)
        gdown_ref[cols, :] = dot(act[:, cols], dy_ref[...], TN)
        gup_ref[:, cols] = dot(b[...], du[:, cols], TN)
        return 0

    lax.fori_loop(0, FF // 256, w_down, 0)
    gout_ref[...] = dot(ctxt[...], dhr[...])

    dkacc[...] = jnp.zeros_like(dkacc)
    dvacc[...] = jnp.zeros_like(dvacc)
    def attb(p, _):
        lanes = pl.ds(pl.multiple_of(p * 128, 128), 128)
        for t in range(8):
            ks, ke = KEYS[t]
            dzl = dz[p, t]
            dp = dot(v_p[p, ks:ke, :], dzl)
            e = es[t][p]
            ef = e.astype(f32)
            tt = ef * dp
            c = jnp.sum(tt, axis=0, keepdims=True) * rinv[p, t, 0:1, :]
            ds = (tt - ef * c).astype(bf16)
            dvacc[p, ks:ke, :] += dot(e, dzl, NT)
            dkacc[p, ks:ke, :] += dot(ds, qz[p, t], NT)
            dqt = dot(k_p[p, ks:ke, :], ds, TN)
            dqt = jnp.concatenate([dqt[0:64, 0:128], dqt[64:128, 128:256]], axis=0) * 0.125
            dqkv[128 * t:128 * t + 128, lanes] = dqt.T.astype(bf16)
        return 0

    lax.fori_loop(0, PAIRS, attb, 0)
    for p in range(PAIRS):
        dqkv[:, D + 128 * p:D + 128 * p + 128] = dkacc[p].astype(bf16)
        dqkv[:, 2 * D + 128 * p:2 * D + 128 * p + 128] = dvacc[p].astype(bf16)

    def w_qkv(i, _):
        cols = pl.ds(pl.multiple_of(i * 384, 384), 384)
        gqkv_ref[:, cols] = dot(a[...], dqkv[:, cols], TN)
        return 0

    lax.fori_loop(0, 3, w_qkv, 0)

    def stage_g(i, gacc):
        rows = pl.ds(pl.multiple_of(i * R, R), R)
        da = dot(dqkv[rows, :], wqkv_ref[...], NT)
        n = xhat[rows, :]
        gacc = gacc + jnp.sum(da * n, axis=0, keepdims=True)
        gx_ref[rows, :] = dh[rows, :] + norm_back(da * G1, n, rstd[0, rows, 0:1])
        return gacc

    def sg():
        ggain_ref[0:1, :] = lax.fori_loop(0, T // R, stage_g, jnp.zeros((1, D), f32))
    sg()


PLAIN_SCRATCH = [
    pltpu.VMEM((T, D), f32),
    pltpu.VMEM((1, T, 128), f32),
    pltpu.VMEM((T, D), bf16),
    pltpu.VMEM((PAIRS, T, 128), bf16),
    pltpu.VMEM((PAIRS, T, 128), bf16),
    pltpu.VMEM((PAIRS, 8, 128, 256), bf16),
    pltpu.VMEM((T, D), bf16),
    pltpu.VMEM((D, T), bf16),
    pltpu.VMEM((8, 128), f32),
    pltpu.VMEM((PAIRS, 8, 8, 256), f32),
    pltpu.VMEM((T, D), bf16),
    pltpu.VMEM((T, FF), bf16),
    pltpu.VMEM((T, FF), bf16),
    pltpu.VMEM((T, D), f32),
    pltpu.VMEM((T, D), bf16),
    pltpu.VMEM((PAIRS, 8, 128, 256), bf16),
    pltpu.VMEM((PAIRS, T, 128), f32),
    pltpu.VMEM((PAIRS, T, 128), f32),
    pltpu.VMEM((T, 3 * D), bf16),
] + [pltpu.VMEM((PAIRS, ke - ks, 256), bf16) for ks, ke in KEYS] + [pltpu.VMEM((ke - ks, 128), f32) for ks, ke in KEYS]


def plain_layer(x, seg, wqkv, wo, w1, w2, gains, dy):
    vm = pl.BlockSpec(memory_space=pltpu.VMEM)
    return pl.pallas_call(
        plain_kernel,
        out_shape=[
            jax.ShapeDtypeStruct((T, D), bf16),
            jax.ShapeDtypeStruct((T, D), f32),
            jax.ShapeDtypeStruct((D, 3 * D), f32),
            jax.ShapeDtypeStruct((D, D), f32),
            jax.ShapeDtypeStruct((D, FF), f32),
            jax.ShapeDtypeStruct((FF, D), f32),
            jax.ShapeDtypeStruct((2, D), f32),
        ],
        in_specs=[vm] * 8,
        out_specs=[vm] * 7,
        scratch_shapes=PLAIN_SCRATCH,
        compiler_params=pltpu.CompilerParams(vmem_limit_bytes=62 * 2**20),
        name="plain_layer",
    )(x, seg, wqkv, wo, w1, w2, gains, dy)


def body_plain(tokens, seg_ids, w_qkv, w_out, w_up, w_down, norm_gains, cotangent):
    whole = [lax.all_gather(w, "fsdp", axis=0, tiled=True) for w in (w_qkv, w_out, w_up, w_down, norm_gains)]
    out, gx, *grads = plain_layer(
        tokens[0], seg_ids, whole[0].reshape(D, 3 * D), whole[1].reshape(D, D), whole[2].reshape(D, FF),
        whole[3].reshape(FF, D), whole[4].astype(f32).reshape(2, D), cotangent[0])
    shards = [lax.psum_scatter(g.reshape(-1), "fsdp", scatter_dimension=0, tiled=True) for g in grads]
    return (out[None], gx[None], *shards)


def solution(mesh):
    direct = mesh.shape["fsdp"] == DEVICES
    rows, flat = P("fsdp", None, None), P("fsdp")
    return jax.shard_map(
        body_direct if direct else body_plain,
        mesh=mesh,
        in_specs=(rows, P("fsdp", None), flat, flat, flat, flat, flat, rows),
        out_specs=(rows, rows, flat, flat, flat, flat, flat),
        check_vma=False,
    )
```

```python
import functools

import jax
import jax.numpy as jnp
from jax import lax
from jax.experimental import pallas as pl
from jax.experimental.pallas import tpu as pltpu
from jax.sharding import PartitionSpec as P

MESH = pl.DeviceIdType.MESH
f32, bf16 = jnp.float32, jnp.bfloat16
D, HEADS, HD, FF, T = 384, 6, 64, 1536, 1024
PAIRS, TILES = 3, 8
EPS = 1e-6
NEG = -1e30
HALF = FF // 2
PAD = 16
KEYS = [(0, 160), (96, 320), (240, 416), (352, 1024)] + [(496, 1024)] * 4
NN = (((1,), (0,)), ((), ()))
NT = (((1,), (1,)), ((), ()))
TN = (((0,), (0,)), ((), ()))
DEVICES = 32
AHEAD = 4


def dot(a, b, dims=NN):
    return lax.dot_general(a, b, dims, preferred_element_type=f32)


def norm_rows(v):
    c = v - jnp.mean(v, axis=-1, keepdims=True)
    r = lax.rsqrt(jnp.mean(c * c, axis=-1, keepdims=True) + EPS)
    return c * r, r


def norm_back(g, xhat, r):
    m1 = jnp.mean(g, axis=-1, keepdims=True)
    m2 = jnp.mean(g * xhat, axis=-1, keepdims=True)
    return (g - m1 - xhat * m2) * r


def spread_matrix(rows, cols):
    r = lax.broadcasted_iota(jnp.int32, (rows, cols), 0)
    q = lax.broadcasted_iota(jnp.int32, (rows, cols), 1)
    at = jnp.where(r < D, r + 4 * ((r * 21846) >> 18), 16 * (r - D) + 12)
    return (at == q).astype(f32).astype(bf16)


def gain_mask():
    d = lax.broadcasted_iota(jnp.int32, (32, 2 * D), 0)
    j = lax.broadcasted_iota(jnp.int32, (32, 2 * D), 1)
    return ((j * 43691) >> 20) == d


def gain_comb():
    i = lax.broadcasted_iota(jnp.int32, (128, 2 * D), 0)
    j = lax.broadcasted_iota(jnp.int32, (128, 2 * D), 1)
    return (j - 24 * ((j * 43691) >> 20) == i).astype(f32).astype(bf16)


BOX = (2, 2, 2, 2, 2)


def place():
    me = lax.axis_index("fsdp")
    return me // 8, (me // 4) % 2, (me // 2) % 2, me % 2


def device(z, y, x, c):
    return (((z * 2 + y) * 2 + x) * 2 + c,)


class Copy:
    def __init__(self, *args):
        self.args = args

    def make(self):
        src, dst, sems, i, to = self.args
        return pltpu.make_async_remote_copy(
            src_ref=src, dst_ref=dst, send_sem=sems.at[0, i], recv_sem=sems.at[1, i],
            device_id=device(*to), device_id_type=MESH)

    def start(self):
        self.make().start()

    def wait(self):
        self.make().wait()


def greet():
    z, y, x, c = place()
    barrier = pltpu.get_barrier_semaphore()
    partners = [(z, y, x, 1 - c), (z, y, 1 - x, c), (z, 1 - y, x, c), (z, 1 - y, 1 - x, c)]
    partners += [(z ^ m, y, x, c) for m in (1, 2, 3)]
    for p in partners:
        pl.semaphore_signal(barrier, inc=1, device_id=device(*p), device_id_type=MESH)
    return lambda: pl.semaphore_wait(barrier, len(partners))


def start(copies):
    for q in copies:
        q.start()


def wait(copies):
    for q in copies:
        q.wait()


def line_of(b, sems):
    z, y, x, c = place()
    own = b.at[z // 2, z % 2, y, x, c]
    return [Copy(own, own, sems, m - 1, (z ^ m, y, x, c)) for m in (1, 2, 3)]


def plane_direct(b, sems):
    z, y, x, c = place()
    col = b.at[:, :, y, x, c]
    near = [Copy(col, col, sems, 3, (z, y, 1 - x, c)), Copy(col, col, sems, 4, (z, 1 - y, x, c)),
            Copy(col, col, sems, 5, (z, 1 - y, 1 - x, c))]
    return [near, [Copy(b.at[:, :, :, :, c], b.at[:, :, :, :, c], sems, 7, (z, y, x, 1 - c))]]


def plane_first(b, sems):
    z, y, x, c = place()
    own, plane = b.at[z // 2, z % 2, y, x, c], b.at[z // 2, z % 2, :, :, c]
    near = [Copy(own, own, sems, m - 1, (z, y ^ (m >> 1), x ^ (m & 1), c)) for m in (1, 2, 3)]
    line = [Copy(plane, plane, sems, m + 2, (z ^ m, y, x, c)) for m in (1, 2, 3)]
    return [near, line, [Copy(b.at[:, :, :, :, c], b.at[:, :, :, :, c], sems, 7, (z, y, x, 1 - c))]]


def plane_split(b, sems, h=pl.ds(0, 2)):
    z, y, x, c = place()
    col = b.at[h, :, y, x, c]
    near = [Copy(col, col, sems, 3, (z, y, 1 - x, c)), Copy(col, col, sems, 4, (z, 1 - y, x, c))]
    fx, fy = b.at[h, 0, y, 1 - x, c], b.at[h, 1, 1 - y, x, c]
    far = [Copy(fx, fx, sems, 5, (z, 1 - y, x, c)), Copy(fy, fy, sems, 6, (z, y, 1 - x, c))]
    return [near, far, [Copy(b.at[h, :, :, :, c], b.at[h, :, :, :, c], sems, 7, (z, y, x, 1 - c))]]


class Scatter:
    def __init__(self, s, rc, rx, ry, sx, sy, sems, h=pl.ds(0, 2), nh=2):
        z, y, x, c = place()
        self.s, self.rc, self.rx, self.ry, self.sx, self.sy, self.h0, self.nh = s, rc, rx, ry, sx, sy, h.start, nh
        self.core = [Copy(s.at[h, :, :, :, 1 - c], rc.at[h], sems, 0, (z, y, x, 1 - c))]
        self.near = [
            Copy(s.at[h, 0, :, 1 - x, c], rx.at[h], sems, 1, (z, y, 1 - x, c)),
            Copy(s.at[h, 1, 1 - y, :, c], ry.at[h], sems, 2, (z, 1 - y, x, c)),
        ]
        self.far = [
            Copy(s.at[h, 0, 1 - y, x, c], sy.at[h], sems, 3, (z, 1 - y, x, c)),
            Copy(s.at[h, 1, y, 1 - x, c], sx.at[h], sems, 4, (z, y, 1 - x, c)),
        ]

    def add_core(self):
        z, y, x, c = place()
        s, rc = self.s, self.rc
        for i in range(self.h0, self.h0 + self.nh):
            for j in range(2):
                for k in range(2):
                    for l in range(2):
                        s[i, j, k, l, c] = (s[i, j, k, l, c].astype(f32) + rc[i, j, k, l].astype(f32)).astype(bf16)

    def add_near(self):
        z, y, x, c = place()
        s = self.s
        for i in range(self.h0, self.h0 + self.nh):
            s[i, 0, 1 - y, x, c] = (s[i, 0, 1 - y, x, c].astype(f32) + self.rx[i, 1 - y].astype(f32)).astype(bf16)
            s[i, 1, y, 1 - x, c] = (s[i, 1, y, 1 - x, c].astype(f32) + self.ry[i, 1 - x].astype(f32)).astype(bf16)

    def add_far(self):
        z, y, x, c = place()
        s = self.s
        for i in range(self.h0, self.h0 + self.nh):
            s[i, 0, y, x, c] = (s[i, 0, y, x, c].astype(f32) + self.rx[i, y].astype(f32)
                                + self.sy[i].astype(f32)).astype(bf16)
            s[i, 1, y, x, c] = (s[i, 1, y, x, c].astype(f32) + self.ry[i, x].astype(f32)
                                + self.sx[i].astype(f32)).astype(bf16)

    def core_to_near(self):
        wait(self.core)
        self.add_core()
        start(self.near)

    def near_to_far(self):
        wait(self.near)
        self.add_near()
        start(self.far)

    def end_far(self):
        wait(self.far)
        self.add_far()


class PlaneScatter(Scatter):
    def __init__(self, s, rc, rp, sems):
        z, y, x, c = place()
        self.s, self.rc, self.rp, self.h0, self.nh = s, rc, rp, 0, 2
        self.core = [Copy(s.at[:, :, :, :, 1 - c], rc, sems, 0, (z, y, x, 1 - c))]
        self.plane = [
            Copy(s.at[:, :, y ^ (m >> 1), x ^ (m & 1), c], rp.at[m - 1], sems, m, (z, y ^ (m >> 1), x ^ (m & 1), c))
            for m in (1, 2, 3)]

    def core_to_plane(self):
        wait(self.core)
        self.add_core()
        start(self.plane)

    def end_plane(self):
        z, y, x, c = place()
        wait(self.plane)
        for i in range(2):
            for j in range(2):
                t = self.s[i, j, y, x, c].astype(f32)
                for m in range(3):
                    t = t + self.rp[m, i, j].astype(f32)
                self.s[i, j, y, x, c] = t.astype(bf16)


def line_steps(s, rz, sems):
    z, y, x, c = place()
    return [Copy(s.at[(z ^ m) // 2, (z ^ m) % 2, y, x, c], rz.at[m - 1], sems, m + 4, (z ^ m, y, x, c))
            for m in (1, 2, 3)]


def line_sum(s, rz):
    z, y, x, c = place()
    return s[z // 2, z % 2, y, x, c].astype(f32) + rz[0].astype(f32) + rz[1].astype(f32) + rz[2].astype(f32)


def layer_kernel(
    x_hbm, seg_ref, fq, fo, fu, fd, fg, dy_hbm,
    out_hbm, gx_hbm, oq, oo, ou, od, og,
    bq, bo, bu, bd, u512, wqkv, wo, w1, gains, flat, sf,
    xhat, rstd, a, k_p, v_p, qz, ctx, ctxt, rinv, hhat, rstd2, act, du, hid, dbacc, dh, dhr, dz,
    dkacc, dvacc, dqkv, es, biases,
    sd, cq, co, cu, cd, xq, xo, xu, xd, yu, yd, vu, vd, hu, hd, zq, zo, zu, zd,
    x_ref, dy_ref, gsem, ssem, lsem,
):
    z, y, x, c = place()
    zh, zl = z // 2, z % 2

    greeted = greet()
    b = out_v = ctx
    sq, so, su = bq, bo, bu
    get_x = pltpu.make_async_copy(x_hbm, x_ref, lsem.at[4])
    get_x.start()
    get_dy = pltpu.make_async_copy(dy_hbm, dy_ref, lsem.at[5])
    get_dy.start()
    sf[...] = jnp.zeros_like(sf)

    def to_slot(src, width, rows, dst, cols):
        n = rows * width
        flat[0:n, :] = src[...].astype(f32)
        for j in cols:
            piece = flat[pl.ds(j, rows, stride=width), :]
            if rows == 12:
                sf[0:12, :] = piece
                piece = sf[...]
            ref, k = dst(j)
            ref[zh, zl, y, x, c, :, 128 * k:128 * k + 128] = piece.astype(bf16)
            if width == 9 and j == 0:
                sf[...] = jnp.zeros_like(sf)

    sf[12:13, 0:24] = fg[...].astype(f32)
    to_slot(fq, 9, 12, lambda j: (bq.at[j % 3], j // 3), (0, 3, 6))
    gq = [[line_of(bq.at[p], gsem.at[p])] + plane_direct(bq.at[p], gsem.at[p]) for p in range(PAIRS)]
    go = [line_of(bo, gsem.at[3])] + plane_direct(bo, gsem.at[3])
    gu = [[line_of(bu.at[0], gsem.at[4])] + plane_split(bu.at[0], gsem.at[4]), plane_first(bu.at[1], gsem.at[5])]
    gd_line = line_of(bd, gsem.at[6])
    gd = [plane_split(bd, gsem.at[6 + k], pl.ds(k, 1)) for k in range(2)]
    greeted()
    start(gq[0][0])
    to_slot(fq, 9, 12, lambda j: (bq.at[j % 3], j // 3), (1, 4, 7, 2, 5, 8))
    start(gq[1][0])
    start(gq[2][0])
    to_slot(fo, 3, 12, lambda j: (bo, j), range(3))
    start(go[0])
    to_slot(fu, 12, 12, lambda j: (bu.at[j // 6], j % 6), range(12))
    start(gu[0][0])
    to_slot(fd, 3, 48, lambda j: (bd, j), range(3))
    start(gd_line)
    start(gu[1][0])

    def norm_in(i, _):
        rows = pl.ds(pl.multiple_of(i * 512, 512), 512)
        n, r = norm_rows(x_ref[rows, :].astype(f32))
        xhat[rows, :] = n
        rstd[rows, :] = jnp.broadcast_to(r, (512, 128))
        return 0

    wait(gq[0][0])
    start(gq[0][1])
    get_x.wait()
    lax.fori_loop(0, T // 512, norm_in, 0)
    wait(gq[1][0])
    start(gq[1][1])
    wait(gq[2][0])
    start(gq[2][1])
    u512[...] = spread_matrix(D + 32, 512)
    qz[...] = jnp.zeros_like(qz)
    dz[...] = jnp.zeros_like(dz)
    wait(gq[0][1])
    start(gq[0][2])
    wait(gu[1][0])
    start(gu[1][1])
    wait(go[0])
    start(go[1])
    segf = seg_ref[0:1, :].astype(f32)
    segcol = jnp.broadcast_to(segf, (128, T)).T
    for t in range(TILES):
        ks, ke = KEYS[t]
        biases[t][...] = jnp.where(segcol[ks:ke, :] == segf[:, 128 * t:128 * t + 128], 0.0, NEG)
    comb, mask = gain_comb(), gain_mask()
    wait(gq[0][2])

    wide = bq[0, ..., 0:128].reshape(512, 128)
    g32 = dot(u512[D:, :], wide).astype(bf16)
    gall = jnp.sum(jnp.where(mask, dot(g32, comb), 0.0), axis=0, keepdims=True)
    gains[0:1, :] = gall[:, 0:D]
    gains[1:2, :] = gall[:, D:]
    G1 = gains[0:1, :]
    G2 = gains[1:2, :]
    a[...] = (xhat[...] * G1).astype(bf16)

    def advance(*moves):
        for g, k in moves:
            wait(g[k])
            start(g[k + 1])

    def project(p):
        if p > 0:
            wait(gq[p][2])
        w = dot(u512[0:D, :], bq[p].reshape(512, D)).astype(bf16)
        for j in range(3):
            wqkv[:, j * D + p * 128:j * D + p * 128 + 128] = w[:, 128 * j:128 * j + 128]
        for i in range(2):
            rows = slice(512 * i, 512 * i + 512)
            qkv = dot(a[rows, :], w)
            q = qkv[:, 0:128].astype(bf16).astype(f32) * 0.125
            k_p[p, rows, :] = qkv[:, 128:256].astype(bf16)
            v_p[p, rows, :] = qkv[:, 256:384].astype(bf16)
            for s in range(4):
                qt = q[128 * s:128 * s + 128, :].T.astype(bf16)
                qz[p, 4 * i + s, 0:64, 0:128] = qt[0:64]
                qz[p, 4 * i + s, 64:128, 128:256] = qt[64:128]

    def scores(p, t):
        ks, ke = KEYS[t]
        return dot(k_p[p, ks:ke, :], qz[p, t])

    def weigh(p, t, s):
        ee, ri = [], []
        for half in range(2):
            sh = s[:, 128 * half:128 * half + 128] + biases[t][...]
            m = jnp.max(sh, axis=0, keepdims=True)
            ex = jnp.exp(sh - m)
            ri.append(1.0 / jnp.sum(ex, axis=0, keepdims=True))
            ee.append(ex.astype(bf16))
        e = jnp.concatenate(ee, axis=1)
        es[t][p] = e
        rinv[p, t] = jnp.broadcast_to(jnp.concatenate(ri, axis=1), (8, 256))
        return p, t, e, ri

    def mix(p, t, e, ri):
        ks, ke = KEYS[t]
        ct = dot(v_p[p, ks:ke, :], e, TN)
        ct = jnp.concatenate([ct[0:64, 0:128] * ri[0], ct[64:128, 128:256] * ri[1]], axis=0)
        ctxt[128 * p:128 * p + 128, 128 * t:128 * t + 128] = ct.astype(bf16)
        ctx[128 * t:128 * t + 128, 128 * p:128 * p + 128] = ct.T.astype(bf16)

    def advance(*moves):
        for g, k in moves:
            wait(g[k])
            start(g[k + 1])

    moves = {
        (0, 0): lambda: advance((gq[1], 1), (gu[0], 0)),
        (0, 6): lambda: (advance((gq[2], 1)), wait(gd_line), start(gd[0][0])),
        (1, 0): lambda: advance((gu[0], 1), (go, 1)),
        (1, 6): lambda: (advance((gd[0], 0)), start(gd[1][0])),
        (2, 4): lambda: advance((gu[0], 2)),
        (2, 7): lambda: advance((gd[0], 1)),
    }
    project(0)
    s, last = scores(0, 0), None
    for n in range(PAIRS * TILES):
        p, t = n // TILES, n % TILES
        if (p, t) in moves:
            moves[p, t]()
        if t == AHEAD and p + 1 < PAIRS:
            project(p + 1)
        ahead = scores((n + 1) // TILES, (n + 1) % TILES) if n + 1 < PAIRS * TILES else None
        now = weigh(p, t, s)
        if last is not None:
            mix(*last)
        s, last = ahead, now
    mix(*last)

    get_dy.wait()
    wait(go[2])
    wo[...] = dot(u512[0:D, :], bo[...].reshape(512, D)).astype(bf16)
    for i in range(2):
        rows = slice(512 * i, 512 * i + 512)
        hh = x_ref[rows, :].astype(f32) + dot(ctx[rows, :], wo[...])
        n, r = norm_rows(hh)
        hhat[rows, :] = n
        rstd2[rows, :] = jnp.broadcast_to(r, (512, 128))
        b[rows, :] = (n * G2).astype(bf16)
        hid[rows, :] = hh

    rs_u = [Scatter(su.at[j], cu.at[j], xu.at[j], yu.at[j], vu.at[j], hu.at[j], ssem.at[j]) for j in range(2)]
    rs_d = [Scatter(sd, cd, xd, yd, vd, hd, ssem.at[2 + j], pl.ds(j, 1), 1) for j in range(2)]
    rs_o = PlaneScatter(so, co, xo, ssem.at[4])
    ln_u = [line_steps(su.at[j], zu.at[j], ssem.at[j]) for j in range(2)]
    ln_d = line_steps(sd, zd, ssem.at[2])
    ln_o = line_steps(so, zo, ssem.at[4])

    def half(j):
        return slice(HALF * j, HALF * j + HALF)

    def block(i):
        return slice(512 * i, 512 * i + 512)

    def up(j, i):
        return dot(b[block(i), :], w1[:, half(j)])

    def bend(j, i, u):
        phi = 0.5 * (1.0 + lax.erf(u * 0.7071067811865476))
        act[block(i), half(j)] = (u * phi).astype(bf16)
        return phi + u * jnp.exp(-0.5 * u * u) * 0.3989422804014327

    def pull(j, i):
        return dot(dy_ref[block(i), :], bd[j].reshape(HALF, D), NT)

    def back(j, i, dul):
        du[block(i), :] = dul
        db = dot(dul, w1[:, half(j)], NT)
        if j == 0:
            dbacc[block(i), :] = db
        else:
            dbacc[block(i), :] += db

    def down_gradient(j):
        sd[j] = dot(act[:, half(j)], dy_ref[...], TN).astype(bf16).reshape((2, 2, 2, 2, 48, D))
        start(rs_d[j].core)

    def up_gradient(j):
        gup = dot(b[...], du[...], TN).astype(bf16)
        su[j] = dot(u512[0:D, :], gup, TN).astype(bf16).reshape(BOX + (PAD, HALF))
        start(rs_u[j].core)

    def arrive(j):
        wait(gu[j][-1])
        w1[:, half(j)] = dot(u512[0:D, :], bu[j].reshape(512, HALF)).astype(bf16)

    arrive(0)
    u, v = up(0, 0), up(0, 1)
    gp0 = bend(0, 0, u)
    du[block(0), :] = gp0.astype(bf16)
    gp1 = bend(0, 1, v)
    du[block(1), :] = gp1.astype(bf16)
    advance((gd[1], 0), (gu[1], 1))
    down_gradient(0)
    wait(gd[0][2])
    for i in range(2):
        back(0, i, (du[block(i), :].astype(f32) * pull(0, i)).astype(bf16))
    advance((gd[1], 1))
    up_gradient(0)
    arrive(1)
    u, v = up(1, 0), up(1, 1)
    gp0 = bend(1, 0, u)
    du[block(0), :] = gp0.astype(bf16)
    rs_d[0].core_to_near()
    gp1 = bend(1, 1, v)
    du[block(1), :] = gp1.astype(bf16)
    down_gradient(1)
    rs_u[0].core_to_near()
    wait(gd[1][2])
    for i in range(2):
        back(1, i, (du[block(i), :].astype(f32) * pull(1, i)).astype(bf16))
    up_gradient(1)

    gg2 = jnp.zeros((1, D), f32)
    for i in range(2):
        rows = slice(512 * i, 512 * i + 512)
        n = hhat[rows, :]
        db = dbacc[rows, :]
        gg2 = gg2 + jnp.sum(db * n, axis=0, keepdims=True)
        dhl = dy_ref[rows, :].astype(f32) + norm_back(db * G2, n, rstd2[rows, 0:1])
        dh[rows, :] = dhl
        dhrl = dhl.astype(bf16)
        dhr[rows, :] = dhrl
        dct = dot(wo[...], dhrl, NT)
        for p in range(PAIRS):
            for s in range(4):
                t = 4 * i + s
                ri = rinv[p, t, 0:1, :]
                top = dct[128 * p:128 * p + 64, 128 * s:128 * s + 128].astype(bf16).astype(f32)
                low = dct[128 * p + 64:128 * p + 128, 128 * s:128 * s + 128].astype(bf16).astype(f32)
                dz[p, t, 0:64, 0:128] = (top * ri[:, 0:128]).astype(bf16)
                dz[p, t, 64:128, 128:256] = (low * ri[:, 128:256]).astype(bf16)
        if i == 0:
            rs_d[0].near_to_far()
            rs_u[0].near_to_far()
            rs_d[1].core_to_near()
        else:
            rs_u[1].core_to_near()
    gout = dot(ctxt[...], dhr[...]).astype(bf16)
    so[...] = dot(u512[0:D, :], gout, TN).astype(bf16).reshape(BOX + (PAD, D))
    start(rs_o.core)


    rs_q = [PlaneScatter(sq.at[p], cq.at[p], xq.at[p], ssem.at[5 + p]) for p in range(PAIRS)]
    ln_q = [line_steps(sq.at[p], zq.at[p], ssem.at[5 + p]) for p in range(PAIRS)]

    def ends(r, line=None):
        r.end_far()
        if line is not None:
            start(line)

    def plane_ends(r, line):
        r.end_plane()
        start(line)

    def pulls(p, t):
        ks, ke = KEYS[t]
        return dot(v_p[p, ks:ke, :], dz[p, t])

    def slope(p, t, dp):
        e = es[t][p].astype(f32)
        tt = e * dp
        cc = jnp.sum(tt, axis=0, keepdims=True) * rinv[p, t, 0:1, :]
        return p, t, (tt - e * cc).astype(bf16)

    def spread(p, t, ds):
        ks, ke = KEYS[t]
        dv = dot(es[t][p], dz[p, t], NT)
        dk = dot(ds, qz[p, t], NT)
        if t == 0:
            dvacc[p % 2] = jnp.zeros((T, 128), f32)
            dkacc[p % 2] = jnp.zeros((T, 128), f32)
        dvacc[p % 2, ks:ke, :] += dv
        dkacc[p % 2, ks:ke, :] += dk
        dqt = dot(k_p[p, ks:ke, :], ds, TN)
        dqt = jnp.concatenate([dqt[0:64, 0:128], dqt[64:128, 128:256]], axis=0) * 0.125
        dqkv[p, 128 * t:128 * t + 128, 0:128] = dqt.T.astype(bf16)

    def pair_gradient(p, gg1):
        dqkv[p, :, 128:256] = dkacc[p % 2].astype(bf16)
        dqkv[p, :, 256:384] = dvacc[p % 2].astype(bf16)
        g = dot(a[...], dqkv[p], TN)
        for j in range(3):
            gg1 = gg1 + wqkv[:, j * D + p * 128:j * D + p * 128 + 128].astype(f32) * g[:, 128 * j:128 * j + 128]
        full = g.astype(bf16)
        if p == PAIRS - 1:
            gsum = jnp.sum(gg1.T, axis=0, keepdims=True) / G1
            grow = jnp.concatenate([gsum, gg2], axis=1)
            grow = jnp.where(gain_mask(), jnp.broadcast_to(grow, (32, 2 * D)), 0.0).astype(bf16)
            grow = dot(grow, gain_comb(), NT).astype(bf16)
            low = jnp.concatenate([grow, jnp.zeros((32, D - 128), bf16)], axis=1)
            full = dot(u512[...], jnp.concatenate([full, low], axis=0), TN)
        else:
            full = dot(u512[0:D, :], full, TN)
        sq[p] = full.astype(bf16).reshape(BOX + (PAD, D))
        start(rs_q[p].core)
        return gg1

    moves = {
        (0, 4): lambda: rs_o.core_to_plane(),
        (0, 6): lambda: (ends(rs_d[0]), ends(rs_u[0], ln_u[0])),
        (1, 4): lambda: rs_q[0].core_to_plane(),
        (1, 7): lambda: rs_d[1].near_to_far(),
        (2, 0): lambda: rs_u[1].near_to_far(),
        (2, 2): lambda: plane_ends(rs_o, ln_o),
        (2, 4): lambda: (rs_q[1].core_to_plane(), plane_ends(rs_q[0], ln_q[0])),
        (2, 6): lambda: (ends(rs_d[1], ln_d), ends(rs_u[1], ln_u[1])),
    }
    gg1 = jnp.zeros((D, 128), f32)
    dp, last = pulls(0, 0), None
    for n in range(PAIRS * TILES):
        p, t = n // TILES, n % TILES
        if (p, t) in moves:
            moves[p, t]()
        ahead = pulls((n + 1) // TILES, (n + 1) % TILES) if n + 1 < PAIRS * TILES else None
        now = slope(p, t, dp)
        if last is not None:
            spread(*last)
        dp, last = ahead, now
        if t == 1 and p > 0:
            gg1 = pair_gradient(p - 1, gg1)
    spread(*last)
    pair_gradient(PAIRS - 1, gg1)
    def da_rows(i):
        rows = slice(512 * i, 512 * i + 512)
        da = jnp.zeros((512, D), f32)
        for p in range(PAIRS):
            w = jnp.concatenate([wqkv[:, j * D + p * 128:j * D + p * 128 + 128] for j in range(3)], axis=1)
            da = da + dot(dqkv[p, rows, :], w, NT)
        dbacc[rows, :] = dh[rows, :] + norm_back(da * G1, xhat[rows, :], rstd[rows, 0:1])
        copy = pltpu.make_async_copy(dbacc.at[rows], gx_hbm.at[rows], lsem.at[i])
        copy.start()
        return copy

    def from_slot(v, width, rows, dst, first=0, cols=None):
        for k, j in enumerate(cols if cols is not None else range(first, first + v.shape[1] // 128)):
            dst[pl.ds(j, rows, stride=width), :] = v[0:rows, 128 * k:128 * k + 128]

    w2 = bd[...].reshape(FF, D)

    def out_rows(i):
        rows = slice(512 * i, 512 * i + 512)
        out_v[rows, :] = (hid[rows, :] + dot(act[rows, :], w2)).astype(bf16)
        copy = pltpu.make_async_copy(out_v.at[rows], out_hbm.at[rows], lsem.at[2 + i])
        copy.start()
        return copy

    done = [da_rows(0)]
    rs_q[2].core_to_plane()
    plane_ends(rs_q[1], ln_q[1])
    done.append(da_rows(1))
    done.append(out_rows(0))
    plane_ends(rs_q[2], ln_q[2])
    done.append(out_rows(1))
    for j in range(2):
        wait(ln_u[j])
        from_slot(line_sum(su.at[j], zu.at[j]), 12, 12, ou, 6 * j)
    wait(ln_d)
    from_slot(line_sum(sd, zd), 3, 48, od)
    wait(ln_o)
    from_slot(line_sum(so, zo), 3, 12, oo)
    for p in range(PAIRS):
        wait(ln_q[p])
        v = line_sum(sq.at[p], zq.at[p])
        from_slot(v, 9, 12, oq, cols=(p, 3 + p, 6 + p))
        if p == 2:
            og[...] = v[12:13, 0:24]
    for q in done:
        q.wait()


def vm(shape, dtype):
    return pltpu.VMEM(shape, dtype)


WIDE = ((PAIRS,), (PAD, D)), ((), (PAD, D)), ((2,), (PAD, HALF)), ((), (48, D))


def layer(x, seg, fq, fo, fu, fd, fg, dy):
    spec = pl.BlockSpec(memory_space=pltpu.VMEM)
    hbm = pl.BlockSpec(memory_space=pl.ANY)
    dma = pltpu.SemaphoreType.DMA
    scratch = [
        vm((PAIRS,) + BOX + (PAD, D), bf16), vm(BOX + (PAD, D), bf16), vm((2,) + BOX + (PAD, HALF), bf16),
        vm(BOX + (48, D), bf16),
        vm((D + 32, 512), bf16), vm((D, 3 * D), bf16), vm((D, D), bf16), vm((D, FF), bf16),
        vm((8, D), f32), vm((144, 128), f32), vm((PAD, 128), f32),
        vm((T, D), f32), vm((T, 128), f32), vm((T, D), bf16), vm((PAIRS, T, 128), bf16), vm((PAIRS, T, 128), bf16),
        vm((PAIRS, TILES, 128, 256), bf16), vm((T, D), bf16), vm((D, T), bf16), vm((PAIRS, TILES, 8, 256), f32),
        vm((T, D), f32), vm((T, 128), f32), vm((T, FF), bf16), vm((T, HALF), bf16),
        vm((T, D), f32), vm((T, D), f32), vm((T, D), f32), vm((T, D), bf16),
        vm((PAIRS, TILES, 128, 256), bf16), vm((2, T, 128), f32), vm((2, T, 128), f32),
        vm((PAIRS, T, D), bf16),
        [vm((PAIRS, ke - ks, 256), bf16) for ks, ke in KEYS],
        [vm((ke - ks, 128), f32) for ks, ke in KEYS],
    ]
    scratch += [vm(BOX + (48, D), bf16)]
    scratch += [vm(g + BOX[:4] + s, bf16) for g, s in WIDE]
    scratch += [vm(g + (3, 2, 2) + s, bf16) for g, s in WIDE[:2]]
    scratch += [vm(g + BOX[:2] + s, bf16) for g, s in WIDE[2:]]
    for lead in (BOX[:2], BOX[:1], BOX[:1]):
        scratch += [vm(g + lead + s, bf16) for g, s in WIDE[2:]]
    scratch += [vm(g + (3,) + s, bf16) for g, s in WIDE]
    scratch += [vm((T, D), bf16), vm((T, D), bf16), dma((8, 2, 8)), dma((8, 2, 8)), dma((6,))]
    flops = 2 * T * (3 * (3 * D * D + D * D + 2 * D * FF)) + 12 * 2 * 330 * T * D
    return pl.pallas_call(
        layer_kernel,
        out_shape=[
            jax.ShapeDtypeStruct((T, D), bf16),
            jax.ShapeDtypeStruct((T, D), f32),
            jax.ShapeDtypeStruct(fq.shape, f32),
            jax.ShapeDtypeStruct(fo.shape, f32),
            jax.ShapeDtypeStruct(fu.shape, f32),
            jax.ShapeDtypeStruct(fd.shape, f32),
            jax.ShapeDtypeStruct(fg.shape, f32),
        ],
        in_specs=[hbm] + [spec] * 6 + [hbm],
        out_specs=[hbm] * 2 + [spec] * 5,
        scratch_shapes=scratch,
        compiler_params=pltpu.CompilerParams(collective_id=0, has_side_effects=True, vmem_limit_bytes=62 * 2**20),
        cost_estimate=pl.CostEstimate(flops=flops, bytes_accessed=5 * 2**20, transcendentals=T * (FF + 2508)),
        name="layer",
    )(x, seg, fq, fo, fu, fd, fg, dy)


def hand_over_kernel(*refs):
    ins, outs, stage, sem = refs[:7], refs[7:14], refs[14:21], refs[21]
    loads, stores = [], []
    for i, (src, mid, dst) in enumerate(zip(ins, stage, outs)):
        parts = PARTS if src.shape[0] == T else 1
        n = src.shape[0] // parts
        for k in range(parts):
            rows = pl.ds(n * k, n)
            loads.append(pltpu.make_async_copy(src.at[rows], mid.at[rows], sem.at[0, i, k]))
            stores.append(pltpu.make_async_copy(mid.at[rows], dst.at[rows], sem.at[1, i, k]))
    for q in loads:
        q.start()
    for p, q in zip(loads, stores):
        p.wait()
        q.start()
    for q in stores:
        q.wait()


PARTS = 4


def hand_over(arrays):
    hbm = pl.BlockSpec(memory_space=pl.ANY)
    return pl.pallas_call(
        hand_over_kernel,
        out_shape=[jax.ShapeDtypeStruct(v.shape, v.dtype) for v in arrays],
        in_specs=[hbm] * 7,
        out_specs=[hbm] * 7,
        scratch_shapes=[pltpu.VMEM(v.shape, v.dtype) for v in arrays] + [pltpu.SemaphoreType.DMA((2, 7, PARTS))],
        name="hand_over",
    )(*arrays)


def body_direct(tokens, seg_ids, w_qkv, w_out, w_up, w_down, norm_gains, cotangent):
    def lanes(w):
        return w.reshape(-1, 128)

    out, gx, oq, oo, ou, od, og = hand_over(layer(
        tokens[0], seg_ids, lanes(w_qkv), lanes(w_out), lanes(w_up), lanes(w_down), norm_gains.reshape(1, -1),
        cotangent[0]))
    return (out[None], gx[None], oq.reshape(-1), oo.reshape(-1), ou.reshape(-1), od.reshape(-1), og.reshape(-1))


def plain_kernel(x_ref, seg_ref, wqkv_ref, wo_ref, w1_ref, w2_ref, gain_ref, dy_ref,
           out_ref, gx_ref, gqkv_ref, gout_ref, gup_ref, gdown_ref, ggain_ref,
           xhat, rstd, a, k_p, v_p, qz, ctx, ctxt, h, rinv, b, act, du, dh, dhr, dz, dkacc, dvacc, dqkv, *rest):
    es, biases = rest[:8], rest[8:]
    G1 = gain_ref[0:1, :]
    G2 = gain_ref[1:2, :]
    R = 256
    qz[...] = jnp.zeros_like(qz)
    dz[...] = jnp.zeros_like(dz)

    def stage_a(i, _):
        rows = pl.ds(pl.multiple_of(i * R, R), R)
        n, r = norm_rows(x_ref[rows, :].astype(f32))
        xhat[rows, :] = n
        rstd[0, rows, :] = jnp.broadcast_to(r, (R, 128))
        al = (n * G1).astype(bf16)
        a[rows, :] = al
        q = dot(al, wqkv_ref[:, 0:D]).astype(bf16).astype(f32) * 0.125
        kk = dot(al, wqkv_ref[:, D:2 * D]).astype(bf16)
        vv = dot(al, wqkv_ref[:, 2 * D:]).astype(bf16)
        for p in range(PAIRS):
            k_p[p, rows, :] = kk[:, 128 * p:128 * p + 128]
            v_p[p, rows, :] = vv[:, 128 * p:128 * p + 128]
            for s in range(R // 128):
                qt = q[128 * s:128 * s + 128, 128 * p:128 * p + 128].T.astype(bf16)
                qz[p, i * (R // 128) + s, 0:64, 0:128] = qt[0:64]
                qz[p, i * (R // 128) + s, 64:128, 128:256] = qt[64:128]
        return 0

    lax.fori_loop(0, T // R, stage_a, 0)

    segf = seg_ref[0:1, :].astype(f32)
    segcol = jnp.broadcast_to(segf, (128, T)).T
    for t in range(8):
        ks, ke = KEYS[t]
        biases[t][...] = jnp.where(segcol[ks:ke, :] == segf[:, 128 * t:128 * t + 128], 0.0, NEG)

    def att(p, _):
        lanes = pl.ds(pl.multiple_of(p * 128, 128), 128)
        for t in range(8):
            ks, ke = KEYS[t]
            s = dot(k_p[p, ks:ke, :], qz[p, t])
            ee, ri = [], []
            for half in range(2):
                sh = s[:, 128 * half:128 * half + 128] + biases[t][...]
                m = jnp.max(sh, axis=0, keepdims=True)
                ex = jnp.exp(sh - m)
                ri.append(1.0 / jnp.sum(ex, axis=0, keepdims=True))
                ee.append(ex.astype(bf16))
            e = jnp.concatenate(ee, axis=1)
            es[t][p] = e
            rr = jnp.concatenate(ri, axis=1)
            rinv[p, t] = jnp.broadcast_to(rr, (8, 256))
            ct = dot(v_p[p, ks:ke, :], e, TN)
            ct = jnp.concatenate([ct[0:64, 0:128] * ri[0], ct[64:128, 128:256] * ri[1]], axis=0)
            ctxt[lanes, 128 * t:128 * t + 128] = ct.astype(bf16)
            ctx[128 * t:128 * t + 128, lanes] = ct.T.astype(bf16)
        return 0

    lax.fori_loop(0, PAIRS, att, 0)

    FC = 512
    def stage_d(i, gacc):
        rows = pl.ds(pl.multiple_of(i * R, R), R)
        hh = x_ref[rows, :].astype(f32) + dot(ctx[rows, :], wo_ref[...])
        n, r = norm_rows(hh)
        bl = (n * G2).astype(bf16)
        b[rows, :] = bl
        dyl = dy_ref[rows, :]
        o = hh
        db = jnp.zeros((R, D), f32)
        for c in range(FF // FC):
            cols = slice(c * FC, c * FC + FC)
            u = dot(bl, w1_ref[:, cols])
            phi = 0.5 * (1.0 + lax.erf(u * 0.7071067811865476))
            al = (u * phi).astype(bf16)
            act[rows, cols] = al
            o = o + dot(al, w2_ref[cols, :])
            gp = phi + u * jnp.exp(-0.5 * u * u) * 0.3989422804014327
            dul = (gp * dot(dyl, w2_ref[cols, :], NT)).astype(bf16)
            du[rows, cols] = dul
            db = db + dot(dul, w1_ref[:, cols], NT)
        out_ref[rows, :] = o.astype(bf16)
        gacc = gacc + jnp.sum(db * n, axis=0, keepdims=True)
        dhl = dyl.astype(f32) + norm_back(db * G2, n, r)
        dh[rows, :] = dhl
        dhrl = dhl.astype(bf16)
        dhr[rows, :] = dhrl
        dct = dot(wo_ref[...], dhrl, NT)
        for p in range(PAIRS):
            for s in range(R // 128):
                tt = i * (R // 128) + s
                ri = rinv[p, tt, 0:1, :]
                dz[p, tt, 0:64, 0:128] = (dct[128 * p:128 * p + 64, 128 * s:128 * s + 128].astype(bf16).astype(f32) * ri[:, 0:128]).astype(bf16)
                dz[p, tt, 64:128, 128:256] = (dct[128 * p + 64:128 * p + 128, 128 * s:128 * s + 128].astype(bf16).astype(f32) * ri[:, 128:256]).astype(bf16)
        return gacc

    def sd():
        ggain_ref[1:2, :] = lax.fori_loop(0, T // R, stage_d, jnp.zeros((1, D), f32))
    sd()

    def w_down(i, _):
        cols = pl.ds(pl.multiple_of(i * 256, 256), 256)
        gdown_ref[cols, :] = dot(act[:, cols], dy_ref[...], TN)
        gup_ref[:, cols] = dot(b[...], du[:, cols], TN)
        return 0

    lax.fori_loop(0, FF // 256, w_down, 0)
    gout_ref[...] = dot(ctxt[...], dhr[...])

    dkacc[...] = jnp.zeros_like(dkacc)
    dvacc[...] = jnp.zeros_like(dvacc)
    def attb(p, _):
        lanes = pl.ds(pl.multiple_of(p * 128, 128), 128)
        for t in range(8):
            ks, ke = KEYS[t]
            dzl = dz[p, t]
            dp = dot(v_p[p, ks:ke, :], dzl)
            e = es[t][p]
            ef = e.astype(f32)
            tt = ef * dp
            c = jnp.sum(tt, axis=0, keepdims=True) * rinv[p, t, 0:1, :]
            ds = (tt - ef * c).astype(bf16)
            dvacc[p, ks:ke, :] += dot(e, dzl, NT)
            dkacc[p, ks:ke, :] += dot(ds, qz[p, t], NT)
            dqt = dot(k_p[p, ks:ke, :], ds, TN)
            dqt = jnp.concatenate([dqt[0:64, 0:128], dqt[64:128, 128:256]], axis=0) * 0.125
            dqkv[128 * t:128 * t + 128, lanes] = dqt.T.astype(bf16)
        return 0

    lax.fori_loop(0, PAIRS, attb, 0)
    for p in range(PAIRS):
        dqkv[:, D + 128 * p:D + 128 * p + 128] = dkacc[p].astype(bf16)
        dqkv[:, 2 * D + 128 * p:2 * D + 128 * p + 128] = dvacc[p].astype(bf16)

    def w_qkv(i, _):
        cols = pl.ds(pl.multiple_of(i * 384, 384), 384)
        gqkv_ref[:, cols] = dot(a[...], dqkv[:, cols], TN)
        return 0

    lax.fori_loop(0, 3, w_qkv, 0)

    def stage_g(i, gacc):
        rows = pl.ds(pl.multiple_of(i * R, R), R)
        da = dot(dqkv[rows, :], wqkv_ref[...], NT)
        n = xhat[rows, :]
        gacc = gacc + jnp.sum(da * n, axis=0, keepdims=True)
        gx_ref[rows, :] = dh[rows, :] + norm_back(da * G1, n, rstd[0, rows, 0:1])
        return gacc

    def sg():
        ggain_ref[0:1, :] = lax.fori_loop(0, T // R, stage_g, jnp.zeros((1, D), f32))
    sg()


PLAIN_SCRATCH = [
    pltpu.VMEM((T, D), f32),
    pltpu.VMEM((1, T, 128), f32),
    pltpu.VMEM((T, D), bf16),
    pltpu.VMEM((PAIRS, T, 128), bf16),
    pltpu.VMEM((PAIRS, T, 128), bf16),
    pltpu.VMEM((PAIRS, 8, 128, 256), bf16),
    pltpu.VMEM((T, D), bf16),
    pltpu.VMEM((D, T), bf16),
    pltpu.VMEM((8, 128), f32),
    pltpu.VMEM((PAIRS, 8, 8, 256), f32),
    pltpu.VMEM((T, D), bf16),
    pltpu.VMEM((T, FF), bf16),
    pltpu.VMEM((T, FF), bf16),
    pltpu.VMEM((T, D), f32),
    pltpu.VMEM((T, D), bf16),
    pltpu.VMEM((PAIRS, 8, 128, 256), bf16),
    pltpu.VMEM((PAIRS, T, 128), f32),
    pltpu.VMEM((PAIRS, T, 128), f32),
    pltpu.VMEM((T, 3 * D), bf16),
] + [pltpu.VMEM((PAIRS, ke - ks, 256), bf16) for ks, ke in KEYS] + [pltpu.VMEM((ke - ks, 128), f32) for ks, ke in KEYS]


def plain_layer(x, seg, wqkv, wo, w1, w2, gains, dy):
    vm = pl.BlockSpec(memory_space=pltpu.VMEM)
    return pl.pallas_call(
        plain_kernel,
        out_shape=[
            jax.ShapeDtypeStruct((T, D), bf16),
            jax.ShapeDtypeStruct((T, D), f32),
            jax.ShapeDtypeStruct((D, 3 * D), f32),
            jax.ShapeDtypeStruct((D, D), f32),
            jax.ShapeDtypeStruct((D, FF), f32),
            jax.ShapeDtypeStruct((FF, D), f32),
            jax.ShapeDtypeStruct((2, D), f32),
        ],
        in_specs=[vm] * 8,
        out_specs=[vm] * 7,
        scratch_shapes=PLAIN_SCRATCH,
        compiler_params=pltpu.CompilerParams(vmem_limit_bytes=62 * 2**20),
        name="plain_layer",
    )(x, seg, wqkv, wo, w1, w2, gains, dy)


def body_plain(tokens, seg_ids, w_qkv, w_out, w_up, w_down, norm_gains, cotangent):
    whole = [lax.all_gather(w, "fsdp", axis=0, tiled=True) for w in (w_qkv, w_out, w_up, w_down, norm_gains)]
    out, gx, *grads = plain_layer(
        tokens[0], seg_ids, whole[0].reshape(D, 3 * D), whole[1].reshape(D, D), whole[2].reshape(D, FF),
        whole[3].reshape(FF, D), whole[4].astype(f32).reshape(2, D), cotangent[0])
    shards = [lax.psum_scatter(g.reshape(-1), "fsdp", scatter_dimension=0, tiled=True) for g in grads]
    return (out[None], gx[None], *shards)


def solution(mesh):
    direct = mesh.shape["fsdp"] == DEVICES
    rows, flat = P("fsdp", None, None), P("fsdp")
    return jax.shard_map(
        body_direct if direct else body_plain,
        mesh=mesh,
        in_specs=(rows, P("fsdp", None), flat, flat, flat, flat, flat, rows),
        out_specs=(rows, rows, flat, flat, flat, flat, flat),
        check_vma=False,
    )
```
